32 devices in a mesh: dp: 2 (over x), seq: 4 (over y, core), tensor: 4 (over z).
Axes of the slice: x: 2, y: 2, z: 4, core: 2. Of those that a mesh axis runs over, the one named last changes fastest.
Arguments:
- attention_output_rows: bfloat16 [2, 4096, 4096], P('dp', 'seq', 'tensor'), may hold values from -6 to 6
- projection_result_gradient: bfloat16 [2, 4096, 4096], P('dp', 'seq'), may hold values from -6 to 6
- adapter_down_weight: bfloat16 [4096, 128], P('tensor'), may hold values from -0.09375 to 0.09375
- adapter_up_weight: bfloat16 [128, 4096], P(None, 'tensor'), may hold values from -0.09375 to 0.09375
- output_projection_weight: bfloat16 [4096, 4096], P('tensor'), may hold values from -0.09375 to 0.09375
- adam_first_moments: float32 [2, 128, 4096], P(None, 'dp', 'tensor'), may hold values from -24 to 24
- adam_second_moments: float32 [2, 128, 4096], P(None, 'dp', 'tensor'), may hold values from 1 to 40
- rank_side_projection: float32 [16, 128], replicated, may hold values from -0.5 to 0.5
- width_side_projection: bfloat16 [4096, 256], replicated, may hold values from -0.09375 to 0.09375
- bounds: int32 [2, 2, 16], P('dp'), may hold values from 0 to 4096, as said below
- example_owner_slot: int32 [2, 16], P('dp'), may hold values from 0 to 15, each once within a row
Outputs:
- attention_out_gradient: bfloat16 [2, 4096, 4096], P('dp', 'seq', 'tensor')
- features: float32 [2, 16, 8192], P('dp', ('seq', 'tensor'))
The draws below stay inside these ranges and needn't reach their ends.
Inputs may be any that keep to these rules, and one draw needn't show every extreme that they name: bounds[s, 0, e] is the first token of example e of pack s and bounds[s, 1, e] its end (exclusive): the first start is 0, each end is the next start, the last end is 4096, every example has one token or more. The tokens of one aligned block of 1024 tokens of a pack belong to at most 8 examples, and every pack has a block whose tokens belong to exactly 8. `example_owner_slot`: each row names every slot once.
All inputs are finite; a program needn't handle non-finite values.
Results may differ from the reference program's by a relative error of at most 0.014.
Values may be sent and summed in bfloat16 or wider, within the bound.
No kernel may reach another device: no remote copies, remote signals or barrier semaphores. Data moves between devices by JAX's collectives and lax.ppermute only.
A program may use at most 128 MiB of HBM per device.

```python
import math
import jax
import jax.numpy as jnp
from jax import lax

MODEL_WIDTH = 4096
ADAPTER_RANK = 128
LEN = 4096
EX = 16
TOUCH = 8
KR = 16
KD = 256
BLK = 1024
SEQS = 2
GROUPS = 2
SLOTS = 16
PROJ = 8192
N_SEQ = 4


def pack_bounds(key):
    n_blocks = LEN // BLK
    others = n_blocks - 2
    remaining = EX - TOUCH
    key_empty, key_full, key_share, key_place = jax.random.split(key, 4)
    empty_block = jax.random.randint(key_empty, (), 1, n_blocks - 1)
    full_pick = jax.random.randint(key_full, (), 0, n_blocks - 1)
    full_block = full_pick + (full_pick >= empty_block).astype(jnp.int32)
    shuffled = jax.random.permutation(key_share, others)
    other_counts = remaining // others + (shuffled < remaining % others).astype(jnp.int32)
    blocks = jnp.arange(n_blocks, dtype=jnp.int32)
    ranked = blocks - (blocks > empty_block).astype(jnp.int32) - (blocks > full_block).astype(jnp.int32)
    ranked = jnp.clip(ranked, 0, others - 1)
    counts = jnp.where(blocks == full_block, TOUCH - 1, jnp.where(blocks == empty_block, 0, other_counts[ranked]))

    def block_cuts(block):
        picked = jax.random.permutation(jax.random.fold_in(key_place, block), BLK - 1)[:TOUCH - 1] + 1
        kept_mask = jnp.arange(TOUCH - 1) < counts[block]
        return jnp.where(kept_mask, block * BLK + picked, LEN)
    cut_points = jnp.sort(jax.vmap(block_cuts)(blocks).reshape(-1))[:EX - 1]
    anchor = jnp.zeros((1,), jnp.int32)
    finish = jnp.full((1,), LEN, jnp.int32)
    starts = jnp.concatenate([anchor, cut_points.astype(jnp.int32)])
    end_points = jnp.concatenate([cut_points.astype(jnp.int32), finish])
    return jnp.stack([starts, end_points]).astype(jnp.int32)


def draw_bounds(key, part):
    sub_keys = jax.random.split(key, SEQS)
    return jax.vmap(pack_bounds)(sub_keys)


def shard_levels(key, shape, cuts, least, top_value):
    def one(position, blocks):
        heights = jax.random.uniform(jax.random.fold_in(jax.random.fold_in(key, 6), position), (blocks,), jnp.float32, least / len(cuts), top_value / len(cuts))
        return jnp.repeat(jnp.exp(heights), shape[position] // blocks).reshape((-1,) + (1,) * (len(shape) - position - 1))

    gain = one(*cuts[0])
    for cut in cuts[1:]:
        gain = gain * one(*cut)
    return gain


def gaussian(stream_key, dims, spread, limit, cuts=(), kind=jnp.bfloat16):
    drawn = spread * jax.random.normal(stream_key, dims, jnp.float32)
    if cuts:
        drawn = drawn * shard_levels(stream_key, dims, cuts, -0.22, 0.18)
    return jnp.clip(drawn, -limit, limit).astype(kind)


def setup_inputs(seed: int = 0) -> dict:
    streams_of = jax.random.split(jax.random.key(seed), 12)
    attention_output_rows = gaussian(streams_of[0], (SEQS, LEN, MODEL_WIDTH), 1.0, 6.0, ((0, 2), (1, 4), (2, 4)))
    projection_result_gradient = gaussian(streams_of[1], (SEQS, LEN, MODEL_WIDTH), 1.0, 6.0, ((0, 2), (1, 4)))
    adapter_down_weight = gaussian(streams_of[2], (MODEL_WIDTH, ADAPTER_RANK), MODEL_WIDTH ** -0.5, 0.09375, ((0, 4),))
    adapter_up_weight = gaussian(streams_of[3], (ADAPTER_RANK, MODEL_WIDTH), MODEL_WIDTH ** -0.5, 0.09375, ((1, 4),))
    output_projection_weight = gaussian(streams_of[4], (MODEL_WIDTH, MODEL_WIDTH), MODEL_WIDTH ** -0.5, 0.09375, ((0, 4),))
    adam_first_moments = gaussian(streams_of[5], (2, ADAPTER_RANK, MODEL_WIDTH), 4.0, 24.0, ((1, 2), (2, 4)), jnp.float32)
    adam_second_moments = jnp.clip(jnp.exp(math.log(40.0) - 3.6888795 * jax.random.uniform(streams_of[6], (2, ADAPTER_RANK, MODEL_WIDTH), jnp.float32) ** shard_levels(streams_of[6], (2, ADAPTER_RANK, MODEL_WIDTH), ((1, 2), (2, 4)), -0.2, 0.2)), 1.0, 40.0)
    rank_side_projection = gaussian(streams_of[7], (KR, ADAPTER_RANK), ADAPTER_RANK ** -0.5, 0.5, (), jnp.float32)
    width_side_projection = gaussian(streams_of[8], (MODEL_WIDTH, KD), MODEL_WIDTH ** -0.5, 0.09375)
    bounds = draw_bounds(jax.random.fold_in(streams_of[11], 71), 0)
    example_owner_slot = jax.vmap(lambda own: jax.random.permutation(own, SLOTS))(jax.random.split(streams_of[10], GROUPS)).reshape((GROUPS, SLOTS)).astype(jnp.int32)
    return {"attention_output_rows": attention_output_rows, "projection_result_gradient": projection_result_gradient, "adapter_down_weight": adapter_down_weight, "adapter_up_weight": adapter_up_weight, "output_projection_weight": output_projection_weight, "adam_first_moments": adam_first_moments, "adam_second_moments": adam_second_moments, "rank_side_projection": rank_side_projection, "width_side_projection": width_side_projection, "bounds": bounds, "example_owner_slot": example_owner_slot}


ADAPTER_SCALE = 4.0
BETA_ONE = 0.9
BETA_TWO = 0.999
EPSILON = 1e-08

def contract_trailing(left, right):
    return lax.dot_general(left, right, (((1,), (1,)), ((), ())), preferred_element_type=jnp.float32)

def normalize(grads, adam_first_moments, adam_second_moments):
    first = BETA_ONE * adam_first_moments + (1.0 - BETA_ONE) * grads
    second = BETA_TWO * adam_second_moments + (1.0 - BETA_TWO) * grads * grads
    return (first / (jnp.sqrt(second) + EPSILON)).astype(jnp.bfloat16)

def project(normed, rank_side_projection, width_side_projection):
    inner = jnp.einsum('emrd,dc->emrc', normed.astype(jnp.float32), width_side_projection.astype(jnp.float32))
    outer = jnp.einsum('qr,emrc->emqc', rank_side_projection, inner, precision=lax.Precision.HIGHEST)
    return outer.reshape(outer.shape[0], -1)

def bundle_terms(token_count, gradient_result, boundary_row, adapter_down_weight, adapter_up_weight, output_projection_weight, adam_first_moments, adam_second_moments, rank_side_projection, width_side_projection):
    reduced_input = jnp.dot(token_count, adapter_down_weight, preferred_element_type=jnp.float32).astype(jnp.bfloat16)
    reduced_gradient = contract_trailing(gradient_result, adapter_up_weight).astype(jnp.bfloat16)
    attention_out_gradient = (contract_trailing(gradient_result, output_projection_weight) + ADAPTER_SCALE * contract_trailing(reduced_gradient, adapter_down_weight)).astype(jnp.bfloat16)
    positions = jnp.arange(LEN, dtype=jnp.int32)
    example_id = lax.optimization_barrier(jnp.sum((boundary_row[0][None, :] <= positions[:, None]).astype(jnp.int32), axis=1)) - 1
    grads = jnp.zeros((EX, 2, ADAPTER_RANK, MODEL_WIDTH), jnp.float32)
    slot_range = jnp.arange(TOUCH, dtype=jnp.int32)
    for block in range(N_SEQ):
        low_t = block * BLK
        block_ids = example_id[low_t:low_t + BLK]
        first_id = block_ids[0]
        in_slot = ((block_ids - first_id)[:, None] == slot_range[None, :]).astype(jnp.bfloat16)
        masked_grad = (reduced_gradient[low_t:low_t + BLK, None, :] * in_slot[:, :, None]).reshape(BLK, TOUCH * ADAPTER_RANK)
        masked_in = (reduced_input[low_t:low_t + BLK, None, :] * in_slot[:, :, None]).reshape(BLK, TOUCH * ADAPTER_RANK)
        part_a = jnp.einsum('tk,td->kd', masked_grad.astype(jnp.float32), token_count[low_t:low_t + BLK].astype(jnp.float32))
        part_b = jnp.einsum('tk,td->kd', masked_in.astype(jnp.float32), gradient_result[low_t:low_t + BLK].astype(jnp.float32))
        parts = ADAPTER_SCALE * jnp.stack([part_a.reshape(TOUCH, ADAPTER_RANK, MODEL_WIDTH), part_b.reshape(TOUCH, ADAPTER_RANK, MODEL_WIDTH)], axis=1)
        parts = lax.optimization_barrier(parts.astype(jnp.bfloat16)).astype(jnp.float32)
        for slot in range(TOUCH):
            target = jnp.minimum(first_id + slot, EX - 1).astype(jnp.int32)
            grads = grads.at[target].add(parts[slot])
    normed = normalize(grads, adam_first_moments, adam_second_moments)
    return (attention_out_gradient, project(normed, rank_side_projection, width_side_projection))

def reference(attention_output_rows, projection_result_gradient, adapter_down_weight, adapter_up_weight, output_projection_weight, adam_first_moments, adam_second_moments, rank_side_projection, width_side_projection, bounds, example_owner_slot):

    def one_pack(entry_list):
        return bundle_terms(entry_list[0], entry_list[1], entry_list[2], adapter_down_weight, adapter_up_weight, output_projection_weight, adam_first_moments, adam_second_moments, rank_side_projection, width_side_projection)
    attention_out_gradient, feature = lax.map(one_pack, (attention_output_rows, projection_result_gradient, bounds))
    grouped = feature.reshape(GROUPS, SLOTS, PROJ)

    def place(row, values):
        return jnp.zeros((SLOTS, PROJ), jnp.float32).at[row].set(values)
    features = jax.vmap(place)(example_owner_slot, grouped)
    return (attention_out_gradient, features)
```

```python
import jax
import jax.numpy as jnp
from jax import lax
from jax.sharding import PartitionSpec as P

TOUCH = 8


ADAPTER_SCALE = 4.0
BETA_ONE = 0.9
BETA_TWO = 0.999
EPSILON = 1e-08


def shifted(value, axis, shift):
    size = lax.axis_size(axis)
    return lax.ppermute(value, axis, [(i, (i + shift) % size) for i in range(size)])


def sum_over(partial, axis):
    size = lax.axis_size(axis)
    place = lax.axis_index(axis)
    rows = partial.shape[0] // size

    def block(index):
        return lax.dynamic_slice_in_dim(partial, (index % size) * rows, rows, 0)

    arrived = [shifted(block(place + k), axis, k) for k in range(1, size)]
    total = block(place).astype(jnp.float32)
    for term in arrived:
        total = total + term.astype(jnp.float32)
    total = total.astype(jnp.bfloat16)
    whole = jnp.zeros_like(partial)
    whole = lax.dynamic_update_slice_in_dim(whole, total, place * rows, 0)
    for k in range(1, size):
        whole = lax.dynamic_update_slice_in_dim(
            whole, shifted(total, axis, k), ((place - k) % size) * rows, 0
        )
    return whole


def carried_in(own, keep, axis):
    size = lax.axis_size(axis)
    place = lax.axis_index(axis)
    incoming = jnp.zeros_like(own)
    for k in range(size - 1):
        outgoing = (
            own.astype(jnp.float32) + keep[:, None, None, None] * incoming.astype(jnp.float32)
        ).astype(jnp.bfloat16)
        arrived = lax.ppermute(outgoing, axis, [(k, k + 1)])
        incoming = jnp.where(place == k + 1, arrived, incoming)
    return incoming


def gather_rows(value, axis, dim):
    size = lax.axis_size(axis)
    if size != 2:
        return lax.all_gather(value, axis, axis=dim, tiled=True)
    other = shifted(value, axis, 1)
    low = lax.axis_index(axis) == 0
    return jnp.concatenate([jnp.where(low, value, other), jnp.where(low, other, value)], axis=dim)


def contract_trailing(left, right):
    return lax.dot_general(
        left, right, (((1,), (1,)), ((), ())), preferred_element_type=jnp.float32
    )


def normalize(grads, moments):
    first = BETA_ONE * moments[0] + (1.0 - BETA_ONE) * grads
    second = BETA_TWO * moments[1] + (1.0 - BETA_TWO) * grads * grads
    return (first / (jnp.sqrt(second) + EPSILON)).astype(jnp.bfloat16)


def project(normed, rank_side_projection, right_rows):
    inner = jnp.einsum("kmrd,dc->kmrc", normed, right_rows, preferred_element_type=jnp.float32)
    outer = jnp.einsum(
        "qr,kmrc->kmqc", rank_side_projection, inner, precision=lax.Precision.HIGHEST
    )
    return outer.reshape(outer.shape[0], -1)


def pick_slot(block_parts, index):
    return lax.dynamic_index_in_dim(block_parts, index, 0, keepdims=False)


def per_device(
    attention_output_rows,
    projection_result_gradient,
    adapter_down_weight,
    adapter_up_weight,
    output_projection_weight,
    adam_first_moments,
    adam_second_moments,
    rank_side_projection,
    width_side_projection,
    bounds,
    example_owner_slot,
):
    packs, blk, width_local = attention_output_rows.shape
    width = projection_result_gradient.shape[2]
    adapter_rank_size = adapter_down_weight.shape[1]
    examples = bounds.shape[2]
    seq_index = lax.axis_index("seq")
    tp_index = lax.axis_index("tensor")
    token_count = attention_output_rows.reshape(packs * blk, width_local)
    gradient_complete = projection_result_gradient.reshape(packs * blk, width)
    gradient_columns = lax.dynamic_slice_in_dim(
        gradient_complete, tp_index * width_local, width_local, 1
    )
    reduced_input = jnp.dot(token_count, adapter_down_weight, preferred_element_type=jnp.float32)
    reduced_gradient = contract_trailing(gradient_columns, adapter_up_weight)
    reduced_input = sum_over(reduced_input.astype(jnp.bfloat16), "tensor")
    reduced_gradient = sum_over(reduced_gradient.astype(jnp.bfloat16), "tensor")
    attention_out_gradient = contract_trailing(
        gradient_complete, output_projection_weight
    ) + ADAPTER_SCALE * contract_trailing(reduced_gradient, adapter_down_weight)
    attention_out_gradient = attention_out_gradient.astype(jnp.bfloat16).reshape(
        packs, blk, width_local
    )
    positions = seq_index * blk + jnp.arange(blk, dtype=jnp.int32)
    starts = bounds[:, 0, :]
    example_id = (
        jnp.sum((starts[:, None, :] <= positions[None, :, None]).astype(jnp.int32), axis=2) - 1
    )
    first_id = example_id[:, 0]
    last_id = example_id[:, blk - 1]
    slot_range = jnp.arange(TOUCH, dtype=jnp.int32)
    in_slot = ((example_id - first_id[:, None])[:, :, None] == slot_range).astype(jnp.bfloat16)
    masked_grad = (
        reduced_gradient.reshape(packs, blk, 1, adapter_rank_size) * in_slot[..., None]
    ).reshape(packs, blk, TOUCH * adapter_rank_size)
    masked_in = (
        reduced_input.reshape(packs, blk, 1, adapter_rank_size) * in_slot[..., None]
    ).reshape(packs, blk, TOUCH * adapter_rank_size)
    part_a = jnp.einsum(
        "ptk,ptd->pkd", masked_grad, attention_output_rows, preferred_element_type=jnp.float32
    )
    part_b = jnp.einsum(
        "ptk,ptd->pkd",
        masked_in,
        gradient_columns.reshape(packs, blk, width_local),
        preferred_element_type=jnp.float32,
    )
    parts = ADAPTER_SCALE * jnp.stack(
        [
            part_a.reshape(packs, TOUCH, adapter_rank_size, width_local),
            part_b.reshape(packs, TOUCH, adapter_rank_size, width_local),
        ],
        axis=2,
    )
    block_parts = parts.astype(jnp.bfloat16)
    owner_row = example_owner_slot[0]
    slots = owner_row.shape[0]
    slot_ids = jnp.arange(slots, dtype=jnp.int32)
    stacked_moments = jnp.stack([adam_first_moments, adam_second_moments])
    moments = gather_rows(stacked_moments.astype(jnp.bfloat16), "dp", 2).astype(
        stacked_moments.dtype
    )
    right_rows = lax.dynamic_slice_in_dim(
        width_side_projection, tp_index * width_local, width_local, 0
    )
    example_range = jnp.arange(examples, dtype=jnp.int32)
    ends = bounds[:, 1, :]
    block_low = seq_index * blk
    start_first = jnp.sum(jnp.where(example_range[None, :] == first_id[:, None], starts, 0), axis=1)
    continued = start_first < block_low
    single = first_id == last_id
    keep_flag = (single & continued).astype(jnp.float32)
    last_part = jax.vmap(pick_slot)(block_parts, last_id - first_id)
    carried = carried_in(last_part, keep_flag, "seq").astype(jnp.float32)
    incoming = jnp.where(continued[:, None, None, None], carried, jnp.zeros_like(carried))
    head_mask = (slot_range == 0).astype(jnp.float32)
    totals = (
        block_parts.astype(jnp.float32) + head_mask[None, :, None, None, None] * incoming[:, None]
    )
    normed = normalize(totals.reshape(packs * TOUCH, 2, adapter_rank_size, width_local), moments)
    partial_features = project(normed, rank_side_projection, right_rows)
    slot_example = first_id[:, None] + slot_range[None, :]
    clipped = jnp.clip(slot_example, 0, examples - 1)
    end_of = jnp.sum(
        jnp.where(clipped[:, :, None] == example_range[None, None, :], ends[:, None, :], 0), axis=2
    )
    finished = (slot_range[None, :] <= (last_id - first_id)[:, None]) & (end_of <= block_low + blk)
    flat_example = jnp.arange(packs, dtype=jnp.int32)[:, None] * examples + clipped
    target = jnp.take(owner_row, flat_example.reshape(-1))
    placing = ((target[None, :] == slot_ids[:, None]) & finished.reshape(-1)[None, :]).astype(
        jnp.float32
    )
    buffer = jnp.dot(placing, partial_features, precision=lax.Precision.HIGHEST)
    arrived = lax.all_to_all(
        buffer.astype(jnp.bfloat16), ("seq", "tensor"), split_axis=0, concat_axis=0, tiled=True
    )
    features = jnp.sum(arrived.astype(jnp.float32), axis=0, keepdims=True)
    return (attention_out_gradient, features[None])


def solution(mesh):
    return jax.shard_map(
        per_device,
        mesh=mesh,
        in_specs=(
            P("dp", "seq", "tensor"),
            P("dp", "seq", None),
            P("tensor", None),
            P(None, "tensor"),
            P("tensor", None),
            P(None, "dp", "tensor"),
            P(None, "dp", "tensor"),
            P(),
            P(),
            P("dp", None, None),
            P("dp", None),
        ),
        out_specs=(P("dp", "seq", "tensor"), P("dp", ("seq", "tensor"), None)),
        check_vma=False,
    )
```

```python
import functools

import jax
import jax.numpy as jnp
from jax import lax
from jax.experimental import pallas as pl
from jax.experimental.pallas import tpu as pltpu
from jax.sharding import PartitionSpec as P

TOUCH = 8
ADAPTER_SCALE = 4.0
BETA_ONE = 0.9
BETA_TWO = 0.999
EPSILON = 1e-08
VMEM_LIMIT = 48 * 2**20
BF16 = jnp.bfloat16
F32 = jnp.float32

ANY = pl.BlockSpec(memory_space=pl.ANY)
VMEM = pl.BlockSpec(memory_space=pltpu.VMEM)
SMEM = pl.BlockSpec(memory_space=pltpu.SMEM)


def dot_trailing(left, right):
    return lax.dot_general(left, right, (((1,), (1,)), ((), ())), preferred_element_type=F32)


def call(kernel, out_shape, in_specs, out_specs, scratch, flops, nbytes, name, aliases=None):
    return pl.pallas_call(
        kernel,
        out_shape=out_shape,
        in_specs=in_specs,
        out_specs=out_specs,
        scratch_shapes=scratch,
        input_output_aliases=aliases or {},
        compiler_params=pltpu.CompilerParams(vmem_limit_bytes=VMEM_LIMIT),
        cost_estimate=pl.CostEstimate(flops=flops, bytes_accessed=nbytes, transcendentals=0),
        name=name,
    )


def pieces_kernel(along_rows, source, weight, *rest):
    *outs, buf, sem = rest
    size = len(outs)
    place = lax.axis_index("tensor")
    rows, width = buf.shape[1:]
    first = 0 if source.shape[1] == width else pl.multiple_of(place * width, width)

    def copy(k):
        block = pl.multiple_of(lax.rem(place + k, size) * rows, rows)
        return pltpu.make_async_copy(
            source.at[pl.ds(block, rows), pl.ds(first, width)], buf.at[k], sem.at[k]
        )

    order = list(range(1, size)) + [0]
    for k in order:
        copy(k).start()
    for k in order:
        copy(k).wait()
        if along_rows:
            outs[k][...] = jnp.dot(buf[k], weight[...], preferred_element_type=F32).T.astype(BF16)
        else:
            outs[k][...] = dot_trailing(weight[...], buf[k]).astype(BF16)


def rank_pieces(source, weight, along_rows, size, width, name):
    tokens = source.shape[0]
    rank = weight.shape[1] if along_rows else weight.shape[0]
    rows = tokens // size
    return call(
        functools.partial(pieces_kernel, along_rows),
        [jax.ShapeDtypeStruct((rank, rows), BF16)] * size,
        [ANY, VMEM],
        [VMEM] * size,
        [pltpu.VMEM((size, rows, width), BF16), pltpu.SemaphoreType.DMA((size,))],
        2 * tokens * width * rank,
        2 * tokens * width,
        name,
    )(source, weight)


def shifted(value, axis, shift):
    size = lax.axis_size(axis)
    return lax.ppermute(value, axis, [(i, (i + shift) % size) for i in range(size)])


def scatter_sum(pieces):
    arrived = [shifted(piece, "tensor", k) for k, piece in enumerate(pieces) if k]
    total = pieces[0].astype(F32)
    for term in arrived:
        total = total + term.astype(F32)
    return total.astype(BF16)


def gather_pieces(total):
    size = lax.axis_size("tensor")
    return [total] + [shifted(total, "tensor", k) for k in range(1, size)]


def example_scalars(bounds, block):
    low = lax.axis_index("seq") * block
    count = bounds.shape[2]
    first = jnp.int32(-1)
    last = jnp.int32(-1)
    for e in range(count):
        start = bounds[0, 0, e]
        first = first + (start <= low).astype(jnp.int32)
        last = last + (start <= low + block - 1).astype(jnp.int32)
    return low, first, last


def place_pieces(pieces, low_scratch):
    size = len(pieces)
    place = lax.axis_index("tensor")
    for k, piece in enumerate(pieces):
        low_scratch[lax.rem(place + size - k, size)] = piece[...]


def masked(low_piece, offset, start, end):
    tokens = offset + lax.broadcasted_iota(jnp.int32, low_piece.shape, 1)
    return jnp.where((tokens >= start) & (tokens < end), low_piece.astype(F32), 0.0).astype(BF16)


def column_copies(source, buf, sem):
    tiles, tokens, columns = buf.shape
    width = tiles * columns
    first = 0 if source.shape[1] == width else lax.axis_index("tensor") * width
    return [
        pltpu.make_async_copy(
            source.at[:, pl.ds(pl.multiple_of(first + t * columns, columns), columns)],
            buf.at[t],
            sem.at[t],
        )
        for t in range(tiles)
    ]


def tail_kernel(size, bounds, source, *rest):
    pieces = rest[:size]
    out, buf, low_scratch, left, sem = rest[size:]
    copies = column_copies(source, buf, sem)
    for c in copies:
        c.start()
    tokens, columns = buf.shape[1:]
    rows = tokens // size
    low, _, last = example_scalars(bounds, tokens)
    start, end = bounds[0, 0, last], bounds[0, 1, last]
    place_pieces(pieces, low_scratch)
    for c in range(size):
        left[:, c * rows : (c + 1) * rows] = masked(low_scratch[c], low + c * rows, start, end)
    for t, c in enumerate(copies):
        c.wait()
        part = jnp.dot(left[...], buf[t], preferred_element_type=F32)
        out[:, t * columns : (t + 1) * columns] = (ADAPTER_SCALE * part).astype(BF16)


def tail_part(bounds, source, pieces, width, name):
    size = len(pieces)
    rank, rows = pieces[0].shape
    tokens = source.shape[0]
    tiles = width // 256
    return call(
        functools.partial(tail_kernel, size),
        jax.ShapeDtypeStruct((rank, width), BF16),
        [SMEM, ANY] + [VMEM] * size,
        VMEM,
        [
            pltpu.VMEM((tiles, tokens, width // tiles), BF16),
            pltpu.VMEM((size, rank, rows), BF16),
            pltpu.VMEM((rank, tokens), BF16),
            pltpu.SemaphoreType.DMA((tiles,)),
        ],
        2 * tokens * width * rank,
        2 * tokens * width,
        name,
    )(bounds, source, *pieces)


def normalize(grads, first_moment, second_moment):
    first = BETA_ONE * first_moment + (1.0 - BETA_ONE) * grads
    second = BETA_TWO * second_moment + ((1.0 - BETA_TWO) * grads) * grads
    guess = lax.rsqrt(second)
    below = second * guess + EPSILON
    return first * (guess * (2.0 - below * guess))


def split_two(value):
    high = value.astype(BF16)
    return high, (value - high.astype(F32)).astype(BF16)


def rank_side_blocks(rank_side, blocks):
    high, low = split_two(rank_side[...])
    rows, rank = high.shape
    blocks[...] = jnp.zeros_like(blocks)
    for i, term in enumerate((high, low)):
        for m in range(2):
            at = (2 * i + m) * rows
            blocks[at : at + rows, m * rank : (m + 1) * rank] = term


def project_rank(blocks, normed):
    both = jnp.dot(blocks[...], normed[...], preferred_element_type=F32)
    half = both.shape[0] // 2
    return both[:half] + both[half:]


def project_width(value, right):
    high, low = split_two(value)
    return jnp.dot(high, right, preferred_element_type=F32) + jnp.dot(
        low, right, preferred_element_type=F32
    )


def slot_end(bounds, index):
    return bounds[0, 1, jnp.minimum(index, bounds.shape[2] - 1)]


def slots_kernel(size, bounds, owner, source_grad, source_in, moments, rank_side, width_side, *rest):
    pieces_grad, pieces_in = rest[:size], rest[size : 2 * size]
    out, head, buf, low_scratch, left, parts, normed, blocks, ranked, wide, right, sem, right_sem = rest[
        2 * size :
    ]
    copies = [column_copies(s, buf.at[m], sem.at[m]) for m, s in enumerate((source_grad, source_in))]
    rows_here = right.shape[0]
    right_copy = pltpu.make_async_copy(
        width_side.at[
            pl.ds(pl.multiple_of(lax.axis_index("tensor") * rows_here, rows_here), rows_here)
        ],
        right,
        right_sem,
    )
    for m in range(2):
        for c in copies[m]:
            c.start()
    right_copy.start()
    tokens, columns = buf.shape[2:]
    rank = head.shape[1]
    rows = tokens // size
    low, first, last = example_scalars(bounds, tokens)
    count = bounds.shape[2]
    rank_side_blocks(rank_side, blocks)
    for m, pieces in enumerate((pieces_grad, pieces_in)):
        place_pieces(pieces, low_scratch.at[m])
        for j in range(TOUCH):
            index = jnp.minimum(first + j, count - 1)
            used = first + j <= last
            start = jnp.where(used, bounds[0, 0, index], 0)
            end = jnp.where(used, bounds[0, 1, index], 0)
            for c in range(size):
                left[m, j * rank : (j + 1) * rank, c * rows : (c + 1) * rows] = masked(
                    low_scratch[m, c], low + c * rows, start, end
                )
        for t, c in enumerate(copies[m]):
            c.wait()
            part = jnp.dot(left[m], buf[m, t], preferred_element_type=F32)
            parts[:, m, :, t * columns : (t + 1) * columns] = (
                (ADAPTER_SCALE * part).astype(BF16).reshape(TOUCH, rank, columns)
            )
        head[m] = parts[0, m]

    def ends_here(j):
        return (first + j <= last) & (slot_end(bounds, first + j) <= low + tokens)

    step = 16

    @pl.loop(1, TOUCH)
    def _(j):
        @pl.when(ends_here(j))
        def _():
            for m in range(2):
                for r in range(0, rank, step):
                    grads = parts[j, m, r : r + step, :].astype(F32)
                    normed[m * rank + r : m * rank + r + step, :] = normalize(
                        grads,
                        moments[0, m, r : r + step, :].astype(F32),
                        moments[1, m, r : r + step, :].astype(F32),
                    ).astype(BF16)
            ranked[j] = project_rank(blocks, normed)

    right_copy.wait()
    width = ranked.shape[2]
    wide[...] = project_width(ranked[...].reshape(-1, width), right[...]).reshape(wide.shape)
    out[...] = jnp.zeros_like(out)
    for j in range(1, TOUCH):

        @pl.when(ends_here(j))
        def _():
            out[owner[0, jnp.minimum(first + j, count - 1)]] = wide[j].astype(BF16)


def slot_features(
    bounds, owner, source_grad, source_in, moments, rank_side, width_side, pieces_grad, pieces_in
):
    size = len(pieces_in)
    rank, rows = pieces_in[0].shape
    tokens, width = source_grad.shape
    tiles = width // 256
    lines = rank_side.shape[0]
    columns = width_side.shape[1]
    return call(
        functools.partial(slots_kernel, size),
        [
            jax.ShapeDtypeStruct((owner.shape[1], 2 * lines, columns), BF16),
            jax.ShapeDtypeStruct((2, rank, width), BF16),
        ],
        [SMEM, SMEM, ANY, ANY, VMEM, VMEM, ANY] + [VMEM] * (2 * size),
        [VMEM, VMEM],
        [
            pltpu.VMEM((2, tiles, tokens, width // tiles), BF16),
            pltpu.VMEM((2, size, rank, rows), BF16),
            pltpu.VMEM((2, TOUCH * rank, tokens), BF16),
            pltpu.VMEM((TOUCH, 2, rank, width), BF16),
            pltpu.VMEM((2 * rank, width), BF16),
            pltpu.VMEM((4 * lines, 2 * rank), BF16),
            pltpu.VMEM((TOUCH, 2 * lines, width), F32),
            pltpu.VMEM((TOUCH, 2 * lines, columns), F32),
            pltpu.VMEM((width, columns), BF16),
            pltpu.SemaphoreType.DMA((2, tiles)),
            pltpu.SemaphoreType.DMA,
        ],
        4 * tokens * width * rank * TOUCH,
        4 * tokens * width,
        "slot_features",
    )(
        bounds,
        owner,
        source_grad,
        source_in,
        moments,
        rank_side,
        width_side,
        *pieces_grad,
        *pieces_in,
    )


def head_kernel(hops, block, bounds, owner, filled, head, moments, rank_side, width_side, *rest):
    arrived = rest[: 2 * hops]
    out, normed, blocks, right, right_sem = rest[2 * hops :]
    rows_here = right.shape[0]
    right_copy = pltpu.make_async_copy(
        width_side.at[
            pl.ds(pl.multiple_of(lax.axis_index("tensor") * rows_here, rows_here), rows_here)
        ],
        right,
        right_sem,
    )
    right_copy.start()
    low, first, last = example_scalars(bounds, block)
    rank = head.shape[1]
    continued = (bounds[0, 0, first] < low).astype(F32)
    rank_side_blocks(rank_side, blocks)
    step = 16
    for m in range(2):
        for r in range(0, rank, step):
            incoming = arrived[m * hops][r : r + step, :].astype(F32)
            for k in range(1, hops):
                incoming = incoming + arrived[m * hops + k][r : r + step, :].astype(F32)
            grads = head[m, r : r + step, :].astype(F32) + continued * incoming
            normed[m * rank + r : m * rank + r + step, :] = normalize(
                grads,
                moments[0, m, r : r + step, :].astype(F32),
                moments[1, m, r : r + step, :].astype(F32),
            ).astype(BF16)
    out[...] = filled[...]
    ranked = project_rank(blocks, normed)
    right_copy.wait()
    wide = project_width(ranked, right[...])

    @pl.when(slot_end(bounds, first) <= low + block)
    def _():
        out[owner[0, first]] = wide.astype(BF16)


def head_features(bounds, owner, filled, head, moments, rank_side, width_side, arrived, block):
    hops = len(arrived[0])
    rank, width = head.shape[1:]
    lines = rank_side.shape[0]
    columns = width_side.shape[1]
    return call(
        functools.partial(head_kernel, hops, block),
        jax.ShapeDtypeStruct(filled.shape, BF16),
        [SMEM, SMEM, VMEM, VMEM, VMEM, VMEM, ANY] + [VMEM] * (2 * hops),
        VMEM,
        [
            pltpu.VMEM((2 * rank, width), BF16),
            pltpu.VMEM((4 * lines, 2 * rank), BF16),
            pltpu.VMEM((width, columns), BF16),
            pltpu.SemaphoreType.DMA,
        ],
        2 * width * 2 * rank * 4 * lines,
        8 * rank * width,
        "head_features",
    )(bounds, owner, filled, head, moments, rank_side, width_side, *arrived[0], *arrived[1])


def first_kernel(steps, rows_ref, weight, out):
    k = pl.program_id(0)
    term = dot_trailing(rows_ref[...], weight[...])

    @pl.when(k == 0)
    def _():
        out[...] = term

    @pl.when(k > 0)
    def _():
        out[...] += term


def second_kernel(steps, split, size, rows_ref, weight, down, done, *rest):
    pieces, out, acc, low_scratch = rest[:size], rest[size], rest[size + 1], rest[size + 2]
    k = pl.program_id(0)
    term = dot_trailing(rows_ref[...], weight[...])

    @pl.when(k == 0)
    def _():
        acc[...] = term

    @pl.when((k > 0) & (k < steps - 1))
    def _():
        acc[...] += term

    @pl.when(k == steps - 1)
    def _():
        place_pieces(pieces, low_scratch)
        rows = out.shape[0] // size
        for c in range(size):
            here = slice(c * rows, (c + 1) * rows)
            extra = ADAPTER_SCALE * dot_trailing(low_scratch[c].astype(F32).T.astype(BF16), down[...])
            out[here, :split] = (done[here, :] + extra[:, :split]).astype(BF16)
            out[here, split:] = (acc[here, :] + term[here, :] + extra[:, split:]).astype(BF16)


def first_product(rows, weight, split, tile):
    tokens, depth = rows.shape
    steps = depth // tile
    return pl.pallas_call(
        functools.partial(first_kernel, steps),
        out_shape=jax.ShapeDtypeStruct((tokens, split), F32),
        grid=(steps,),
        in_specs=[
            pl.BlockSpec((tokens, tile), lambda k: (0, k)),
            pl.BlockSpec((split, tile), lambda k: (0, k)),
        ],
        out_specs=pl.BlockSpec((tokens, split), lambda k: (0, 0)),
        compiler_params=pltpu.CompilerParams(vmem_limit_bytes=VMEM_LIMIT),
        cost_estimate=pl.CostEstimate(
            flops=2 * tokens * depth * split,
            bytes_accessed=2 * depth * (tokens + split),
            transcendentals=0,
        ),
        name="first_product",
    )(rows, weight)


def second_product(rows, weight, down, done, pieces, tile):
    tokens, depth = rows.shape
    width, rank = down.shape
    split = done.shape[1]
    rest = width - split
    steps = depth // tile
    size = len(pieces)
    whole = lambda k: (0, 0)
    return pl.pallas_call(
        functools.partial(second_kernel, steps, split, size),
        out_shape=jax.ShapeDtypeStruct((tokens, width), BF16),
        grid=(steps,),
        in_specs=[
            pl.BlockSpec((tokens, tile), lambda k: (0, k)),
            pl.BlockSpec((rest, tile), lambda k: (split // rest, k)),
            pl.BlockSpec((width, rank), whole),
            pl.BlockSpec((tokens, split), whole),
        ]
        + [pl.BlockSpec(pieces[0].shape, whole)] * size,
        out_specs=pl.BlockSpec((tokens, width), whole),
        scratch_shapes=[
            pltpu.VMEM((tokens, rest), F32),
            pltpu.VMEM((size,) + pieces[0].shape, BF16),
        ],
        compiler_params=pltpu.CompilerParams(vmem_limit_bytes=VMEM_LIMIT),
        cost_estimate=pl.CostEstimate(
            flops=2 * tokens * depth * rest,
            bytes_accessed=2 * depth * (tokens + rest),
            transcendentals=0,
        ),
        name="second_product",
    )(rows, weight, down, done, *pieces)


def carry_chain(tail, keep):
    arrived = []
    outgoing = tail
    for k in range(lax.axis_size("seq") - 1):
        arrived.append(lax.ppermute(outgoing, "seq", [(k, k + 1)]))
        outgoing = (tail.astype(F32) + keep * arrived[-1].astype(F32)).astype(BF16)
    return arrived


def gather_rows(value, axis, dim):
    size = lax.axis_size(axis)
    if size != 2:
        return lax.all_gather(value, axis, axis=dim, tiled=True)
    other = shifted(value, axis, 1)
    low = lax.axis_index(axis) == 0
    return jnp.concatenate([jnp.where(low, value, other), jnp.where(low, other, value)], axis=dim)


def per_device(
    attention_output_rows,
    projection_result_gradient,
    adapter_down_weight,
    adapter_up_weight,
    output_projection_weight,
    adam_first_moments,
    adam_second_moments,
    rank_side_projection,
    width_side_projection,
    bounds,
    example_owner_slot,
):
    packs, blk, width_local = attention_output_rows.shape
    assert packs == 1
    width = projection_result_gradient.shape[2]
    size = lax.axis_size("tensor")
    rows_in = attention_output_rows.reshape(blk, width_local)
    rows_grad = projection_result_gradient.reshape(blk, width)

    partial_in = rank_pieces(rows_in, adapter_down_weight, True, size, width_local, "pieces_in")
    partial_grad = rank_pieces(rows_grad, adapter_up_weight, False, size, width_local, "pieces_grad")
    low_in = gather_pieces(scatter_sum(partial_in))
    low_grad = gather_pieces(scatter_sum(partial_grad))
    stacked = jnp.stack([adam_first_moments, adam_second_moments]).astype(BF16)
    moments = gather_rows(stacked, "dp", 2)
    done = first_product(rows_grad, output_projection_weight, width_local // 2, 1024)

    low = lax.axis_index("seq") * blk
    starts, ends = bounds[0, 0], bounds[0, 1]
    spans = jnp.any((starts < low) & (ends >= low + blk)).astype(F32)

    tail_in = tail_part(bounds, rows_grad, low_in, width_local, "tail_in")
    tail_grad = tail_part(bounds, rows_in, low_grad, width_local, "tail_grad")
    arrived_in = carry_chain(tail_in, spans)
    arrived_grad = carry_chain(tail_grad, spans)
    filled, head = slot_features(
        bounds,
        example_owner_slot,
        rows_in,
        rows_grad,
        moments,
        rank_side_projection,
        width_side_projection,
        low_grad,
        low_in,
    )
    buffer = head_features(
        bounds,
        example_owner_slot,
        filled,
        head,
        moments,
        rank_side_projection,
        width_side_projection,
        (arrived_grad, arrived_in),
        blk,
    )
    arrived = lax.all_to_all(buffer, ("seq", "tensor"), split_axis=0, concat_axis=0, tiled=True)
    features = jnp.sum(arrived.astype(F32), axis=0).reshape(1, 1, -1)
    out = second_product(
        rows_grad, output_projection_weight, adapter_down_weight, done, low_grad, 1024
    )
    return (out.reshape(attention_output_rows.shape), features)


def solution(mesh):
    return jax.shard_map(
        per_device,
        mesh=mesh,
        in_specs=(
            P("dp", "seq", "tensor"),
            P("dp", "seq", None),
            P("tensor", None),
            P(None, "tensor"),
            P("tensor", None),
            P(None, "dp", "tensor"),
            P(None, "dp", "tensor"),
            P(),
            P(),
            P("dp", None, None),
            P("dp", None),
        ),
        out_specs=(P("dp", "seq", "tensor"), P("dp", ("seq", "tensor"), None)),
        check_vma=False,
    )
```

```python
import functools

import jax
import jax.numpy as jnp
from jax import lax
from jax.experimental import pallas as pl
from jax.experimental.pallas import tpu as pltpu
from jax.sharding import PartitionSpec as P

TOUCH = 8
ADAPTER_SCALE = 4.0
BETA_ONE = 0.9
BETA_TWO = 0.999
EPSILON = 1e-08
VMEM_LIMIT = 32 * 2**20
BF16 = jnp.bfloat16
F32 = jnp.float32

HBM = pl.BlockSpec(memory_space=pltpu.HBM)
VMEM = pl.BlockSpec(memory_space=pltpu.VMEM)
SMEM = pl.BlockSpec(memory_space=pltpu.SMEM)


def dot_trailing(left, right):
    return lax.dot_general(left, right, (((1,), (1,)), ((), ())), preferred_element_type=F32)


def call(kernel, out_shape, in_specs, out_specs, scratch, flops, nbytes, name, aliases=None):
    return pl.pallas_call(
        kernel,
        out_shape=out_shape,
        in_specs=in_specs,
        out_specs=out_specs,
        scratch_shapes=scratch,
        input_output_aliases=aliases or {},
        compiler_params=pltpu.CompilerParams(vmem_limit_bytes=VMEM_LIMIT),
        cost_estimate=pl.CostEstimate(flops=flops, bytes_accessed=nbytes, transcendentals=0),
        name=name,
    )


def pieces_kernel(along_rows, source, weight, *rest):
    *outs, columns, weight_buf, sem, weight_sem = rest
    size = len(outs)
    place = lax.axis_index("tensor")
    tokens, width = columns.shape
    rows = tokens // size
    first = 0 if source.shape[1] == width else pl.multiple_of(place * width, width)

    def rows_of(k):
        return pl.ds(pl.multiple_of(lax.rem(place + k, size) * rows, rows), rows)

    def copy(k):
        return pltpu.make_async_copy(
            source.at[rows_of(k), pl.ds(first, width)], columns.at[rows_of(k)], sem.at[k]
        )

    order = list(range(1, size)) + [0]
    weight_copy = pltpu.make_async_copy(weight, weight_buf, weight_sem)
    weight_copy.start()
    for k in order:
        copy(k).start()
    weight_copy.wait()
    for k in order:
        copy(k).wait()
        block = columns[rows_of(k), :]
        if along_rows:
            product = jnp.dot(block, weight_buf[...], preferred_element_type=F32)
        else:
            product = dot_trailing(block, weight_buf[...])
        outs[k][...] = product.T.astype(BF16)


def rank_pieces(source, weight, along_rows, size, width, name):
    tokens = source.shape[0]
    rank = weight.shape[1] if along_rows else weight.shape[0]
    rows = tokens // size
    *pieces, columns = call(
        functools.partial(pieces_kernel, along_rows),
        [jax.ShapeDtypeStruct((rank, rows), BF16)] * size
        + [jax.ShapeDtypeStruct((tokens, width), BF16)],
        [HBM, HBM],
        [VMEM] * (size + 1),
        [
            pltpu.VMEM(weight.shape, BF16),
            pltpu.SemaphoreType.DMA((size,)),
            pltpu.SemaphoreType.DMA,
        ],
        2 * tokens * width * rank,
        2 * tokens * width,
        name,
    )(source, weight)
    return pieces, columns


def shifted(value, axis, shift):
    size = lax.axis_size(axis)
    return lax.ppermute(value, axis, [(i, (i + shift) % size) for i in range(size)])


def scatter(pieces):
    return [shifted(piece, "tensor", k) if k else piece for k, piece in enumerate(pieces)]


def total_of(terms):
    total = terms[0].astype(F32)
    for term in terms[1:]:
        total = total + term.astype(F32)
    return total.astype(BF16)


def gather_pieces(total):
    size = lax.axis_size("tensor")
    return [total] + [shifted(total, "tensor", k) for k in range(1, size)]


def example_scalars(bounds, block):
    low = lax.axis_index("seq") * block
    count = bounds.shape[2]
    first = jnp.int32(-1)
    last = jnp.int32(-1)
    for e in range(count):
        start = bounds[0, 0, e]
        first = first + (start <= low).astype(jnp.int32)
        last = last + (start <= low + block - 1).astype(jnp.int32)
    return low, first, last


def place_pieces(pieces, low_scratch):
    size = len(pieces)
    place = lax.axis_index("tensor")
    for k, piece in enumerate(pieces):
        low_scratch[lax.rem(place + size - k, size)] = piece[...]


def masked(low_piece, offset, start, end):
    tokens = offset + lax.broadcasted_iota(jnp.int32, low_piece.shape, 1)
    return jnp.where((tokens >= start) & (tokens < end), low_piece.astype(F32), 0.0).astype(BF16)


def tails_kernel(size, bounds, rows_in, rows_grad, *rest):
    pieces = rest[: 2 * size]
    out, low_scratch, acc = rest[2 * size :]
    tokens, width = rows_in.shape
    rows = tokens // size
    low, _, last = example_scalars(bounds, tokens)
    start = bounds[0, 0, last]
    for m, source in enumerate((rows_in, rows_grad)):
        place_pieces(pieces[m * size : (m + 1) * size], low_scratch)

        def chunk(c):
            left = masked(low_scratch[c], low + c * rows, start, low + tokens)
            return jnp.dot(left, source[c * rows : (c + 1) * rows, :], preferred_element_type=F32)

        acc[...] = chunk(size - 1)
        for c in range(size - 1):

            @pl.when(start < low + (c + 1) * rows)
            def _():
                acc[...] += chunk(c)

        out[m] = (ADAPTER_SCALE * acc[...]).astype(BF16)


def tail_parts(bounds, rows_in, rows_grad, low_grad, low_in):
    size = len(low_in)
    rank, rows = low_in[0].shape
    tokens, width = rows_in.shape
    return call(
        functools.partial(tails_kernel, size),
        jax.ShapeDtypeStruct((2, rank, width), BF16),
        [SMEM] + [VMEM] * (2 + 2 * size),
        VMEM,
        [pltpu.VMEM((size, rank, rows), BF16), pltpu.VMEM((rank, width), F32)],
        4 * tokens * width * rank,
        4 * tokens * width,
        "tail_parts",
    )(bounds, rows_in, rows_grad, *low_grad, *low_in)


def normalize(grads, first_moment, second_moment):
    first = BETA_ONE * first_moment + (1.0 - BETA_ONE) * grads
    second = BETA_TWO * second_moment + ((1.0 - BETA_TWO) * grads) * grads
    guess = lax.rsqrt(second)
    below = second * guess + EPSILON
    return first * (guess * (2.0 - below * guess))


def split_two(value):
    high = value.astype(BF16)
    return high, (value - high.astype(F32)).astype(BF16)


def project_rank(rank_side, normed):
    both = jnp.dot(
        jnp.concatenate(split_two(rank_side[...]), axis=0), normed, preferred_element_type=F32
    )
    half = both.shape[0] // 2
    return both[:half] + both[half:]


def project_width(value, right):
    high, low = split_two(value)
    return jnp.dot(high, right, preferred_element_type=F32) + jnp.dot(
        low, right, preferred_element_type=F32
    )


def right_rows_copy(width_side, right, sem):
    rows = right.shape[0]
    first = pl.multiple_of(lax.axis_index("tensor") * rows, rows)
    return pltpu.make_async_copy(width_side.at[pl.ds(first, rows)], right, sem)


def slots_kernel(m, size, bounds, owner, source, moments, rank_side, width_side, *rest):
    pieces = rest[:size]
    out, head, low_scratch, acc, normed, ranked, wide, right, sem = rest[size:]
    right_copy = right_rows_copy(width_side, right, sem)
    right_copy.start()
    tokens, width = source.shape
    rank = head.shape[0]
    rows = tokens // size
    low, first, last = example_scalars(bounds, tokens)
    count = bounds.shape[2]
    place_pieces(pieces, low_scratch)
    step = 16

    def slot(j):
        return jnp.minimum(first + j, count - 1)

    def ends_here(j):
        return (first + j <= last) & (bounds[0, 1, slot(j)] <= low + tokens)

    @pl.loop(0, TOUCH)
    def _(j):
        start, end = bounds[0, 0, slot(j)], bounds[0, 1, slot(j)]

        @pl.when(ends_here(j) | (j == 0))
        def _():
            for c in range(size):
                begin = low + c * rows

                @pl.when((start < begin + rows) & (end > begin))
                def _():
                    left = masked(low_scratch[c], begin, start, end)
                    term = jnp.dot(
                        left, source[c * rows : (c + 1) * rows, :], preferred_element_type=F32
                    )
                    fresh = (start >= begin) | (c == 0)
                    acc[...] = jnp.where(fresh, 0.0, acc[...]) + term

            @pl.when(j == 0)
            def _():
                head[...] = (ADAPTER_SCALE * acc[...]).astype(BF16)

            @pl.when(j > 0)
            def _():
                for r in range(0, rank, step):
                    normed[r : r + step, :] = normalize(
                        ADAPTER_SCALE * acc[r : r + step, :],
                        moments[0, m, r : r + step, :].astype(F32),
                        moments[1, m, r : r + step, :].astype(F32),
                    ).astype(BF16)
                ranked[j] = project_rank(rank_side, normed[...])

    right_copy.wait()
    wide[...] = project_width(ranked[...].reshape(-1, width), right[...]).reshape(wide.shape)
    out[...] = jnp.zeros_like(out)
    for j in range(1, TOUCH):

        @pl.when(ends_here(j))
        def _():
            out[owner[0, slot(j)]] = wide[j].astype(BF16)


def slot_features(
    m, bounds, owner, source, moments, rank_side, width_side, pieces, name
):
    size = len(pieces)
    rank, rows = pieces[0].shape
    tokens, width = source.shape
    lines = rank_side.shape[0]
    columns = width_side.shape[1]
    return call(
        functools.partial(slots_kernel, m, size),
        [
            jax.ShapeDtypeStruct((owner.shape[1], lines, columns), BF16),
            jax.ShapeDtypeStruct((rank, width), BF16),
        ],
        [SMEM, SMEM, VMEM, VMEM, VMEM, HBM] + [VMEM] * size,
        [VMEM, VMEM],
        [
            pltpu.VMEM((size, rank, rows), BF16),
            pltpu.VMEM((rank, width), F32),
            pltpu.VMEM((rank, width), BF16),
            pltpu.VMEM((TOUCH, lines, width), F32),
            pltpu.VMEM((TOUCH, lines, columns), F32),
            pltpu.VMEM((width, columns), BF16),
            pltpu.SemaphoreType.DMA,
        ],
        2 * tokens * width * rank * TOUCH,
        4 * tokens * width,
        name,
    )(bounds, owner, source, moments, rank_side, width_side, *pieces)


def head_kernel(
    hops, block, bounds, owner, filled_grad, filled_in, head_grad, head_in, moments, rank_side, width_side, *rest
):
    arrived = rest[:hops]
    out, normed, ranked, right, sem = rest[hops:]
    right_copy = right_rows_copy(width_side, right, sem)
    right_copy.start()
    low, first, last = example_scalars(bounds, block)
    rank = head_in.shape[0]
    lines = rank_side.shape[0]
    continued = (bounds[0, 0, first] < low).astype(F32)
    step = 16
    out[:, :lines] = filled_grad[...]
    out[:, lines:] = filled_in[...]
    ends = bounds[0, 1, first] <= low + block

    @pl.when(ends)
    def _():
        for m, head in enumerate((head_grad, head_in)):
            for r in range(0, rank, step):
                here = slice(r, r + step)
                incoming = arrived[0][m, here, :].astype(F32)
                for k in range(1, hops):
                    incoming = incoming + arrived[k][m, here, :].astype(F32)
                normed[here, :] = normalize(
                    head[here, :].astype(F32) + continued * incoming,
                    moments[0, m, here, :].astype(F32),
                    moments[1, m, here, :].astype(F32),
                ).astype(BF16)
            ranked[m * lines : (m + 1) * lines, :] = project_rank(rank_side, normed[...])

    right_copy.wait()

    @pl.when(ends)
    def _():
        out[owner[0, first]] = project_width(ranked[...], right[...]).astype(BF16)


def head_features(
    bounds, owner, filled_grad, filled_in, head_grad, head_in, moments, rank_side, width_side, arrived, block
):
    hops = len(arrived)
    rank, width = head_in.shape
    slots, lines, columns = filled_in.shape
    return call(
        functools.partial(head_kernel, hops, block),
        jax.ShapeDtypeStruct((slots, 2 * lines, columns), BF16),
        [SMEM, SMEM] + [VMEM] * 6 + [HBM] + [VMEM] * hops,
        VMEM,
        [
            pltpu.VMEM((rank, width), BF16),
            pltpu.VMEM((2 * lines, width), F32),
            pltpu.VMEM((width, columns), BF16),
            pltpu.SemaphoreType.DMA,
        ],
        2 * width * 2 * rank * 4 * lines,
        8 * rank * width,
        "head_features",
    )(
        bounds,
        owner,
        filled_grad,
        filled_in,
        head_grad,
        head_in,
        moments,
        rank_side,
        width_side,
        *arrived,
    )


TILE = 256


def first_kernel(source, weight, out, held, weight_buf, source_sem, weight_sem):
    blocks = held.shape[0] // TILE
    parts = weight_buf.shape[0] // TILE

    def rows_copy(i):
        here = pl.ds(pl.multiple_of(i * TILE, TILE), TILE)
        return pltpu.make_async_copy(source.at[here], held.at[here], source_sem.at[i])

    def weight_copy(n):
        here = pl.ds(n * TILE, TILE)
        return pltpu.make_async_copy(weight.at[here], weight_buf.at[here], weight_sem.at[n])

    weight_copy(0).start()
    rows_copy(0).start()
    for n in range(1, parts):
        weight_copy(n).start()
    for i in range(1, blocks):
        rows_copy(i).start()

    @pl.loop(0, blocks)
    def _(i):
        rows_copy(i).wait()
        here = pl.ds(pl.multiple_of(i * TILE, TILE), TILE)
        for n in range(parts):

            @pl.when(i == 0)
            def _():
                weight_copy(n).wait()

            there = slice(n * TILE, (n + 1) * TILE)
            out[here, there] = dot_trailing(held[here, :], weight_buf[there, :])


def second_kernel(size, held, weight, down, done, *rest):
    pieces = rest[:size]
    out, result, low_scratch, low_rows, weight_buf, weight_sem, out_sem = rest[size:]
    tokens, width = result.shape
    split = done.shape[1]
    parts = weight_buf.shape[0] // TILE
    rows = tokens // size

    def weight_copy(n):
        return pltpu.make_async_copy(
            weight.at[pl.ds(split + n * TILE, TILE)],
            weight_buf.at[pl.ds(n * TILE, TILE)],
            weight_sem.at[n],
        )

    def out_copy(first, columns, k):
        here = pl.ds(first, columns)
        return pltpu.make_async_copy(result.at[:, here], out.at[:, here], out_sem.at[k])

    for n in range(parts):
        weight_copy(n).start()
    place_pieces(pieces, low_scratch)
    for c in range(size):
        here = slice(c * rows, (c + 1) * rows)
        low_rows[here, :] = low_scratch[c].astype(F32).T.astype(BF16)
        extra = ADAPTER_SCALE * dot_trailing(low_rows[here, :], down[:split, :])
        result[here, :split] = (done[here, :] + extra).astype(BF16)
    out_copy(0, split, 0).start()
    for n in range(parts):
        weight_copy(n).wait()

        @pl.loop(0, tokens // TILE)
        def _(i):
            here = pl.ds(pl.multiple_of(i * TILE, TILE), TILE)
            first = split + n * TILE
            extra = dot_trailing(low_rows[here, :], down[first : first + TILE, :])
            term = dot_trailing(held[here, :], weight_buf[n * TILE : (n + 1) * TILE, :])
            result[here, first : first + TILE] = (term + ADAPTER_SCALE * extra).astype(BF16)

        out_copy(split + n * TILE, TILE, n + 1).start()
    out_copy(0, split, 0).wait()
    for n in range(parts):
        out_copy(split + n * TILE, TILE, n + 1).wait()


def first_product(rows, weight, split):
    tokens, depth = rows.shape
    return call(
        first_kernel,
        [jax.ShapeDtypeStruct((tokens, split), F32), jax.ShapeDtypeStruct((tokens, depth), BF16)],
        [HBM, HBM],
        [VMEM, VMEM],
        [
            pltpu.VMEM((split, depth), BF16),
            pltpu.SemaphoreType.DMA((tokens // TILE,)),
            pltpu.SemaphoreType.DMA((split // TILE,)),
        ],
        2 * tokens * depth * split,
        2 * depth * (tokens + split),
        "first_product",
    )(rows, weight)


def second_product(held, weight, down, done, pieces):
    tokens, depth = held.shape
    width, rank = down.shape
    split = done.shape[1]
    parts = (width - split) // TILE
    size = len(pieces)
    return call(
        functools.partial(second_kernel, size),
        jax.ShapeDtypeStruct((tokens, width), BF16),
        [VMEM, HBM, VMEM, VMEM] + [VMEM] * size,
        HBM,
        [
            pltpu.VMEM((tokens, width), BF16),
            pltpu.VMEM((size,) + pieces[0].shape, BF16),
            pltpu.VMEM((tokens, rank), BF16),
            pltpu.VMEM((width - split, depth), BF16),
            pltpu.SemaphoreType.DMA((parts,)),
            pltpu.SemaphoreType.DMA((parts + 1,)),
        ],
        2 * tokens * depth * (width - split),
        2 * depth * (tokens + width - split),
        "second_product",
    )(held, weight, down, done, *pieces)


def gather_rows(value, axis, dim):
    size = lax.axis_size(axis)
    if size != 2:
        return lax.all_gather(value, axis, axis=dim, tiled=True)
    other = shifted(value, axis, 1)
    low = lax.axis_index(axis) == 0
    return jnp.concatenate([jnp.where(low, value, other), jnp.where(low, other, value)], axis=dim)


def per_device(
    attention_output_rows,
    projection_result_gradient,
    adapter_down_weight,
    adapter_up_weight,
    output_projection_weight,
    adam_first_moments,
    adam_second_moments,
    rank_side_projection,
    width_side_projection,
    bounds,
    example_owner_slot,
):
    packs, blk, width_local = attention_output_rows.shape
    assert packs == 1
    width = projection_result_gradient.shape[2]
    size = lax.axis_size("tensor")
    rows_in = attention_output_rows.reshape(blk, width_local)
    rows_grad = projection_result_gradient.reshape(blk, width)

    partial_in, rows_in = rank_pieces(
        rows_in, adapter_down_weight, True, size, width_local, "pieces_in"
    )
    partial_grad, columns_grad = rank_pieces(
        rows_grad, adapter_up_weight, False, size, width_local, "pieces_grad"
    )
    stacked = jnp.stack([adam_first_moments, adam_second_moments]).astype(BF16)
    moments = gather_rows(stacked, "dp", 2)
    low = lax.axis_index("seq") * blk
    starts, ends = bounds[0, 0], bounds[0, 1]
    spans = jnp.any((starts < low) & (ends >= low + blk)).astype(F32)

    sent_in = scatter(partial_in)
    sent_grad = scatter(partial_grad)
    low_in = gather_pieces(total_of(sent_in))
    rows_here, low_in[0] = lax.optimization_barrier((rows_grad, low_in[0]))
    done, held = first_product(rows_here, output_projection_weight, width_local // 2)
    sent_grad, done = lax.optimization_barrier((sent_grad, done))
    low_grad = gather_pieces(total_of(sent_grad))

    low_in, low_grad, moments, spans = lax.optimization_barrier((low_in, low_grad, moments, spans))
    tails = tail_parts(bounds, rows_in, columns_grad, low_grad, low_in)
    shared = (rank_side_projection, width_side_projection)

    def hop(outgoing, k):
        return lax.ppermute(outgoing, "seq", [(k, k + 1)])

    def onward(arrived):
        return (tails.astype(F32) + spans * arrived.astype(F32)).astype(BF16)

    arrived = [hop(tails, 0)]
    filled_in, head_in = slot_features(
        1, bounds, example_owner_slot, columns_grad, moments, *shared, low_in, "slots_in"
    )
    arrived[0], head_in = lax.optimization_barrier((arrived[0], head_in))
    arrived.append(hop(onward(arrived[0]), 1))
    filled_grad, head_grad = slot_features(
        0, bounds, example_owner_slot, rows_in, moments, *shared, low_grad, "slots_grad"
    )
    arrived[1], head_grad = lax.optimization_barrier((arrived[1], head_grad))
    for k in range(2, lax.axis_size("seq") - 1):
        arrived.append(hop(onward(arrived[-1]), k))
    buffer = head_features(
        bounds,
        example_owner_slot,
        filled_grad,
        filled_in,
        head_grad,
        head_in,
        moments,
        *shared,
        arrived,
        blk,
    )
    arrived = lax.all_to_all(buffer, ("seq", "tensor"), split_axis=0, concat_axis=0, tiled=True)
    features = jnp.sum(arrived.astype(F32), axis=0).reshape(1, 1, -1)
    out = second_product(held, output_projection_weight, adapter_down_weight, done, low_grad)
    return (out.reshape(attention_output_rows.shape), features)


def solution(mesh):
    return jax.shard_map(
        per_device,
        mesh=mesh,
        in_specs=(
            P("dp", "seq", "tensor"),
            P("dp", "seq", None),
            P("tensor", None),
            P(None, "tensor"),
            P("tensor", None),
            P(None, "dp", "tensor"),
            P(None, "dp", "tensor"),
            P(),
            P(),
            P("dp", None, None),
            P("dp", None),
        ),
        out_specs=(P("dp", "seq", "tensor"), P("dp", ("seq", "tensor"), None)),
        check_vma=False,
    )
```

```python
import functools

import jax
import jax.numpy as jnp
from jax import lax
from jax.experimental import pallas as pl
from jax.experimental.pallas import tpu as pltpu
from jax.sharding import PartitionSpec as P

TOUCH = 8
ADAPTER_SCALE = 4.0
BETA_ONE = 0.9
BETA_TWO = 0.999
EPSILON = 1e-08
MIB = 2**20
BF16 = jnp.bfloat16
F32 = jnp.float32

HBM = pl.BlockSpec(memory_space=pltpu.HBM)
VMEM = pl.BlockSpec(memory_space=pltpu.VMEM)
SMEM = pl.BlockSpec(memory_space=pltpu.SMEM)


def dot_trailing(left, right):
    return lax.dot_general(left, right, (((1,), (1,)), ((), ())), preferred_element_type=F32)


def call(kernel, out_shape, in_specs, out_specs, scratch, flops, nbytes, name, vmem=32):
    return pl.pallas_call(
        kernel,
        out_shape=out_shape,
        in_specs=in_specs,
        out_specs=out_specs,
        scratch_shapes=scratch,
        compiler_params=pltpu.CompilerParams(vmem_limit_bytes=vmem * MIB),
        cost_estimate=pl.CostEstimate(flops=flops, bytes_accessed=nbytes, transcendentals=0),
        name=name,
    )


def pieces_kernel(source_in, source_grad, down, up, *rest):
    *outs, rows_in, rows_grad, down_buf, up_buf, sem, weight_sem = rest
    size = len(outs)
    place = lax.axis_index("tensor")
    rows, width = rows_in.shape[1:]
    rank = up_buf.shape[0]

    def copies(k):
        here = pl.ds(pl.multiple_of(lax.rem(place + k, size) * rows, rows), rows)
        there = pl.ds(pl.multiple_of(place * width, width), width)
        return (
            pltpu.make_async_copy(source_in.at[here], rows_in.at[k], sem.at[0, k]),
            pltpu.make_async_copy(source_grad.at[here, there], rows_grad.at[k], sem.at[1, k]),
        )

    weights = (
        pltpu.make_async_copy(down, down_buf, weight_sem.at[0]),
        pltpu.make_async_copy(up, up_buf, weight_sem.at[1]),
    )
    order = list(range(1, size)) + [0]
    for c in weights:
        c.start()
    for k in order:
        for c in copies(k):
            c.start()
    for c in weights:
        c.wait()
    for k in order:
        wait_in, wait_grad = copies(k)
        wait_in.wait()
        product = jnp.dot(rows_in[k], down_buf[...], preferred_element_type=F32)
        outs[k][:rank, :] = product.T.astype(BF16)
        wait_grad.wait()
        product = dot_trailing(rows_grad[k], up_buf[...])
        outs[k][rank:, :] = product.T.astype(BF16)


def rank_pieces(rows_in, rows_grad, down, up, size):
    tokens, width = rows_in.shape
    rank = up.shape[0]
    rows = tokens // size
    return call(
        pieces_kernel,
        [jax.ShapeDtypeStruct((2 * rank, rows), BF16)] * size,
        [HBM] * 4,
        [VMEM] * size,
        [
            pltpu.VMEM((size, rows, width), BF16),
            pltpu.VMEM((size, rows, width), BF16),
            pltpu.VMEM(down.shape, BF16),
            pltpu.VMEM(up.shape, BF16),
            pltpu.SemaphoreType.DMA((2, size)),
            pltpu.SemaphoreType.DMA((2,)),
        ],
        4 * tokens * width * rank,
        4 * tokens * width,
        "rank_pieces",
        62,
    )(rows_in, rows_grad, down, up)


def shifted(value, axis, shift):
    size = lax.axis_size(axis)
    return lax.ppermute(value, axis, [(i, (i + shift) % size) for i in range(size)])


def scatter(pieces):
    return [shifted(piece, "tensor", k) if k else piece for k, piece in enumerate(pieces)]


def total_of(terms):
    total = terms[0].astype(F32)
    for term in terms[1:]:
        total = total + term.astype(F32)
    return total.astype(BF16)


def gather_pieces(total):
    size = lax.axis_size("tensor")
    return [total] + [shifted(total, "tensor", k) for k in range(1, size)]


def example_scalars(bounds, block):
    low = lax.axis_index("seq") * block
    count = bounds.shape[2]
    first = jnp.int32(-1)
    last = jnp.int32(-1)
    for e in range(count):
        start = bounds[0, 0, e]
        first = first + (start <= low).astype(jnp.int32)
        last = last + (start <= low + block - 1).astype(jnp.int32)
    return low, first, last


def place_pieces(pieces, m, low_scratch):
    size = len(pieces)
    place = lax.axis_index("tensor")
    rank = low_scratch.shape[1]
    first = (1 - m) * rank
    for k, piece in enumerate(pieces):
        low_scratch[lax.rem(place + size - k, size)] = piece[first : first + rank, :]


def masked(low_piece, offset, start, end):
    tokens = offset + lax.broadcasted_iota(jnp.int32, low_piece.shape, 1)
    return jnp.where((tokens >= start) & (tokens < end), low_piece.astype(F32), 0.0).astype(BF16)


def tails_kernel(size, bounds, rows_in, rows_grad, *rest):
    pieces = rest[:size]
    out, low_scratch, acc = rest[size:]
    tokens, width = rows_in.shape
    rows = tokens // size
    low, _, last = example_scalars(bounds, tokens)
    start = bounds[0, 0, last]
    for m, source in enumerate((rows_in, rows_grad)):
        place_pieces(pieces, m, low_scratch)

        def chunk(c):
            left = masked(low_scratch[c], low + c * rows, start, low + tokens)
            return jnp.dot(left, source[c * rows : (c + 1) * rows, :], preferred_element_type=F32)

        acc[...] = chunk(size - 1)
        for c in range(size - 1):

            @pl.when(start < low + (c + 1) * rows)
            def _():
                acc[...] += chunk(c)

        out[m] = (ADAPTER_SCALE * acc[...]).astype(BF16)


def tail_parts(bounds, rows_in, rows_grad, low):
    size = len(low)
    rank, rows = low[0].shape[0] // 2, low[0].shape[1]
    tokens, width = rows_in.shape
    return call(
        functools.partial(tails_kernel, size),
        jax.ShapeDtypeStruct((2, rank, width), BF16),
        [SMEM] + [VMEM] * (2 + size),
        VMEM,
        [pltpu.VMEM((size, rank, rows), BF16), pltpu.VMEM((rank, width), F32)],
        4 * tokens * width * rank,
        4 * tokens * width,
        "tail_parts",
    )(bounds, rows_in, rows_grad, *low)


def normalize(grads, first_moment, second_moment):
    first = first_moment + (1.0 - BETA_ONE) * grads
    second = second_moment + ((1.0 - BETA_TWO) * grads) * grads
    guess = lax.rsqrt(second)
    below = second * guess + EPSILON
    return first * (guess * (2.0 - below * guess))


def split_two(value):
    high = value.astype(BF16)
    return high, (value - high.astype(F32)).astype(BF16)


def project_rank(rank_side, normed):
    both = jnp.dot(
        jnp.concatenate(split_two(rank_side[...]), axis=0), normed, preferred_element_type=F32
    )
    half = both.shape[0] // 2
    return both[:half] + both[half:]


def project_width(value, right):
    high, low = split_two(value)
    return jnp.dot(high, right, preferred_element_type=F32) + jnp.dot(
        low, right, preferred_element_type=F32
    )


def right_rows_copy(width_side, right, sem):
    rows = right.shape[0]
    first = pl.multiple_of(lax.axis_index("tensor") * rows, rows)
    return pltpu.make_async_copy(width_side.at[pl.ds(first, rows)], right, sem)


def slots_kernel(m, size, bounds, owner, source, moments, rank_side, width_side, *rest):
    pieces = rest[:size]
    out, head, low_scratch, acc, normed, ranked, wide, right, sem = rest[size:]
    right_copy = right_rows_copy(width_side, right, sem)
    right_copy.start()
    tokens, width = source.shape
    rank = head.shape[0]
    rows = tokens // size
    low, first, last = example_scalars(bounds, tokens)
    count = bounds.shape[2]
    place_pieces(pieces, m, low_scratch)
    step = 16

    def slot(j):
        return jnp.minimum(first + j, count - 1)

    def ends_here(j):
        return (first + j <= last) & (bounds[0, 1, slot(j)] <= low + tokens)

    @pl.loop(0, TOUCH)
    def _(j):
        start, end = bounds[0, 0, slot(j)], bounds[0, 1, slot(j)]

        @pl.when(ends_here(j) | (j == 0))
        def _():
            for c in range(size):
                begin = low + c * rows

                @pl.when((start < begin + rows) & (end > begin))
                def _():
                    left = masked(low_scratch[c], begin, start, end)
                    term = jnp.dot(
                        left, source[c * rows : (c + 1) * rows, :], preferred_element_type=F32
                    )
                    fresh = (start >= begin) | (c == 0)
                    acc[...] = jnp.where(fresh, 0.0, acc[...]) + term

            @pl.when(j == 0)
            def _():
                head[...] = (ADAPTER_SCALE * acc[...]).astype(BF16)

            @pl.when(j > 0)
            def _():
                for r in range(0, rank, step):
                    normed[r : r + step, :] = normalize(
                        ADAPTER_SCALE * acc[r : r + step, :],
                        moments[0, m, r : r + step, :],
                        moments[1, m, r : r + step, :],
                    ).astype(BF16)
                ranked[j] = project_rank(rank_side, normed[...])

    right_copy.wait()
    wide[...] = project_width(ranked[...].reshape(-1, width), right[...]).reshape(wide.shape)
    out[...] = jnp.zeros_like(out)
    for j in range(1, TOUCH):

        @pl.when(ends_here(j))
        def _():
            out[owner[0, slot(j)]] = wide[j].astype(BF16)


def slot_features(
    m, bounds, owner, source, moments, rank_side, width_side, pieces, name
):
    size = len(pieces)
    rank, rows = pieces[0].shape[0] // 2, pieces[0].shape[1]
    tokens, width = source.shape
    lines = rank_side.shape[0]
    columns = width_side.shape[1]
    return call(
        functools.partial(slots_kernel, m, size),
        [
            jax.ShapeDtypeStruct((owner.shape[1], lines, columns), BF16),
            jax.ShapeDtypeStruct((rank, width), BF16),
        ],
        [SMEM, SMEM, VMEM, VMEM, VMEM, HBM] + [VMEM] * size,
        [VMEM, VMEM],
        [
            pltpu.VMEM((size, rank, rows), BF16),
            pltpu.VMEM((rank, width), F32),
            pltpu.VMEM((rank, width), BF16),
            pltpu.VMEM((TOUCH, lines, width), F32),
            pltpu.VMEM((TOUCH, lines, columns), F32),
            pltpu.VMEM((width, columns), BF16),
            pltpu.SemaphoreType.DMA,
        ],
        2 * tokens * width * rank * TOUCH,
        4 * tokens * width,
        name,
    )(bounds, owner, source, moments, rank_side, width_side, *pieces)


def head_kernel(
    hops, block, bounds, owner, filled_grad, filled_in, head_grad, head_in, moments, rank_side, width_side, *rest
):
    arrived = rest[:hops]
    out, normed, ranked, right, sem = rest[hops:]
    right_copy = right_rows_copy(width_side, right, sem)
    right_copy.start()
    low, first, last = example_scalars(bounds, block)
    rank = head_in.shape[0]
    lines = rank_side.shape[0]
    continued = (bounds[0, 0, first] < low).astype(F32)
    step = 16
    out[:, :lines] = filled_grad[...]
    out[:, lines:] = filled_in[...]
    ends = bounds[0, 1, first] <= low + block

    @pl.when(ends)
    def _():
        for m, head in enumerate((head_grad, head_in)):
            for r in range(0, rank, step):
                here = slice(r, r + step)
                incoming = arrived[0][m, here, :].astype(F32)
                for k in range(1, hops):
                    incoming = incoming + arrived[k][m, here, :].astype(F32)
                normed[here, :] = normalize(
                    head[here, :].astype(F32) + continued * incoming,
                    moments[0, m, here, :],
                    moments[1, m, here, :],
                ).astype(BF16)
            ranked[m * lines : (m + 1) * lines, :] = project_rank(rank_side, normed[...])

    right_copy.wait()

    @pl.when(ends)
    def _():
        out[owner[0, first]] = project_width(ranked[...], right[...]).astype(BF16)


def head_features(
    bounds, owner, filled_grad, filled_in, head_grad, head_in, moments, rank_side, width_side, arrived, block
):
    hops = len(arrived)
    rank, width = head_in.shape
    slots, lines, columns = filled_in.shape
    return call(
        functools.partial(head_kernel, hops, block),
        jax.ShapeDtypeStruct((slots, 2 * lines, columns), BF16),
        [SMEM, SMEM] + [VMEM] * 6 + [HBM] + [VMEM] * hops,
        VMEM,
        [
            pltpu.VMEM((rank, width), BF16),
            pltpu.VMEM((2 * lines, width), F32),
            pltpu.VMEM((width, columns), BF16),
            pltpu.SemaphoreType.DMA,
        ],
        2 * width * 2 * rank * 4 * lines,
        8 * rank * width,
        "head_features",
    )(
        bounds,
        owner,
        filled_grad,
        filled_in,
        head_grad,
        head_in,
        moments,
        rank_side,
        width_side,
        *arrived,
    )


def depth_chunks(depth):
    return [0, depth // 8, depth // 2, depth]


def operand_copies(source, weight, held, weight_buf, sem, column):
    edges = depth_chunks(held.shape[1])
    pairs = []
    for c, (begin, end) in enumerate(zip(edges, edges[1:])):
        depth = pl.ds(begin, end - begin)
        columns = pl.ds(column, weight_buf.shape[0])
        pair = (
            pltpu.make_async_copy(source.at[:, depth], held.at[:, depth], sem.at[0, c]),
            pltpu.make_async_copy(weight.at[columns, depth], weight_buf.at[:, depth], sem.at[1, c]),
        )
        for copy in pair:
            copy.start()
        pairs.append((slice(begin, end), pair))
    return pairs


def chunked_product(pairs, held, weight_buf, out):
    for c, (depth, pair) in enumerate(pairs):
        for copy in pair:
            copy.wait()
        term = dot_trailing(held[:, depth], weight_buf[:, depth])
        out[...] = term if c == 0 else out[...] + term


def first_kernel(source, weight, out, held, weight_buf, sem):
    chunked_product(
        operand_copies(source, weight, held, weight_buf, sem, 0), held, weight_buf, out
    )


def second_kernel(size, source, weight, down, done, *rest):
    pieces = rest[:size]
    out, result, acc, low_rows, held, weight_buf, sem, out_sem = rest[size:]
    tokens, width = result.shape
    split = done.shape[1]
    pairs = operand_copies(source, weight, held, weight_buf, sem, split)
    place = lax.axis_index("tensor")
    rows = tokens // size
    rank = low_rows.shape[1]
    for k, piece in enumerate(pieces):
        block = lax.rem(place + size - k, size)
        low_rows[pl.ds(pl.multiple_of(block * rows, rows), rows), :] = (
            piece[rank:, :].astype(F32).T.astype(BF16)
        )

    def out_copy(begin, end, k):
        here = pl.ds(begin, end - begin)
        return pltpu.make_async_copy(result.at[:, here], out.at[:, here], out_sem.at[k])

    def finish(base, begin, end, k):
        extra = dot_trailing(low_rows[...], down[begin:end, :])
        result[:, begin:end] = (base[...] + ADAPTER_SCALE * extra).astype(BF16)
        out_copy(begin, end, k).start()

    finish(done, 0, split, 0)
    chunked_product(pairs, held, weight_buf, acc)
    finish(acc, split, width, 1)
    out_copy(0, split, 0).wait()
    out_copy(split, width, 1).wait()


def first_product(source, weight, split):
    tokens, depth = source.shape
    return call(
        first_kernel,
        jax.ShapeDtypeStruct((tokens, split), F32),
        [HBM, HBM],
        VMEM,
        [
            pltpu.VMEM((tokens, depth), BF16),
            pltpu.VMEM((split, depth), BF16),
            pltpu.SemaphoreType.DMA((2, len(depth_chunks(depth)) - 1)),
        ],
        2 * tokens * depth * split,
        2 * depth * (tokens + split),
        "first_product",
        56,
    )(source, weight)


def second_product(source, weight, down, done, pieces):
    tokens, depth = source.shape
    width, rank = down.shape
    rest = width - done.shape[1]
    size = len(pieces)
    return call(
        functools.partial(second_kernel, size),
        jax.ShapeDtypeStruct((tokens, width), BF16),
        [HBM, HBM] + [VMEM] * (2 + size),
        HBM,
        [
            pltpu.VMEM((tokens, width), BF16),
            pltpu.VMEM((tokens, rest), F32),
            pltpu.VMEM((tokens, rank), BF16),
            pltpu.VMEM((tokens, depth), BF16),
            pltpu.VMEM((rest, depth), BF16),
            pltpu.SemaphoreType.DMA((2, len(depth_chunks(depth)) - 1)),
            pltpu.SemaphoreType.DMA((2,)),
        ],
        2 * tokens * depth * rest,
        2 * depth * (tokens + rest),
        "second_product",
        56,
    )(source, weight, down, done, *pieces)


def gather_rows(value, axis, dim):
    size = lax.axis_size(axis)
    if size != 2:
        return lax.all_gather(value, axis, axis=dim, tiled=True)
    other = shifted(value, axis, 1)
    low = lax.axis_index(axis) == 0
    return jnp.concatenate([jnp.where(low, value, other), jnp.where(low, other, value)], axis=dim)


def per_device(
    attention_output_rows,
    projection_result_gradient,
    adapter_down_weight,
    adapter_up_weight,
    output_projection_weight,
    adam_first_moments,
    adam_second_moments,
    rank_side_projection,
    width_side_projection,
    bounds,
    example_owner_slot,
):
    packs, blk, width_local = attention_output_rows.shape
    assert packs == 1
    width = projection_result_gradient.shape[2]
    size = lax.axis_size("tensor")
    rows_in = attention_output_rows.reshape(blk, width_local)
    rows_grad = projection_result_gradient.reshape(blk, width)

    pieces = rank_pieces(rows_in, rows_grad, adapter_down_weight, adapter_up_weight, size)
    stacked = jnp.stack([adam_first_moments, adam_second_moments]).astype(BF16)
    betas = jnp.array([BETA_ONE, BETA_TWO], F32).reshape(2, 1, 1, 1)
    moments = betas * gather_rows(stacked, "dp", 2).astype(F32)
    first_token = lax.axis_index("seq") * blk
    starts, ends = bounds[0, 0], bounds[0, 1]
    spans = jnp.any((starts < first_token) & (ends >= first_token + blk)).astype(F32)

    columns_grad = lax.dynamic_slice_in_dim(
        rows_grad, lax.axis_index("tensor") * width_local, width_local, 1
    )
    done = first_product(rows_grad, output_projection_weight, width_local // 2)
    sent, done = lax.optimization_barrier((scatter(pieces), done))
    low, moments, spans, columns_grad = lax.optimization_barrier(
        (gather_pieces(total_of(sent)), moments, spans, columns_grad)
    )
    tails = tail_parts(bounds, rows_in, columns_grad, low)
    shared = (rank_side_projection, width_side_projection)

    def hop(outgoing, k):
        return lax.ppermute(outgoing, "seq", [(k, k + 1)])

    def onward(arrived):
        return (tails.astype(F32) + spans * arrived.astype(F32)).astype(BF16)

    arrived = [hop(tails, 0)]
    outgoing, columns_grad = lax.optimization_barrier((onward(arrived[0]), columns_grad))
    arrived.append(hop(outgoing, 1))
    filled_in, head_in = slot_features(
        1, bounds, example_owner_slot, columns_grad, moments, *shared, low, "slots_in"
    )
    arrived[1], rows_in, head_in = lax.optimization_barrier((arrived[1], rows_in, head_in))
    for k in range(2, lax.axis_size("seq") - 1):
        arrived.append(hop(onward(arrived[-1]), k))
    filled_grad, head_grad = slot_features(
        0, bounds, example_owner_slot, rows_in, moments, *shared, low, "slots_grad"
    )
    arrived, head_grad = lax.optimization_barrier((arrived, head_grad))
    buffer = head_features(
        bounds,
        example_owner_slot,
        filled_grad,
        filled_in,
        head_grad,
        head_in,
        moments,
        *shared,
        arrived,
        blk,
    )
    arrived = lax.all_to_all(buffer, ("seq", "tensor"), split_axis=0, concat_axis=0, tiled=True)
    features = jnp.sum(arrived.astype(F32), axis=0).reshape(1, 1, -1)
    out = second_product(
        rows_grad,
        output_projection_weight,
        adapter_down_weight,
        done,
        low,
    )
    return (out.reshape(attention_output_rows.shape), features)


def solution(mesh):
    return jax.shard_map(
        per_device,
        mesh=mesh,
        in_specs=(
            P("dp", "seq", "tensor"),
            P("dp", "seq", None),
            P("tensor", None),
            P(None, "tensor"),
            P("tensor", None),
            P(None, "dp", "tensor"),
            P(None, "dp", "tensor"),
            P(),
            P(),
            P("dp", None, None),
            P("dp", None),
        ),
        out_specs=(P("dp", "seq", "tensor"), P("dp", ("seq", "tensor"), None)),
        check_vma=False,
    )
```

```python
import functools

import jax
import jax.numpy as jnp
from jax import lax
from jax.experimental import pallas as pl
from jax.experimental.pallas import tpu as pltpu
from jax.sharding import PartitionSpec as P

TOUCH = 8
ADAPTER_SCALE = 4.0
BETA_ONE = 0.9
BETA_TWO = 0.999
EPSILON = 1e-08
MIB = 2**20
PIECES_VMEM, FIRST_VMEM, PREPARE_VMEM, SECOND_VMEM = 53.4, 48, 45, 54
BF16 = jnp.bfloat16
F32 = jnp.float32

HBM = pl.BlockSpec(memory_space=pltpu.HBM)
VMEM = pl.BlockSpec(memory_space=pltpu.VMEM)
SMEM = pl.BlockSpec(memory_space=pltpu.SMEM)


def dot_trailing(left, right):
    return lax.dot_general(left, right, (((1,), (1,)), ((), ())), preferred_element_type=F32)


def call(kernel, out_shape, in_specs, out_specs, scratch, flops, nbytes, name, vmem=32):
    return pl.pallas_call(
        kernel,
        out_shape=out_shape,
        in_specs=in_specs,
        out_specs=out_specs,
        scratch_shapes=scratch,
        compiler_params=pltpu.CompilerParams(vmem_limit_bytes=int(vmem * MIB)),
        cost_estimate=pl.CostEstimate(flops=flops, bytes_accessed=nbytes, transcendentals=0),
        name=name,
    )


def pieces_kernel(source_in, source_grad, down, up, *rest):
    *outs, rows_in, rows_grad, down_buf, up_buf, sem = rest
    size = len(outs)
    place = lax.axis_index("tensor")
    tokens, width = rows_in.shape
    rows = tokens // size
    rank = up_buf.shape[0]
    there = pl.ds(pl.multiple_of(place * width, width), width)
    copies = []
    for i in range(size):
        here = pl.ds(i * rows, rows)
        copies.append(pltpu.make_async_copy(source_in.at[here], rows_in.at[here], sem.at[0, i]))
    for i in range(size):
        here = pl.ds(i * rows, rows)
        copies.append(
            pltpu.make_async_copy(source_grad.at[here, there], rows_grad.at[here], sem.at[1, i])
        )
    copies.insert(0, pltpu.make_async_copy(down, down_buf, sem.at[0, size]))
    copies.insert(size + 1, pltpu.make_async_copy(up, up_buf, sem.at[1, size]))
    for copy in copies:
        copy.start()

    def keep(product, first):
        for i in range(size):
            part = product[i * rows : (i + 1) * rows, :].astype(BF16)
            for k, out in enumerate(outs):

                @pl.when(lax.rem(place + k, size) == i)
                def _():
                    out[:, first : first + rank] = part

    for copy in copies[: size + 1]:
        copy.wait()
    keep(jnp.dot(rows_in[...], down_buf[...], preferred_element_type=F32), 0)
    for copy in copies[size + 1 :]:
        copy.wait()
    keep(dot_trailing(rows_grad[...], up_buf[...]), rank)


def rank_pieces(rows_in, rows_grad, down, up, size):
    tokens, width = rows_in.shape
    rank = up.shape[0]
    rows = tokens // size
    return call(
        pieces_kernel,
        [jax.ShapeDtypeStruct((rows, 2 * rank), BF16)] * size,
        [HBM] * 4,
        [VMEM] * size,
        [
            pltpu.VMEM((tokens, width), BF16),
            pltpu.VMEM((tokens, width), BF16),
            pltpu.VMEM(down.shape, BF16),
            pltpu.VMEM(up.shape, BF16),
            pltpu.SemaphoreType.DMA((2, size + 1)),
        ],
        4 * tokens * width * rank,
        4 * tokens * width,
        "rank_pieces",
        PIECES_VMEM,
    )(rows_in, rows_grad, down, up)


def shifted(value, axis, shift):
    size = lax.axis_size(axis)
    return lax.ppermute(value, axis, [(i, (i + shift) % size) for i in range(size)])


def scatter(pieces):
    return [shifted(piece, "tensor", k) if k else piece for k, piece in enumerate(pieces)]


def total_kernel(*refs):
    *terms, out = refs
    total = terms[0][...].astype(F32)
    for term in terms[1:]:
        total = total + term[...].astype(F32)
    out[...] = total.T.astype(BF16)


def total_of(terms):
    rows, ranks = terms[0].shape
    return call(
        total_kernel,
        jax.ShapeDtypeStruct((ranks, rows), BF16),
        [VMEM] * len(terms),
        VMEM,
        [],
        len(terms) * rows * ranks,
        2 * (len(terms) + 1) * rows * ranks,
        "total_low",
    )(*terms)


def gather_pieces(total):
    size = lax.axis_size("tensor")
    return [total] + [shifted(total, "tensor", k) for k in range(1, size)]


def example_scalars(bounds, block):
    low = lax.axis_index("seq") * block
    count = bounds.shape[2]
    first = jnp.int32(-1)
    last = jnp.int32(-1)
    for e in range(count):
        start = bounds[0, 0, e]
        first = first + (start <= low).astype(jnp.int32)
        last = last + (start <= low + block - 1).astype(jnp.int32)
    return low, first, last


def place_pieces(pieces, m, low_scratch):
    size = len(pieces)
    place = lax.axis_index("tensor")
    rank = low_scratch.shape[1]
    first = (1 - m) * rank
    for k, piece in enumerate(pieces):
        low_scratch[lax.rem(place + size - k, size)] = piece[first : first + rank, :]


def masked(low_piece, offset, start, end):
    tokens = offset + lax.broadcasted_iota(jnp.int32, low_piece.shape, 1)
    return jnp.where((tokens >= start) & (tokens < end), low_piece.astype(F32), 0.0).astype(BF16)


def left_side():
    return lax.axis_index("seq") < lax.axis_size("seq") // 2


def fits(bounds, example, low, tokens):
    return bounds[0, 0, example] >= low, bounds[0, 1, example] <= low + tokens


def edges(bounds, low, first, last, tokens):
    left = left_side()
    inner = jnp.where(left, last, first)
    outer = jnp.where(left, first, last)
    inner_starts, inner_ends = fits(bounds, inner, low, tokens)
    outer_starts, outer_ends = fits(bounds, outer, low, tokens)
    inner_on = (left & ~inner_ends) | (~left & ~inner_starts)
    outer_on = (left & ~outer_starts) | (~left & ~outer_ends)
    outer_inside = (left & outer_ends) | (~left & outer_starts)
    return inner, outer, inner_on, outer_on, outer_on & outer_inside


def sum_part(acc, source, low_scratch, low, start, end):
    size, _, rows = low_scratch.shape
    for c in range(size):
        begin = low + c * rows

        @pl.when((start < begin + rows) & (end > begin))
        def _():
            left = masked(low_scratch[c], begin, start, end)
            term = jnp.dot(
                left, source[c * rows : (c + 1) * rows, :], preferred_element_type=F32
            )
            fresh = (start >= begin) | (c == 0)
            acc[...] = jnp.where(fresh, 0.0, acc[...]) + term


def inner_kernel(size, bounds, rows_in, rows_grad, *rest):
    pieces = rest[:size]
    out, low_scratch, acc = rest[size:]
    tokens = rows_in.shape[0]
    low, first, last = example_scalars(bounds, tokens)
    inner = edges(bounds, low, first, last, tokens)[0]
    for m, source in enumerate((rows_in, rows_grad)):
        place_pieces(pieces, m, low_scratch)
        sum_part(acc, source, low_scratch, low, bounds[0, 0, inner], bounds[0, 1, inner])
        out[m] = (ADAPTER_SCALE * acc[...]).astype(BF16)


def inner_parts(bounds, rows_in, rows_grad, low):
    size = len(low)
    rank, rows = low[0].shape[0] // 2, low[0].shape[1]
    tokens, width = rows_in.shape
    return call(
        functools.partial(inner_kernel, size),
        jax.ShapeDtypeStruct((2, rank, width), BF16),
        [SMEM] + [VMEM] * (2 + size),
        VMEM,
        [pltpu.VMEM((size, rank, rows), BF16), pltpu.VMEM((rank, width), F32)],
        4 * tokens * width * rank,
        4 * tokens * width,
        "inner_parts",
    )(bounds, rows_in, rows_grad, *low)


def normalize(grads, first_moment, second_moment):
    first = first_moment + (1.0 - BETA_ONE) * grads
    second = second_moment + ((1.0 - BETA_TWO) * grads) * grads
    guess = lax.rsqrt(second)
    below = second * guess + EPSILON
    return first * (guess * (2.0 - below * guess))


def split_two(value):
    high = value.astype(BF16)
    return high, (value - high.astype(F32)).astype(BF16)


def rank_side_pair(rank_side, blocks):
    lines, rank = rank_side.shape
    blocks[...] = jnp.zeros_like(blocks)
    for i, term in enumerate(split_two(rank_side[...])):
        for j in range(2):
            at = (2 * i + j) * lines
            blocks[at : at + lines, j * rank : (j + 1) * rank] = term


def project_rank(blocks, normed):
    both = jnp.dot(blocks[...], normed, preferred_element_type=F32)
    half = both.shape[0] // 2
    return both[:half] + both[half:]


def project_width(value, right):
    high, low = split_two(value)
    return jnp.dot(high, right, preferred_element_type=F32) + jnp.dot(
        low, right, preferred_element_type=F32
    )


STEP = 16


def slots_kernel(m, size, bounds, owner, source, moments, rank_side, width_side, *rest):
    pieces = rest[:size]
    out, outer_part, low_scratch, acc, normed, blocks, ranked, wide = rest[size:]
    tokens = source.shape[0]
    rank, width = outer_part.shape
    lines = rank_side.shape[0]
    low, first, last = example_scalars(bounds, tokens)
    count = bounds.shape[2]
    _, outer, _, outer_on, _ = edges(bounds, low, first, last, tokens)
    place_pieces(pieces, m, low_scratch)
    rank_side_pair(rank_side, blocks)

    def slot(j):
        return jnp.minimum(first + j, count - 1)

    def inside(j):
        starts, ends = fits(bounds, slot(j), low, tokens)
        return (first + j <= last) & starts & ends

    @pl.loop(0, TOUCH)
    def _(j):
        here = inside(j)
        is_outer = (first + j == outer) & outer_on

        @pl.when(here | is_outer)
        def _():
            start, end = bounds[0, 0, slot(j)], bounds[0, 1, slot(j)]
            sum_part(acc, source, low_scratch, low, start, end)

        @pl.when(is_outer)
        def _():
            outer_part[...] = (ADAPTER_SCALE * acc[...]).astype(BF16)

        @pl.when(here)
        def _():
            for r in range(0, rank, STEP):
                normed[j, r : r + STEP, :] = normalize(
                    ADAPTER_SCALE * acc[r : r + STEP, :],
                    moments[0, m, r : r + STEP, :],
                    moments[1, m, r : r + STEP, :],
                ).astype(BF16)

        @pl.when(~here)
        def _():
            normed[j] = jnp.zeros((rank, width), BF16)

    for j in range(0, TOUCH, 2):
        ranked[j * lines : (j + 2) * lines, :] = project_rank(
            blocks, normed[j : j + 2].reshape(2 * rank, width)
        )
    wide[...] = project_width(ranked[...], width_side[...]).reshape(wide.shape)
    out[...] = jnp.zeros_like(out)
    for j in range(TOUCH):

        @pl.when(inside(j))
        def _():
            out[owner[0, slot(j)]] = wide[j].astype(BF16)


def slot_features(m, bounds, owner, source, moments, rank_side, width_side, pieces, name):
    size = len(pieces)
    rank, rows = pieces[0].shape[0] // 2, pieces[0].shape[1]
    tokens, width = source.shape
    lines = rank_side.shape[0]
    columns = width_side.shape[1]
    return call(
        functools.partial(slots_kernel, m, size),
        [
            jax.ShapeDtypeStruct((owner.shape[1], lines, columns), BF16),
            jax.ShapeDtypeStruct((rank, width), BF16),
        ],
        [SMEM, SMEM] + [VMEM] * (4 + size),
        [VMEM, VMEM],
        [
            pltpu.VMEM((size, rank, rows), BF16),
            pltpu.VMEM((rank, width), F32),
            pltpu.VMEM((TOUCH, rank, width), BF16),
            pltpu.VMEM((4 * lines, 2 * rank), BF16),
            pltpu.VMEM((TOUCH * lines, width), F32),
            pltpu.VMEM((TOUCH, lines, columns), F32),
        ],
        2 * tokens * width * rank * TOUCH,
        4 * tokens * width,
        name,
    )(bounds, owner, source, moments, rank_side, width_side, *pieces)


def crossing_kernel(
    tokens,
    hops,
    bounds,
    owner,
    filled_grad,
    filled_in,
    outer_grad,
    outer_in,
    kept,
    received,
    moments,
    rank_side,
    width_side,
    *rest
):
    arrived = rest[:hops]
    out, normed, blocks, ranked = rest[hops:]
    low, first, last = example_scalars(bounds, tokens)
    rank = outer_in.shape[0]
    lines = rank_side.shape[0]
    half = kept.shape[1]
    inner, outer, inner_on, _, outer_done = edges(bounds, low, first, last, tokens)
    place, middle = lax.axis_index("seq"), lax.axis_size("seq") // 2
    inner_done = inner_on & ((place == middle - 1) | (place == middle))
    out[:, :lines] = filled_grad[...]
    out[:, lines:] = filled_in[...]
    rank_side_pair(rank_side, blocks)

    @pl.when(outer_done)
    def _():
        for m, part in enumerate((outer_grad, outer_in)):
            for r in range(0, rank, STEP):
                here = slice(r, r + STEP)
                grads = part[here, :].astype(F32)
                for k in range(hops):
                    grads = grads + arrived[k][m, here, :].astype(F32)
                normed[m * rank + r : m * rank + r + STEP, :] = normalize(
                    grads, moments[0, m, here, :], moments[1, m, here, :]
                ).astype(BF16)
        ranked[: 2 * lines, :] = project_rank(blocks, normed[...])

    @pl.when(inner_done)
    def _():
        offset = jnp.where(left_side(), 0, half)
        normed[...] = jnp.zeros_like(normed)
        for m in range(2):
            for r in range(0, half, STEP):
                here = pl.ds(pl.multiple_of(offset + r, STEP), STEP)
                there = pl.ds(pl.multiple_of(m * rank + offset + r, STEP), STEP)
                grads = kept[m, r : r + STEP, :].astype(F32)
                grads = grads + received[m, r : r + STEP, :].astype(F32)
                normed[there, :] = normalize(
                    grads, moments[0, m, here, :], moments[1, m, here, :]
                ).astype(BF16)
        ranked[2 * lines :, :] = project_rank(blocks, normed[...])

    @pl.when(outer_done | inner_done)
    def _():
        wide = project_width(ranked[...], width_side[...]).astype(BF16)

        @pl.when(outer_done)
        def _():
            out[owner[0, outer]] = wide[: 2 * lines]

        @pl.when(inner_done)
        def _():
            out[owner[0, inner]] = wide[2 * lines :]


def crossing_features(
    tokens, bounds, owner, filled, outer, kept, received, moments, rank_side, width_side, arrived
):
    hops = len(arrived)
    rank, width = outer[0].shape
    slots, lines, columns = filled[0].shape
    return call(
        functools.partial(crossing_kernel, tokens, hops),
        jax.ShapeDtypeStruct((slots, 2 * lines, columns), BF16),
        [SMEM, SMEM] + [VMEM] * (9 + hops),
        VMEM,
        [
            pltpu.VMEM((2 * rank, width), BF16),
            pltpu.VMEM((4 * lines, 2 * rank), BF16),
            pltpu.VMEM((4 * lines, width), F32),
        ],
        8 * width * 2 * rank * 4 * lines,
        12 * rank * width,
        "crossing_features",
    )(
        bounds,
        owner,
        *filled,
        *outer,
        kept,
        received,
        moments,
        rank_side,
        width_side,
        *arrived,
    )


def owned_kernel(arrived, out):
    total = arrived[0].astype(F32)
    for k in range(1, arrived.shape[0]):
        total = total + arrived[k].astype(F32)
    columns = total.shape[1]
    for line in range(total.shape[0]):
        out[:, line * columns : (line + 1) * columns] = total[line : line + 1, :]


def owned_features(arrived):
    _, lines, columns = arrived.shape
    return call(
        owned_kernel,
        jax.ShapeDtypeStruct((1, lines * columns), F32),
        [VMEM],
        VMEM,
        [],
        arrived.size,
        2 * arrived.size,
        "owned_features",
    )(arrived)


TILE = 256


def depth_chunks(depth):
    return [0, depth // 8, 3 * depth // 8, 5 * depth // 8, 7 * depth // 8, depth]


def operand_copies(source, weight, held, weight_buf, sem, column):
    edges = depth_chunks(held.shape[1])
    pairs = []
    for c, (begin, end) in enumerate(zip(edges, edges[1:])):
        depth = pl.ds(begin, end - begin)
        columns = pl.ds(column, weight_buf.shape[0])
        pair = (
            pltpu.make_async_copy(source.at[:, depth], held.at[:, depth], sem.at[0, c]),
            pltpu.make_async_copy(weight.at[columns, depth], weight_buf.at[:, depth], sem.at[1, c]),
        )
        pairs.append((slice(begin, end), pair))
    return pairs


def start_all(pairs):
    for _, pair in pairs:
        for copy in pair:
            copy.start()


def add_chunk(pairs, c, held, weight_buf, out):
    depth, pair = pairs[c]
    for copy in pair:
        copy.wait()
    for n in range(0, weight_buf.shape[0], TILE):
        there = slice(n, n + TILE)
        term = dot_trailing(held[:, depth], weight_buf[there, depth])
        out[:, there] = term if c == 0 else out[:, there] + term


def first_kernel(column, source, weight, out, acc, held, weight_buf, sem):
    pairs = operand_copies(source, weight, held, weight_buf, sem, column)
    start_all(pairs)
    for c in range(len(pairs)):
        add_chunk(pairs, c, held, weight_buf, acc)
    out[...] = acc[...].astype(BF16)


def second_kernel(size, count, source, weight, down, *rest):
    done, pieces = rest[:count], rest[count : count + size]
    out, result, acc, low_rows, held, weight_buf, *bufs = rest[count + size :]
    down_buf, *bufs = bufs
    done_bufs, (pieces_buf, sem, extra_sem, out_sem) = bufs[:count], bufs[count:]
    tokens, width = result.shape
    split = sum(part.shape[1] for part in done)
    place = lax.axis_index("tensor")
    rows = tokens // size
    rank = low_rows.shape[1]
    extras = [pltpu.make_async_copy(down, down_buf, extra_sem.at[0])]
    for k, piece in enumerate(pieces):
        extras.append(pltpu.make_async_copy(piece, pieces_buf.at[k], extra_sem.at[1 + k]))
    for k, part in enumerate(done):
        extras.append(pltpu.make_async_copy(part, done_bufs[k], extra_sem.at[1 + size + k]))
    pairs = operand_copies(source, weight, held, weight_buf, sem, split)
    early = 2
    start_all(pairs[:early])
    for copy in extras:
        copy.start()
    start_all(pairs[early:])
    for c in range(early):
        add_chunk(pairs, c, held, weight_buf, acc)
    for copy in extras:
        copy.wait()
    for k in range(size):
        block = lax.rem(place + size - k, size)
        low_rows[pl.ds(pl.multiple_of(block * rows, rows), rows), :] = (
            pieces_buf[k, rank:, :].astype(F32).T.astype(BF16)
        )

    def out_copy(begin, end, k):
        here = pl.ds(begin, end - begin)
        return pltpu.make_async_copy(result.at[:, here], out.at[:, here], out_sem.at[k])

    def finish(base, begin, end, k):
        extra = dot_trailing(low_rows[...], down_buf[begin:end, :])
        result[:, begin:end] = (base[...].astype(F32) + ADAPTER_SCALE * extra).astype(BF16)
        out_copy(begin, end, k).start()

    cuts = [0]
    for k, part in enumerate(done_bufs):
        cuts.append(cuts[-1] + part.shape[1])
        finish(part, cuts[-2], cuts[-1], k)
    cuts.append(width)
    for c in range(early, len(pairs)):
        add_chunk(pairs, c, held, weight_buf, acc)
    finish(acc, split, width, count)
    for k in range(count + 1):
        out_copy(cuts[k], cuts[k + 1], k).wait()


def first_product(source, weight, column, split):
    tokens, depth = source.shape
    return call(
        functools.partial(first_kernel, column),
        jax.ShapeDtypeStruct((tokens, split), BF16),
        [HBM, HBM],
        VMEM,
        [
            pltpu.VMEM((tokens, split), F32),
            pltpu.VMEM((tokens, depth), BF16),
            pltpu.VMEM((split, depth), BF16),
            pltpu.SemaphoreType.DMA((2, len(depth_chunks(depth)) - 1)),
        ],
        2 * tokens * depth * split,
        2 * depth * (tokens + split),
        "first_product",
        FIRST_VMEM,
    )(source, weight)


def second_product(source, weight, down, done, pieces):
    tokens, depth = source.shape
    width, rank = down.shape
    rest = width - sum(part.shape[1] for part in done)
    size, count = len(pieces), len(done)
    return call(
        functools.partial(second_kernel, size, count),
        jax.ShapeDtypeStruct((tokens, width), BF16),
        [HBM] * (3 + count + size),
        HBM,
        [
            pltpu.VMEM((tokens, width), BF16),
            pltpu.VMEM((tokens, rest), F32),
            pltpu.VMEM((tokens, rank), BF16),
            pltpu.VMEM((tokens, depth), BF16),
            pltpu.VMEM((rest, depth), BF16),
            pltpu.VMEM(down.shape, BF16),
        ]
        + [pltpu.VMEM(part.shape, BF16) for part in done]
        + [
            pltpu.VMEM((size,) + pieces[0].shape, BF16),
            pltpu.SemaphoreType.DMA((2, len(depth_chunks(depth)) - 1)),
            pltpu.SemaphoreType.DMA((1 + size + count,)),
            pltpu.SemaphoreType.DMA((count + 1,)),
        ],
        2 * tokens * depth * rest,
        2 * depth * (tokens + rest),
        "second_product",
        SECOND_VMEM,
    )(source, weight, down, *done, *pieces)


def prepare_kernel(source_in, source_grad, width_side, first, second, other, *rest):
    rows_in, columns_grad, right, moments, own, arrived, sem = rest
    place = lax.axis_index("tensor")
    width, rows = right.shape[0], own.shape[2]
    here = pl.ds(pl.multiple_of(place * width, width), width)
    copies = [
        pltpu.make_async_copy(first, own.at[0], sem.at[0]),
        pltpu.make_async_copy(second, own.at[1], sem.at[1]),
        pltpu.make_async_copy(other, arrived, sem.at[2]),
        pltpu.make_async_copy(source_grad.at[:, here], columns_grad, sem.at[3]),
        pltpu.make_async_copy(source_in, rows_in, sem.at[4]),
        pltpu.make_async_copy(width_side.at[here], right, sem.at[5]),
    ]
    for copy in copies:
        copy.start()
    for copy in copies[:3]:
        copy.wait()
    mine = lax.axis_index("dp")
    for i, beta in enumerate((BETA_ONE, BETA_TWO)):
        for m in range(2):
            if arrived.shape[2] == rows:
                at = pl.ds(pl.multiple_of(mine * rows, rows), rows)
                moments[i, m, at, :] = beta * own[i, m]
                at = pl.ds(pl.multiple_of((1 - mine) * rows, rows), rows)
                moments[i, m, at, :] = beta * arrived[i, m].astype(F32)
            else:
                moments[i, m] = beta * arrived[i, m].astype(F32)
    for copy in copies[3:]:
        copy.wait()


def other_moments(first, second):
    sent = jnp.stack([first, second]).astype(BF16)
    if lax.axis_size("dp") != 2:
        return lax.all_gather(sent, "dp", axis=2, tiled=True)
    return shifted(sent, "dp", 1)


def prepare(rows_in, rows_grad, width_side, first, second, other):
    tokens, width = rows_in.shape
    columns = width_side.shape[1]
    rank = first.shape[1] * lax.axis_size("dp")
    return call(
        prepare_kernel,
        [
            jax.ShapeDtypeStruct((tokens, width), BF16),
            jax.ShapeDtypeStruct((tokens, width), BF16),
            jax.ShapeDtypeStruct((width, columns), BF16),
            jax.ShapeDtypeStruct((2, 2, rank, width), F32),
        ],
        [HBM] * 6,
        [VMEM] * 4,
        [
            pltpu.VMEM((2,) + first.shape, F32),
            pltpu.VMEM(other.shape, BF16),
            pltpu.SemaphoreType.DMA((6,)),
        ],
        8 * rank * width,
        4 * tokens * width + 8 * rank * width,
        "prepare",
        PREPARE_VMEM,
    )(rows_in, rows_grad, width_side, first, second, other)


def per_device(
    attention_output_rows,
    projection_result_gradient,
    adapter_down_weight,
    adapter_up_weight,
    output_projection_weight,
    adam_first_moments,
    adam_second_moments,
    rank_side_projection,
    width_side_projection,
    bounds,
    example_owner_slot,
):
    packs, blk, width_local = attention_output_rows.shape
    assert packs == 1
    width = projection_result_gradient.shape[2]
    size = lax.axis_size("tensor")
    rows_in = attention_output_rows.reshape(blk, width_local)
    rows_grad = projection_result_gradient.reshape(blk, width)

    pieces = rank_pieces(rows_in, rows_grad, adapter_down_weight, adapter_up_weight, size)
    pieces, own_moments = lax.optimization_barrier(
        (pieces, (adam_first_moments, adam_second_moments))
    )
    other = other_moments(*own_moments)

    cuts = [0, width_local // 4, 3 * width_local // 4]

    def product(rows, k):
        return first_product(rows, output_projection_weight, cuts[k], cuts[k + 1] - cuts[k])

    done = [product(rows_grad, 0)]
    sent, done = lax.optimization_barrier((scatter(pieces), done))
    total, rows_late, bounds_late = lax.optimization_barrier((total_of(sent), rows_grad, bounds))
    done.append(product(rows_late, 1))
    done, rows_late, other = lax.optimization_barrier((done, rows_late, other))
    prepared = prepare(rows_in, rows_late, width_side_projection, *own_moments, other)
    first_token = lax.axis_index("seq") * blk
    end_token = first_token + blk
    starts, ends = bounds_late[0, 0], bounds_late[0, 1]
    left = left_side()
    spans = jnp.any(
        jnp.where(
            left,
            (starts < first_token) & (ends >= end_token),
            (starts <= first_token) & (ends > end_token),
        )
    ).astype(F32)
    low, prepared, done, spans = lax.optimization_barrier(
        (gather_pieces(total), prepared, done, spans)
    )
    rows_in, columns_grad, right, moments = prepared
    inner = inner_parts(bounds, rows_in, columns_grad, low)
    shared = (rank_side_projection, right)
    seq = lax.axis_size("seq")
    middle = seq // 2

    def onward(arrived):
        return inner.astype(F32) + spans * arrived.astype(F32)

    arrived = []
    outgoing = inner
    for k in range(middle - 1):
        pairs = [(k, k + 1), (k + 1, k), (seq - 1 - k, seq - 2 - k), (seq - 2 - k, seq - 1 - k)]
        moved = lax.ppermute(outgoing, "seq", pairs)
        if middle > 2:
            place = lax.axis_index("seq")
            moved = jnp.where((place == k + 1) | (place == seq - 2 - k), moved, 0)
        arrived.append(moved)
        outgoing = onward(arrived[-1]).astype(BF16)
    filled_in, outer_in = slot_features(
        1, bounds, example_owner_slot, columns_grad, moments, *shared, low, "slots_in"
    )
    arrived, rows_in, outer_in = lax.optimization_barrier((arrived, rows_in, outer_in))
    summed = onward(arrived[-1]).astype(BF16)
    half = summed.shape[1] // 2
    kept = jnp.where(left, summed[:, :half], summed[:, half:])
    sent = jnp.where(left, summed[:, half:], summed[:, :half])
    received = lax.ppermute(sent, "seq", [(middle - 1, middle), (middle, middle - 1)])
    filled_grad, outer_grad = slot_features(
        0, bounds, example_owner_slot, rows_in, moments, *shared, low, "slots_grad"
    )
    received, outer_grad = lax.optimization_barrier((received, outer_grad))
    buffer = crossing_features(
        blk,
        bounds,
        example_owner_slot,
        (filled_grad, filled_in),
        (outer_grad, outer_in),
        kept,
        received,
        moments,
        *shared,
        arrived,
    )
    arrived = lax.all_to_all(buffer, ("seq", "tensor"), split_axis=0, concat_axis=0, tiled=True)
    features = owned_features(arrived)[None]
    out = second_product(
        rows_grad,
        output_projection_weight,
        adapter_down_weight,
        done,
        low,
    )
    return (out.reshape(attention_output_rows.shape), features)


def solution(mesh):
    return jax.shard_map(
        per_device,
        mesh=mesh,
        in_specs=(
            P("dp", "seq", "tensor"),
            P("dp", "seq", None),
            P("tensor", None),
            P(None, "tensor"),
            P("tensor", None),
            P(None, "dp", "tensor"),
            P(None, "dp", "tensor"),
            P(),
            P(),
            P("dp", None, None),
            P("dp", None),
        ),
        out_specs=(P("dp", "seq", "tensor"), P("dp", ("seq", "tensor"), None)),
        check_vma=False,
    )
```

```python
import functools

import jax
import jax.numpy as jnp
from jax import lax
from jax.experimental import pallas as pl
from jax.experimental.pallas import tpu as pltpu
from jax.sharding import PartitionSpec as P

TOUCH = 8
ADAPTER_SCALE = 4.0
BETA_ONE = 0.9
BETA_TWO = 0.999
EPSILON = 1e-08
MIB = 2**20
PIECES_VMEM, FIRST_VMEM, PREPARE_VMEM, SECOND_VMEM = 53.4, 48, 45, 46
BF16 = jnp.bfloat16
F32 = jnp.float32

HBM = pl.BlockSpec(memory_space=pltpu.HBM)
VMEM = pl.BlockSpec(memory_space=pltpu.VMEM)
SMEM = pl.BlockSpec(memory_space=pltpu.SMEM)


def dot_trailing(left, right):
    return lax.dot_general(left, right, (((1,), (1,)), ((), ())), preferred_element_type=F32)


def call(kernel, out_shape, in_specs, out_specs, scratch, flops, nbytes, name, vmem=32):
    return pl.pallas_call(
        kernel,
        out_shape=out_shape,
        in_specs=in_specs,
        out_specs=out_specs,
        scratch_shapes=scratch,
        compiler_params=pltpu.CompilerParams(vmem_limit_bytes=int(vmem * MIB)),
        cost_estimate=pl.CostEstimate(flops=flops, bytes_accessed=nbytes, transcendentals=0),
        name=name,
    )


def pieces_kernel(source_in, source_grad, down, up, first, second, *rest):
    *outs, moments, rows_in, rows_grad, partial, own, cast, down_buf, up_buf, sem, own_sem = rest
    size = len(outs)
    own_copies = [
        pltpu.make_async_copy(moment, own.at[i], own_sem.at[i])
        for i, moment in enumerate((first, second))
    ]
    place = lax.axis_index("tensor")
    tokens, width = rows_in.shape
    rows = tokens // size
    rank = up_buf.shape[0]
    there = pl.ds(pl.multiple_of(place * width, width), width)
    copies = []
    for i in range(size):
        here = pl.ds(i * rows, rows)
        copies.append(pltpu.make_async_copy(source_in.at[here], rows_in.at[here], sem.at[0, i]))
    for i in range(size):
        here = pl.ds(i * rows, rows)
        copies.append(
            pltpu.make_async_copy(source_grad.at[here, there], rows_grad.at[here], sem.at[1, i])
        )
    copies.insert(0, pltpu.make_async_copy(down, down_buf, sem.at[0, size]))
    copies.insert(size + 1, pltpu.make_async_copy(up, up_buf, sem.at[1, size]))
    for copy in copies[: size + 1] + own_copies + copies[size + 1 :]:
        copy.start()
    for copy in copies[: size + 1]:
        copy.wait()
    product = jnp.dot(rows_in[...], down_buf[...], preferred_element_type=F32)
    partial[:, :rank] = product.astype(BF16)
    for i, copy in enumerate(own_copies):
        copy.wait()
        cast[i] = own[i].astype(BF16)
    cast_copy = pltpu.make_async_copy(cast, moments, own_sem.at[2])
    cast_copy.start()
    for copy in copies[size + 1 :]:
        copy.wait()
    partial[:, rank:] = dot_trailing(rows_grad[...], up_buf[...]).astype(BF16)
    for k, out in enumerate(outs):
        block = pl.multiple_of(lax.rem(place + k, size) * rows, rows)
        out[...] = partial[pl.ds(block, rows), :]
    cast_copy.wait()


def rank_pieces(rows_in, rows_grad, down, up, first, second, size):
    tokens, width = rows_in.shape
    rank = up.shape[0]
    rows = tokens // size
    return call(
        pieces_kernel,
        [jax.ShapeDtypeStruct((rows, 2 * rank), BF16)] * size
        + [jax.ShapeDtypeStruct((2,) + first.shape, BF16)],
        [HBM] * 6,
        [VMEM] * size + [HBM],
        [
            pltpu.VMEM((tokens, width), BF16),
            pltpu.VMEM((tokens, width), BF16),
            pltpu.VMEM((tokens, 2 * rank), BF16),
            pltpu.VMEM((2,) + first.shape, F32),
            pltpu.VMEM((2,) + first.shape, BF16),
            pltpu.VMEM(down.shape, BF16),
            pltpu.VMEM(up.shape, BF16),
            pltpu.SemaphoreType.DMA((2, size + 1)),
            pltpu.SemaphoreType.DMA((3,)),
        ],
        4 * tokens * width * rank,
        4 * tokens * width,
        "rank_pieces",
        PIECES_VMEM,
    )(rows_in, rows_grad, down, up, first, second)


def shifted(value, axis, shift):
    size = lax.axis_size(axis)
    return lax.ppermute(value, axis, [(i, (i + shift) % size) for i in range(size)])


def scatter(pieces):
    return [shifted(piece, "tensor", k) if k else piece for k, piece in enumerate(pieces)]


def total_kernel(*refs):
    *terms, out = refs
    total = terms[0][...].astype(F32)
    for term in terms[1:]:
        total = total + term[...].astype(F32)
    out[...] = total.T.astype(BF16)


def total_of(terms):
    rows, ranks = terms[0].shape
    return call(
        total_kernel,
        jax.ShapeDtypeStruct((ranks, rows), BF16),
        [VMEM] * len(terms),
        VMEM,
        [],
        len(terms) * rows * ranks,
        2 * (len(terms) + 1) * rows * ranks,
        "total_low",
    )(*terms)


def gather_pieces(total):
    size = lax.axis_size("tensor")
    return [total] + [shifted(total, "tensor", k) for k in range(1, size)]


def example_scalars(bounds, block):
    low = lax.axis_index("seq") * block
    count = bounds.shape[2]
    first = jnp.int32(-1)
    last = jnp.int32(-1)
    for e in range(count):
        start = bounds[0, 0, e]
        first = first + (start <= low).astype(jnp.int32)
        last = last + (start <= low + block - 1).astype(jnp.int32)
    return low, first, last


def place_pieces(pieces, m, low_scratch):
    size = len(pieces)
    place = lax.axis_index("tensor")
    rank = low_scratch.shape[1]
    first = (1 - m) * rank
    for k, piece in enumerate(pieces):
        low_scratch[lax.rem(place + size - k, size)] = piece[first : first + rank, :]


def masked(low_piece, offset, start, end):
    tokens = offset + lax.broadcasted_iota(jnp.int32, low_piece.shape, 1)
    return jnp.where((tokens >= start) & (tokens < end), low_piece.astype(F32), 0.0).astype(BF16)


def left_side():
    return lax.axis_index("seq") < lax.axis_size("seq") // 2


def fits(bounds, example, low, tokens):
    return bounds[0, 0, example] >= low, bounds[0, 1, example] <= low + tokens


def edges(bounds, low, first, last, tokens):
    left = left_side()
    inner = jnp.where(left, last, first)
    outer = jnp.where(left, first, last)
    inner_starts, inner_ends = fits(bounds, inner, low, tokens)
    outer_starts, outer_ends = fits(bounds, outer, low, tokens)
    inner_on = (left & ~inner_ends) | (~left & ~inner_starts)
    outer_on = (left & ~outer_starts) | (~left & ~outer_ends)
    outer_inside = (left & outer_ends) | (~left & outer_starts)
    return inner, outer, inner_on, outer_on, outer_on & outer_inside


def sum_part(acc, source, low_scratch, low, start, end):
    size, _, rows = low_scratch.shape
    for c in range(size):
        begin = low + c * rows

        @pl.when((start < begin + rows) & (end > begin))
        def _():
            left = masked(low_scratch[c], begin, start, end)
            term = jnp.dot(
                left, source[c * rows : (c + 1) * rows, :], preferred_element_type=F32
            )
            fresh = (start >= begin) | (c == 0)
            acc[...] = jnp.where(fresh, 0.0, acc[...]) + term


def inner_kernel(size, bounds, rows_in, rows_grad, *rest):
    pieces = rest[:size]
    out, ordered, acc = rest[size:]
    tokens = rows_in.shape[0]
    low, first, last = example_scalars(bounds, tokens)
    inner = edges(bounds, low, first, last, tokens)[0]
    for m, source in enumerate((rows_in, rows_grad)):
        place_pieces(pieces, m, ordered.at[m])
        sum_part(acc, source, ordered.at[m], low, bounds[0, 0, inner], bounds[0, 1, inner])
        out[m] = (ADAPTER_SCALE * acc[...]).astype(BF16)


def inner_parts(bounds, rows_in, rows_grad, low):
    size = len(low)
    rank, rows = low[0].shape[0] // 2, low[0].shape[1]
    tokens, width = rows_in.shape
    return call(
        functools.partial(inner_kernel, size),
        [
            jax.ShapeDtypeStruct((2, rank, width), BF16),
            jax.ShapeDtypeStruct((2, size, rank, rows), BF16),
        ],
        [SMEM] + [VMEM] * (2 + size),
        [VMEM, VMEM],
        [pltpu.VMEM((rank, width), F32)],
        4 * tokens * width * rank,
        4 * tokens * width,
        "inner_parts",
    )(bounds, rows_in, rows_grad, *low)


def normalize(grads, first_moment, second_moment):
    first = first_moment + (1.0 - BETA_ONE) * grads
    second = second_moment + ((1.0 - BETA_TWO) * grads) * grads
    guess = lax.rsqrt(second)
    below = second * guess + EPSILON
    return first * (guess * (2.0 - below * guess))


def split_two(value):
    high = value.astype(BF16)
    return high, (value - high.astype(F32)).astype(BF16)


def rank_side_pair(rank_side, blocks):
    lines, rank = rank_side.shape
    blocks[...] = jnp.zeros_like(blocks)
    for i, term in enumerate(split_two(rank_side[...])):
        for j in range(2):
            at = (2 * i + j) * lines
            blocks[at : at + lines, j * rank : (j + 1) * rank] = term


def project_rank(blocks, normed):
    both = jnp.dot(blocks[...], normed, preferred_element_type=F32)
    half = both.shape[0] // 2
    return both[:half] + both[half:]


def project_width(value, right):
    high, low = split_two(value)
    return jnp.dot(high, right, preferred_element_type=F32) + jnp.dot(
        low, right, preferred_element_type=F32
    )


STEP = 16


def slots_kernel(m, bounds, owner, source, moments, rank_side, width_side, ordered, *rest):
    out, outer_part, acc, normed, blocks, ranked, wide = rest
    size = ordered.shape[1]
    tokens = source.shape[0]
    rows = tokens // size
    rank, width = outer_part.shape
    lines = rank_side.shape[0]
    low, first, last = example_scalars(bounds, tokens)
    count = bounds.shape[2]
    _, outer, _, outer_on, _ = edges(bounds, low, first, last, tokens)
    rank_side_pair(rank_side, blocks)

    def slot(j):
        return jnp.minimum(first + j, count - 1)

    def inside(j):
        starts, ends = fits(bounds, slot(j), low, tokens)
        return (first + j <= last) & starts & ends

    @pl.loop(0, TOUCH // 2)
    def _(pair):
        slots = (2 * pair, 2 * pair + 1)
        here = [inside(j) for j in slots]
        is_outer = [(first + j == outer) & outer_on for j in slots]
        wanted = [h | o for h, o in zip(here, is_outer)]
        starts = [jnp.where(w, bounds[0, 0, slot(j)], 0) for w, j in zip(wanted, slots)]
        ends = [jnp.where(w, bounds[0, 1, slot(j)], 0) for w, j in zip(wanted, slots)]
        begin_pair = jnp.where(wanted[0], starts[0], starts[1])
        end_pair = jnp.where(wanted[1], ends[1], ends[0])
        for c in range(size):
            begin = low + c * rows

            @pl.when((begin_pair < begin + rows) & (end_pair > begin))
            def _():
                left = jnp.concatenate(
                    [masked(ordered[m, c], begin, s, e) for s, e in zip(starts, ends)], axis=0
                )
                term = jnp.dot(
                    left, source[c * rows : (c + 1) * rows, :], preferred_element_type=F32
                )
                fresh = (begin_pair >= begin) | (c == 0)
                acc[...] = jnp.where(fresh, 0.0, acc[...]) + term

        for k, j in enumerate(slots):

            @pl.when(is_outer[k])
            def _():
                part = ADAPTER_SCALE * acc[k * rank : (k + 1) * rank, :]
                outer_part[...] = part.astype(BF16)

            @pl.when(here[k])
            def _():
                for r in range(0, rank, STEP):
                    normed[j, r : r + STEP, :] = normalize(
                        ADAPTER_SCALE * acc[k * rank + r : k * rank + r + STEP, :],
                        moments[0, m, r : r + STEP, :],
                        moments[1, m, r : r + STEP, :],
                    ).astype(BF16)

            @pl.when(~here[k])
            def _():
                normed[j] = jnp.zeros((rank, width), BF16)

    for j in range(0, TOUCH, 2):
        ranked[j * lines : (j + 2) * lines, :] = project_rank(
            blocks, normed[j : j + 2].reshape(2 * rank, width)
        )
    wide[...] = project_width(ranked[...], width_side[...]).reshape(wide.shape)
    out[...] = jnp.zeros_like(out)
    for j in range(TOUCH):

        @pl.when(inside(j))
        def _():
            out[owner[0, slot(j)]] = wide[j].astype(BF16)


def slot_features(m, bounds, owner, source, moments, rank_side, width_side, ordered, name):
    rank = ordered.shape[2]
    tokens, width = source.shape
    lines = rank_side.shape[0]
    columns = width_side.shape[1]
    return call(
        functools.partial(slots_kernel, m),
        [
            jax.ShapeDtypeStruct((owner.shape[1], lines, columns), BF16),
            jax.ShapeDtypeStruct((rank, width), BF16),
        ],
        [SMEM, SMEM] + [VMEM] * 5,
        [VMEM, VMEM],
        [
            pltpu.VMEM((2 * rank, width), F32),
            pltpu.VMEM((TOUCH, rank, width), BF16),
            pltpu.VMEM((4 * lines, 2 * rank), BF16),
            pltpu.VMEM((TOUCH * lines, width), F32),
            pltpu.VMEM((TOUCH, lines, columns), F32),
        ],
        2 * tokens * width * rank * TOUCH,
        4 * tokens * width,
        name,
    )(bounds, owner, source, moments, rank_side, width_side, ordered)


def crossing_kernel(
    tokens,
    hops,
    bounds,
    owner,
    filled_grad,
    filled_in,
    outer_grad,
    outer_in,
    kept,
    received,
    moments,
    rank_side,
    width_side,
    *rest
):
    arrived = rest[:hops]
    out, normed, blocks, ranked = rest[hops:]
    low, first, last = example_scalars(bounds, tokens)
    rank = outer_in.shape[0]
    lines = rank_side.shape[0]
    half = kept.shape[1]
    inner, outer, inner_on, _, outer_done = edges(bounds, low, first, last, tokens)
    place, middle = lax.axis_index("seq"), lax.axis_size("seq") // 2
    inner_done = inner_on & ((place == middle - 1) | (place == middle))
    out[:, :lines] = filled_grad[...]
    out[:, lines:] = filled_in[...]
    rank_side_pair(rank_side, blocks)

    @pl.when(outer_done)
    def _():
        for m, part in enumerate((outer_grad, outer_in)):
            for r in range(0, rank, STEP):
                here = slice(r, r + STEP)
                grads = part[here, :].astype(F32)
                for k in range(hops):
                    grads = grads + arrived[k][m, here, :].astype(F32)
                normed[m * rank + r : m * rank + r + STEP, :] = normalize(
                    grads, moments[0, m, here, :], moments[1, m, here, :]
                ).astype(BF16)
        ranked[: 2 * lines, :] = project_rank(blocks, normed[...])

    @pl.when(inner_done)
    def _():
        offset = jnp.where(left_side(), 0, half)
        normed[...] = jnp.zeros_like(normed)
        for m in range(2):
            for r in range(0, half, STEP):
                here = pl.ds(pl.multiple_of(offset + r, STEP), STEP)
                there = pl.ds(pl.multiple_of(m * rank + offset + r, STEP), STEP)
                grads = kept[m, r : r + STEP, :].astype(F32)
                grads = grads + received[m, r : r + STEP, :].astype(F32)
                normed[there, :] = normalize(
                    grads, moments[0, m, here, :], moments[1, m, here, :]
                ).astype(BF16)
        ranked[2 * lines :, :] = project_rank(blocks, normed[...])

    @pl.when(outer_done | inner_done)
    def _():
        wide = project_width(ranked[...], width_side[...]).astype(BF16)

        @pl.when(outer_done)
        def _():
            out[owner[0, outer]] = wide[: 2 * lines]

        @pl.when(inner_done)
        def _():
            out[owner[0, inner]] = wide[2 * lines :]


def crossing_features(
    tokens, bounds, owner, filled, outer, kept, received, moments, rank_side, width_side, arrived
):
    hops = len(arrived)
    rank, width = outer[0].shape
    slots, lines, columns = filled[0].shape
    return call(
        functools.partial(crossing_kernel, tokens, hops),
        jax.ShapeDtypeStruct((slots, 2 * lines, columns), BF16),
        [SMEM, SMEM] + [VMEM] * (9 + hops),
        VMEM,
        [
            pltpu.VMEM((2 * rank, width), BF16),
            pltpu.VMEM((4 * lines, 2 * rank), BF16),
            pltpu.VMEM((4 * lines, width), F32),
        ],
        8 * width * 2 * rank * 4 * lines,
        12 * rank * width,
        "crossing_features",
    )(
        bounds,
        owner,
        *filled,
        *outer,
        kept,
        received,
        moments,
        rank_side,
        width_side,
        *arrived,
    )


def owned_kernel(arrived, out):
    total = arrived[0].astype(F32)
    for k in range(1, arrived.shape[0]):
        total = total + arrived[k].astype(F32)
    columns = total.shape[1]
    for line in range(total.shape[0]):
        out[:, line * columns : (line + 1) * columns] = total[line : line + 1, :]


def owned_features(arrived):
    _, lines, columns = arrived.shape
    return call(
        owned_kernel,
        jax.ShapeDtypeStruct((1, lines * columns), F32),
        [VMEM],
        VMEM,
        [],
        arrived.size,
        2 * arrived.size,
        "owned_features",
    )(arrived)


TILE = 256


def depth_chunks(depth):
    return [0, depth // 8, 3 * depth // 8, 5 * depth // 8, 7 * depth // 8, depth]


def operand_copies(source, weight, held, weight_buf, sem, column):
    edges = depth_chunks(held.shape[1])
    pairs = []
    for c, (begin, end) in enumerate(zip(edges, edges[1:])):
        depth = pl.ds(begin, end - begin)
        columns = pl.ds(column, weight_buf.shape[0])
        pair = (
            pltpu.make_async_copy(source.at[:, depth], held.at[:, depth], sem.at[0, c]),
            pltpu.make_async_copy(weight.at[columns, depth], weight_buf.at[:, depth], sem.at[1, c]),
        )
        pairs.append((slice(begin, end), pair))
    return pairs


def start_all(pairs):
    for _, pair in pairs:
        for copy in pair:
            copy.start()


def add_chunk(pairs, c, held, weight_buf, out):
    depth, pair = pairs[c]
    for copy in pair:
        copy.wait()
    for n in range(0, weight_buf.shape[0], TILE):
        there = slice(n, n + TILE)
        term = dot_trailing(held[:, depth], weight_buf[there, depth])
        out[:, there] = term if c == 0 else out[:, there] + term


def first_kernel(column, source, weight, out, acc, held, weight_buf, sem):
    pairs = operand_copies(source, weight, held, weight_buf, sem, column)
    start_all(pairs)
    for c in range(len(pairs)):
        add_chunk(pairs, c, held, weight_buf, acc)
    out[...] = acc[...].astype(BF16)


def second_kernel(size, count, source, weight, down, *rest):
    done, pieces = rest[:count], rest[count : count + size]
    out, result, acc, low_rows, held, weight_buf, *bufs = rest[count + size :]
    down_buf, *bufs = bufs
    done_bufs, (pieces_buf, sem, extra_sem, out_sem) = bufs[:count], bufs[count:]
    tokens, width = result.shape
    split = sum(part.shape[1] for part in done)
    place = lax.axis_index("tensor")
    rows = tokens // size
    rank = low_rows.shape[1]
    extras = [pltpu.make_async_copy(down, down_buf, extra_sem.at[0])]
    for k, piece in enumerate(pieces):
        extras.append(pltpu.make_async_copy(piece, pieces_buf.at[k], extra_sem.at[1 + k]))
    for k, part in enumerate(done):
        extras.append(pltpu.make_async_copy(part, done_bufs[k], extra_sem.at[1 + size + k]))
    pairs = operand_copies(source, weight, held, weight_buf, sem, split)
    early = 2
    start_all(pairs[:early])
    for copy in extras:
        copy.start()
    start_all(pairs[early:])
    for c in range(early):
        add_chunk(pairs, c, held, weight_buf, acc)
    for copy in extras:
        copy.wait()
    for k in range(size):
        block = lax.rem(place + size - k, size)
        low_rows[pl.ds(pl.multiple_of(block * rows, rows), rows), :] = (
            pieces_buf[k, rank:, :].astype(F32).T.astype(BF16)
        )

    def out_copy(begin, end, k):
        here = pl.ds(begin, end - begin)
        return pltpu.make_async_copy(result.at[:, here], out.at[:, here], out_sem.at[k])

    def finish(base, begin, end, k):
        extra = dot_trailing(low_rows[...], down_buf[begin:end, :])
        result[:, begin:end] = (base[...].astype(F32) + ADAPTER_SCALE * extra).astype(BF16)
        out_copy(begin, end, k).start()

    cuts = [0]
    for k, part in enumerate(done_bufs):
        cuts.append(cuts[-1] + part.shape[1])
        finish(part, cuts[-2], cuts[-1], k)
    cuts.append(width)
    for c in range(early, len(pairs)):
        add_chunk(pairs, c, held, weight_buf, acc)
    finish(acc, split, width, count)
    for k in range(count + 1):
        out_copy(cuts[k], cuts[k + 1], k).wait()


def first_product(source, weight, column, split):
    tokens, depth = source.shape
    return call(
        functools.partial(first_kernel, column),
        jax.ShapeDtypeStruct((tokens, split), BF16),
        [HBM, HBM],
        VMEM,
        [
            pltpu.VMEM((tokens, split), F32),
            pltpu.VMEM((tokens, depth), BF16),
            pltpu.VMEM((split, depth), BF16),
            pltpu.SemaphoreType.DMA((2, len(depth_chunks(depth)) - 1)),
        ],
        2 * tokens * depth * split,
        2 * depth * (tokens + split),
        "first_product",
        FIRST_VMEM,
    )(source, weight)


def second_product(source, weight, down, done, pieces):
    tokens, depth = source.shape
    width, rank = down.shape
    rest = width - sum(part.shape[1] for part in done)
    size, count = len(pieces), len(done)
    return call(
        functools.partial(second_kernel, size, count),
        jax.ShapeDtypeStruct((tokens, width), BF16),
        [HBM] * (3 + count + size),
        HBM,
        [
            pltpu.VMEM((tokens, width), BF16),
            pltpu.VMEM((tokens, rest), F32),
            pltpu.VMEM((tokens, rank), BF16),
            pltpu.VMEM((tokens, depth), BF16),
            pltpu.VMEM((rest, depth), BF16),
            pltpu.VMEM(down.shape, BF16),
        ]
        + [pltpu.VMEM(part.shape, BF16) for part in done]
        + [
            pltpu.VMEM((size,) + pieces[0].shape, BF16),
            pltpu.SemaphoreType.DMA((2, len(depth_chunks(depth)) - 1)),
            pltpu.SemaphoreType.DMA((1 + size + count,)),
            pltpu.SemaphoreType.DMA((count + 1,)),
        ],
        2 * tokens * depth * rest,
        2 * depth * (tokens + rest),
        "second_product",
        SECOND_VMEM,
    )(source, weight, down, *done, *pieces)


def prepare_kernel(source_in, source_grad, width_side, first, second, other, *rest):
    rows_in, columns_grad, right, moments, own, arrived, sem = rest
    place = lax.axis_index("tensor")
    width, rows = right.shape[0], own.shape[2]
    here = pl.ds(pl.multiple_of(place * width, width), width)
    copies = [
        pltpu.make_async_copy(first, own.at[0], sem.at[0]),
        pltpu.make_async_copy(second, own.at[1], sem.at[1]),
        pltpu.make_async_copy(other, arrived, sem.at[2]),
        pltpu.make_async_copy(source_grad.at[:, here], columns_grad, sem.at[3]),
        pltpu.make_async_copy(source_in, rows_in, sem.at[4]),
        pltpu.make_async_copy(width_side.at[here], right, sem.at[5]),
    ]
    for copy in copies:
        copy.start()
    for copy in copies[:3]:
        copy.wait()
    mine = lax.axis_index("dp")
    for i, beta in enumerate((BETA_ONE, BETA_TWO)):
        for m in range(2):
            if arrived.shape[2] == rows:
                at = pl.ds(pl.multiple_of(mine * rows, rows), rows)
                moments[i, m, at, :] = beta * own[i, m]
                at = pl.ds(pl.multiple_of((1 - mine) * rows, rows), rows)
                moments[i, m, at, :] = beta * arrived[i, m].astype(F32)
            else:
                moments[i, m] = beta * arrived[i, m].astype(F32)
    for copy in copies[3:]:
        copy.wait()


def other_moments(own):
    if lax.axis_size("dp") != 2:
        return lax.all_gather(own, "dp", axis=2, tiled=True)
    return shifted(own, "dp", 1)


def prepare(rows_in, rows_grad, width_side, first, second, other):
    tokens, width = rows_in.shape
    columns = width_side.shape[1]
    rank = first.shape[1] * lax.axis_size("dp")
    return call(
        prepare_kernel,
        [
            jax.ShapeDtypeStruct((tokens, width), BF16),
            jax.ShapeDtypeStruct((tokens, width), BF16),
            jax.ShapeDtypeStruct((width, columns), BF16),
            jax.ShapeDtypeStruct((2, 2, rank, width), F32),
        ],
        [HBM] * 6,
        [VMEM] * 4,
        [
            pltpu.VMEM((2,) + first.shape, F32),
            pltpu.VMEM(other.shape, BF16),
            pltpu.SemaphoreType.DMA((6,)),
        ],
        8 * rank * width,
        4 * tokens * width + 8 * rank * width,
        "prepare",
        PREPARE_VMEM,
    )(rows_in, rows_grad, width_side, first, second, other)


def per_device(
    attention_output_rows,
    projection_result_gradient,
    adapter_down_weight,
    adapter_up_weight,
    output_projection_weight,
    adam_first_moments,
    adam_second_moments,
    rank_side_projection,
    width_side_projection,
    bounds,
    example_owner_slot,
):
    packs, blk, width_local = attention_output_rows.shape
    assert packs == 1
    width = projection_result_gradient.shape[2]
    size = lax.axis_size("tensor")
    rows_in = attention_output_rows.reshape(blk, width_local)
    rows_grad = projection_result_gradient.reshape(blk, width)

    own_moments = (adam_first_moments, adam_second_moments)
    *pieces, sent_moments = rank_pieces(
        rows_in, rows_grad, adapter_down_weight, adapter_up_weight, *own_moments, size
    )
    other = other_moments(sent_moments)
    cuts = [0, width_local // 4, 3 * width_local // 4]

    def product(rows, k):
        return first_product(rows, output_projection_weight, cuts[k], cuts[k + 1] - cuts[k])

    done = [product(rows_grad, 0)]
    sent, done = lax.optimization_barrier((scatter(pieces), done))
    total, rows_late, bounds_late = lax.optimization_barrier((total_of(sent), rows_grad, bounds))
    done.append(product(rows_late, 1))
    done, rows_late, other = lax.optimization_barrier((done, rows_late, other))
    prepared = prepare(rows_in, rows_late, width_side_projection, *own_moments, other)
    first_token = lax.axis_index("seq") * blk
    end_token = first_token + blk
    starts, ends = bounds_late[0, 0], bounds_late[0, 1]
    left = left_side()
    spans = jnp.any(
        jnp.where(
            left,
            (starts < first_token) & (ends >= end_token),
            (starts <= first_token) & (ends > end_token),
        )
    ).astype(F32)
    low, prepared, done, spans = lax.optimization_barrier(
        (gather_pieces(total), prepared, done, spans)
    )
    rows_in, columns_grad, right, moments = prepared
    inner, ordered = inner_parts(bounds, rows_in, columns_grad, low)
    shared = (rank_side_projection, right)
    seq = lax.axis_size("seq")
    middle = seq // 2

    def onward(arrived):
        return inner.astype(F32) + spans * arrived.astype(F32)

    arrived = []
    outgoing = inner
    for k in range(middle - 1):
        pairs = [(k, k + 1), (k + 1, k), (seq - 1 - k, seq - 2 - k), (seq - 2 - k, seq - 1 - k)]
        moved = lax.ppermute(outgoing, "seq", pairs)
        if middle > 2:
            place = lax.axis_index("seq")
            moved = jnp.where((place == k + 1) | (place == seq - 2 - k), moved, 0)
        arrived.append(moved)
        outgoing = onward(arrived[-1]).astype(BF16)
    filled_in, outer_in = slot_features(
        1, bounds, example_owner_slot, columns_grad, moments, *shared, ordered, "slots_in"
    )
    arrived, rows_in, outer_in = lax.optimization_barrier((arrived, rows_in, outer_in))
    summed = onward(arrived[-1]).astype(BF16)
    half = summed.shape[1] // 2
    kept = jnp.where(left, summed[:, :half], summed[:, half:])
    sent = jnp.where(left, summed[:, half:], summed[:, :half])
    received = lax.ppermute(sent, "seq", [(middle - 1, middle), (middle, middle - 1)])
    filled_grad, outer_grad = slot_features(
        0, bounds, example_owner_slot, rows_in, moments, *shared, ordered, "slots_grad"
    )
    received, outer_grad = lax.optimization_barrier((received, outer_grad))
    buffer = crossing_features(
        blk,
        bounds,
        example_owner_slot,
        (filled_grad, filled_in),
        (outer_grad, outer_in),
        kept,
        received,
        moments,
        *shared,
        arrived,
    )
    arrived = lax.all_to_all(buffer, ("seq", "tensor"), split_axis=0, concat_axis=0, tiled=True)
    features = owned_features(arrived)[None]
    out = second_product(
        rows_grad,
        output_projection_weight,
        adapter_down_weight,
        done,
        low,
    )
    return (out.reshape(attention_output_rows.shape), features)


def solution(mesh):
    return jax.shard_map(
        per_device,
        mesh=mesh,
        in_specs=(
            P("dp", "seq", "tensor"),
            P("dp", "seq", None),
            P("tensor", None),
            P(None, "tensor"),
            P("tensor", None),
            P(None, "dp", "tensor"),
            P(None, "dp", "tensor"),
            P(),
            P(),
            P("dp", None, None),
            P("dp", None),
        ),
        out_specs=(P("dp", "seq", "tensor"), P("dp", ("seq", "tensor"), None)),
        check_vma=False,
    )
```

```python
import functools

import jax
import jax.numpy as jnp
from jax import lax
from jax.experimental import pallas as pl
from jax.experimental.pallas import tpu as pltpu
from jax.sharding import PartitionSpec as P

TOUCH = 8
ADAPTER_SCALE = 4.0
BETA_ONE = 0.9
BETA_TWO = 0.999
EPSILON = 1e-08
MIB = 2**20
PIECES_VMEM, FIRST_VMEM, PREPARE_VMEM, SECOND_VMEM = 53.4, 48, 45, 46
BF16 = jnp.bfloat16
F32 = jnp.float32

HBM = pl.BlockSpec(memory_space=pltpu.HBM)
VMEM = pl.BlockSpec(memory_space=pltpu.VMEM)
SMEM = pl.BlockSpec(memory_space=pltpu.SMEM)


def dot_trailing(left, right):
    return lax.dot_general(left, right, (((1,), (1,)), ((), ())), preferred_element_type=F32)


def call(kernel, out_shape, in_specs, out_specs, scratch, flops, nbytes, name, vmem=32):
    return pl.pallas_call(
        kernel,
        out_shape=out_shape,
        in_specs=in_specs,
        out_specs=out_specs,
        scratch_shapes=scratch,
        compiler_params=pltpu.CompilerParams(vmem_limit_bytes=int(vmem * MIB)),
        cost_estimate=pl.CostEstimate(flops=flops, bytes_accessed=nbytes, transcendentals=0),
        name=name,
    )


def pieces_kernel(source_in, source_grad, down, up, first, second, *rest):
    *outs, moments, rows_in, rows_grad, partial, own, cast, down_buf, up_buf, sem, own_sem = rest
    size = len(outs)
    own_copies = [
        pltpu.make_async_copy(moment, own.at[i], own_sem.at[i])
        for i, moment in enumerate((first, second))
    ]
    place = lax.axis_index("tensor")
    tokens, width = rows_in.shape
    rows = tokens // size
    rank = up_buf.shape[0]
    there = pl.ds(pl.multiple_of(place * width, width), width)
    copies = []
    for i in range(size):
        here = pl.ds(i * rows, rows)
        copies.append(pltpu.make_async_copy(source_in.at[here], rows_in.at[here], sem.at[0, i]))
    for i in range(size):
        here = pl.ds(i * rows, rows)
        copies.append(
            pltpu.make_async_copy(source_grad.at[here, there], rows_grad.at[here], sem.at[1, i])
        )
    copies.insert(0, pltpu.make_async_copy(down, down_buf, sem.at[0, size]))
    copies.insert(size + 1, pltpu.make_async_copy(up, up_buf, sem.at[1, size]))
    for copy in copies[: size + 1] + own_copies + copies[size + 1 :]:
        copy.start()
    for copy in copies[: size + 1]:
        copy.wait()
    product = jnp.dot(rows_in[...], down_buf[...], preferred_element_type=F32)
    partial[:, :rank] = product.astype(BF16)
    for i, copy in enumerate(own_copies):
        copy.wait()
        cast[i] = own[i].astype(BF16)
    cast_copy = pltpu.make_async_copy(cast, moments, own_sem.at[2])
    cast_copy.start()
    for copy in copies[size + 1 :]:
        copy.wait()
    partial[:, rank:] = dot_trailing(rows_grad[...], up_buf[...]).astype(BF16)
    for k, out in enumerate(outs):
        block = pl.multiple_of(lax.rem(place + k, size) * rows, rows)
        out[...] = partial[pl.ds(block, rows), :]
    cast_copy.wait()


def rank_pieces(rows_in, rows_grad, down, up, first, second, size):
    tokens, width = rows_in.shape
    rank = up.shape[0]
    rows = tokens // size
    return call(
        pieces_kernel,
        [jax.ShapeDtypeStruct((rows, 2 * rank), BF16)] * size
        + [jax.ShapeDtypeStruct((2,) + first.shape, BF16)],
        [HBM] * 6,
        [VMEM] * size + [HBM],
        [
            pltpu.VMEM((tokens, width), BF16),
            pltpu.VMEM((tokens, width), BF16),
            pltpu.VMEM((tokens, 2 * rank), BF16),
            pltpu.VMEM((2,) + first.shape, F32),
            pltpu.VMEM((2,) + first.shape, BF16),
            pltpu.VMEM(down.shape, BF16),
            pltpu.VMEM(up.shape, BF16),
            pltpu.SemaphoreType.DMA((2, size + 1)),
            pltpu.SemaphoreType.DMA((3,)),
        ],
        4 * tokens * width * rank,
        4 * tokens * width,
        "rank_pieces",
        PIECES_VMEM,
    )(rows_in, rows_grad, down, up, first, second)


def shifted(value, axis, shift):
    size = lax.axis_size(axis)
    return lax.ppermute(value, axis, [(i, (i + shift) % size) for i in range(size)])


def scatter(pieces):
    return [shifted(piece, "tensor", k) if k else piece for k, piece in enumerate(pieces)]


def total_kernel(*refs):
    *terms, out = refs
    total = terms[0][...].astype(F32)
    for term in terms[1:]:
        total = total + term[...].astype(F32)
    out[...] = total.T.astype(BF16)


def total_of(terms):
    rows, ranks = terms[0].shape
    return call(
        total_kernel,
        jax.ShapeDtypeStruct((ranks, rows), BF16),
        [VMEM] * len(terms),
        VMEM,
        [],
        len(terms) * rows * ranks,
        2 * (len(terms) + 1) * rows * ranks,
        "total_low",
    )(*terms)


def gather_pieces(total):
    size = lax.axis_size("tensor")
    return [total] + [shifted(total, "tensor", k) for k in range(1, size)]


def example_scalars(bounds, block):
    low = lax.axis_index("seq") * block
    count = bounds.shape[2]
    first = jnp.int32(-1)
    last = jnp.int32(-1)
    for e in range(count):
        start = bounds[0, 0, e]
        first = first + (start <= low).astype(jnp.int32)
        last = last + (start <= low + block - 1).astype(jnp.int32)
    return low, first, last


def place_pieces(pieces, m, low_scratch):
    size = len(pieces)
    place = lax.axis_index("tensor")
    rank = low_scratch.shape[1]
    first = (1 - m) * rank
    for k, piece in enumerate(pieces):
        low_scratch[lax.rem(place + size - k, size)] = piece[first : first + rank, :]


def masked(low_piece, offset, start, end):
    tokens = offset + lax.broadcasted_iota(jnp.int32, low_piece.shape, 1)
    return jnp.where((tokens >= start) & (tokens < end), low_piece.astype(F32), 0.0).astype(BF16)


def left_side():
    return lax.axis_index("seq") < lax.axis_size("seq") // 2


def fits(bounds, example, low, tokens):
    return bounds[0, 0, example] >= low, bounds[0, 1, example] <= low + tokens


def edges(bounds, low, first, last, tokens):
    left = left_side()
    inner = jnp.where(left, last, first)
    outer = jnp.where(left, first, last)
    inner_starts, inner_ends = fits(bounds, inner, low, tokens)
    outer_starts, outer_ends = fits(bounds, outer, low, tokens)
    inner_on = (left & ~inner_ends) | (~left & ~inner_starts)
    outer_on = (left & ~outer_starts) | (~left & ~outer_ends)
    outer_inside = (left & outer_ends) | (~left & outer_starts)
    return inner, outer, inner_on, outer_on, outer_on & outer_inside


def sum_part(acc, source, low_scratch, low, start, end):
    size, _, rows = low_scratch.shape
    for c in range(size):
        begin = low + c * rows

        @pl.when((start < begin + rows) & (end > begin))
        def _():
            left = masked(low_scratch[c], begin, start, end)
            term = jnp.dot(
                left, source[c * rows : (c + 1) * rows, :], preferred_element_type=F32
            )
            fresh = (start >= begin) | (c == 0)
            acc[...] = jnp.where(fresh, 0.0, acc[...]) + term


def inner_kernel(size, bounds, rows_in, rows_grad, *rest):
    pieces = rest[:size]
    out, ordered, acc = rest[size:]
    tokens = rows_in.shape[0]
    low, first, last = example_scalars(bounds, tokens)
    inner = edges(bounds, low, first, last, tokens)[0]
    for m, source in enumerate((rows_in, rows_grad)):
        place_pieces(pieces, m, ordered.at[m])
        sum_part(acc, source, ordered.at[m], low, bounds[0, 0, inner], bounds[0, 1, inner])
        out[m] = (ADAPTER_SCALE * acc[...]).astype(BF16)


def inner_parts(bounds, rows_in, rows_grad, low):
    size = len(low)
    rank, rows = low[0].shape[0] // 2, low[0].shape[1]
    tokens, width = rows_in.shape
    return call(
        functools.partial(inner_kernel, size),
        [
            jax.ShapeDtypeStruct((2, rank, width), BF16),
            jax.ShapeDtypeStruct((2, size, rank, rows), BF16),
        ],
        [SMEM] + [VMEM] * (2 + size),
        [VMEM, VMEM],
        [pltpu.VMEM((rank, width), F32)],
        4 * tokens * width * rank,
        4 * tokens * width,
        "inner_parts",
    )(bounds, rows_in, rows_grad, *low)


def normalize(grads, first_moment, second_moment):
    first = first_moment + (1.0 - BETA_ONE) * grads
    second = second_moment + ((1.0 - BETA_TWO) * grads) * grads
    guess = lax.rsqrt(second)
    below = second * guess + EPSILON
    return first * (guess * (2.0 - below * guess))


def split_two(value):
    high = value.astype(BF16)
    return high, (value - high.astype(F32)).astype(BF16)


def rank_side_pair(rank_side, blocks):
    lines, rank = rank_side.shape
    blocks[...] = jnp.zeros_like(blocks)
    for i, term in enumerate(split_two(rank_side[...])):
        for j in range(2):
            at = (2 * i + j) * lines
            blocks[at : at + lines, j * rank : (j + 1) * rank] = term


def project_rank(blocks, normed):
    both = jnp.dot(blocks[...], normed, preferred_element_type=F32)
    half = both.shape[0] // 2
    return both[:half] + both[half:]


def project_width(value, right):
    high, low = split_two(value)
    return jnp.dot(high, right, preferred_element_type=F32) + jnp.dot(
        low, right, preferred_element_type=F32
    )


STEP = 16


def slots_kernel(m, bounds, owner, source, moments, rank_side, width_side, ordered, *rest):
    out, outer_part, acc, normed, blocks, ranked, wide = rest
    size = ordered.shape[1]
    tokens = source.shape[0]
    rows = tokens // size
    rank, width = outer_part.shape
    lines = rank_side.shape[0]
    low, first, last = example_scalars(bounds, tokens)
    count = bounds.shape[2]
    _, outer, _, outer_on, _ = edges(bounds, low, first, last, tokens)
    rank_side_pair(rank_side, blocks)

    def slot(j):
        return jnp.minimum(first + j, count - 1)

    def inside(j):
        starts, ends = fits(bounds, slot(j), low, tokens)
        return (first + j <= last) & starts & ends

    @pl.loop(0, TOUCH // 2)
    def _(pair):
        slots = (2 * pair, 2 * pair + 1)
        here = [inside(j) for j in slots]
        is_outer = [(first + j == outer) & outer_on for j in slots]
        wanted = [h | o for h, o in zip(here, is_outer)]
        starts = [jnp.where(w, bounds[0, 0, slot(j)], 0) for w, j in zip(wanted, slots)]
        ends = [jnp.where(w, bounds[0, 1, slot(j)], 0) for w, j in zip(wanted, slots)]
        begin_pair = jnp.where(wanted[0], starts[0], starts[1])
        end_pair = jnp.where(wanted[1], ends[1], ends[0])
        for c in range(size):
            begin = low + c * rows

            @pl.when((begin_pair < begin + rows) & (end_pair > begin))
            def _():
                left = jnp.concatenate(
                    [masked(ordered[m, c], begin, s, e) for s, e in zip(starts, ends)], axis=0
                )
                term = jnp.dot(
                    left, source[c * rows : (c + 1) * rows, :], preferred_element_type=F32
                )
                fresh = (begin_pair >= begin) | (c == 0)
                acc[...] = jnp.where(fresh, 0.0, acc[...]) + term

        for k, j in enumerate(slots):

            @pl.when(is_outer[k])
            def _():
                part = ADAPTER_SCALE * acc[k * rank : (k + 1) * rank, :]
                outer_part[...] = part.astype(BF16)

            @pl.when(here[k])
            def _():
                for r in range(0, rank, STEP):
                    normed[j, r : r + STEP, :] = normalize(
                        ADAPTER_SCALE * acc[k * rank + r : k * rank + r + STEP, :],
                        moments[0, m, r : r + STEP, :],
                        moments[1, m, r : r + STEP, :],
                    ).astype(BF16)

            @pl.when(~here[k])
            def _():
                normed[j] = jnp.zeros((rank, width), BF16)

    for j in range(0, TOUCH, 2):
        ranked[j * lines : (j + 2) * lines, :] = project_rank(
            blocks, normed[j : j + 2].reshape(2 * rank, width)
        )
    wide[...] = project_width(ranked[...], width_side[...]).reshape(wide.shape)
    out[...] = jnp.zeros_like(out)
    for j in range(TOUCH):

        @pl.when(inside(j))
        def _():
            out[owner[0, slot(j)]] = wide[j].astype(BF16)


def slot_features(m, bounds, owner, source, moments, rank_side, width_side, ordered, name):
    rank = ordered.shape[2]
    tokens, width = source.shape
    lines = rank_side.shape[0]
    columns = width_side.shape[1]
    return call(
        functools.partial(slots_kernel, m),
        [
            jax.ShapeDtypeStruct((owner.shape[1], lines, columns), BF16),
            jax.ShapeDtypeStruct((rank, width), BF16),
        ],
        [SMEM, SMEM] + [VMEM] * 5,
        [VMEM, VMEM],
        [
            pltpu.VMEM((2 * rank, width), F32),
            pltpu.VMEM((TOUCH, rank, width), BF16),
            pltpu.VMEM((4 * lines, 2 * rank), BF16),
            pltpu.VMEM((TOUCH * lines, width), F32),
            pltpu.VMEM((TOUCH, lines, columns), F32),
        ],
        2 * tokens * width * rank * TOUCH,
        4 * tokens * width,
        name,
    )(bounds, owner, source, moments, rank_side, width_side, ordered)


def crossing_kernel(
    tokens,
    hops,
    bounds,
    owner,
    filled_grad,
    filled_in,
    outer_grad,
    outer_in,
    kept,
    received,
    moments,
    rank_side,
    width_side,
    *rest
):
    arrived = rest[:hops]
    out, normed, blocks, ranked = rest[hops:]
    low, first, last = example_scalars(bounds, tokens)
    rank = outer_in.shape[0]
    lines = rank_side.shape[0]
    half = kept.shape[1]
    inner, outer, inner_on, _, outer_done = edges(bounds, low, first, last, tokens)
    place, middle = lax.axis_index("seq"), lax.axis_size("seq") // 2
    inner_done = inner_on & ((place == middle - 1) | (place == middle))
    out[:, :lines] = filled_grad[...]
    out[:, lines:] = filled_in[...]
    rank_side_pair(rank_side, blocks)

    @pl.when(outer_done)
    def _():
        for m, part in enumerate((outer_grad, outer_in)):
            for r in range(0, rank, STEP):
                here = slice(r, r + STEP)
                grads = part[here, :].astype(F32)
                for k in range(hops):
                    grads = grads + arrived[k][m, here, :].astype(F32)
                normed[m * rank + r : m * rank + r + STEP, :] = normalize(
                    grads, moments[0, m, here, :], moments[1, m, here, :]
                ).astype(BF16)
        ranked[: 2 * lines, :] = project_rank(blocks, normed[...])

    @pl.when(inner_done)
    def _():
        offset = jnp.where(left_side(), 0, half)
        normed[...] = jnp.zeros_like(normed)
        for m in range(2):
            for r in range(0, half, STEP):
                here = pl.ds(pl.multiple_of(offset + r, STEP), STEP)
                there = pl.ds(pl.multiple_of(m * rank + offset + r, STEP), STEP)
                grads = kept[m, r : r + STEP, :].astype(F32)
                grads = grads + received[m, r : r + STEP, :].astype(F32)
                normed[there, :] = normalize(
                    grads, moments[0, m, here, :], moments[1, m, here, :]
                ).astype(BF16)
        ranked[2 * lines :, :] = project_rank(blocks, normed[...])

    @pl.when(outer_done | inner_done)
    def _():
        wide = project_width(ranked[...], width_side[...]).astype(BF16)

        @pl.when(outer_done)
        def _():
            out[owner[0, outer]] = wide[: 2 * lines]

        @pl.when(inner_done)
        def _():
            out[owner[0, inner]] = wide[2 * lines :]


def crossing_features(
    tokens, bounds, owner, filled, outer, kept, received, moments, rank_side, width_side, arrived
):
    hops = len(arrived)
    rank, width = outer[0].shape
    slots, lines, columns = filled[0].shape
    return call(
        functools.partial(crossing_kernel, tokens, hops),
        jax.ShapeDtypeStruct((slots, 2 * lines, columns), BF16),
        [SMEM, SMEM] + [VMEM] * (9 + hops),
        VMEM,
        [
            pltpu.VMEM((2 * rank, width), BF16),
            pltpu.VMEM((4 * lines, 2 * rank), BF16),
            pltpu.VMEM((4 * lines, width), F32),
        ],
        8 * width * 2 * rank * 4 * lines,
        12 * rank * width,
        "crossing_features",
    )(
        bounds,
        owner,
        *filled,
        *outer,
        kept,
        received,
        moments,
        rank_side,
        width_side,
        *arrived,
    )


def owned_kernel(arrived, out):
    total = arrived[0].astype(F32)
    for k in range(1, arrived.shape[0]):
        total = total + arrived[k].astype(F32)
    columns = total.shape[1]
    for line in range(total.shape[0]):
        out[:, line * columns : (line + 1) * columns] = total[line : line + 1, :]


def owned_features(arrived):
    _, lines, columns = arrived.shape
    return call(
        owned_kernel,
        jax.ShapeDtypeStruct((1, lines * columns), F32),
        [VMEM],
        VMEM,
        [],
        arrived.size,
        2 * arrived.size,
        "owned_features",
    )(arrived)


TILE = 256


def depth_chunks(depth):
    return [0, depth // 8, 3 * depth // 8, 5 * depth // 8, 7 * depth // 8, depth]


def operand_copies(source, weight, held, weight_buf, sem, column):
    edges = depth_chunks(held.shape[1])
    pairs = []
    for c, (begin, end) in enumerate(zip(edges, edges[1:])):
        depth = pl.ds(begin, end - begin)
        columns = pl.ds(column, weight_buf.shape[0])
        pair = (
            pltpu.make_async_copy(source.at[:, depth], held.at[:, depth], sem.at[0, c]),
            pltpu.make_async_copy(weight.at[columns, depth], weight_buf.at[:, depth], sem.at[1, c]),
        )
        pairs.append((slice(begin, end), pair))
    return pairs


def start_all(pairs):
    for _, pair in pairs:
        for copy in pair:
            copy.start()


def add_chunk(pairs, c, held, weight_buf, out):
    depth, pair = pairs[c]
    for copy in pair:
        copy.wait()
    for n in range(0, weight_buf.shape[0], TILE):
        there = slice(n, min(n + TILE, weight_buf.shape[0]))
        term = dot_trailing(held[:, depth], weight_buf[there, depth])
        out[:, there] = term if c == 0 else out[:, there] + term


def first_kernel(column, source, weight, out, acc, held, weight_buf, sem):
    pairs = operand_copies(source, weight, held, weight_buf, sem, column)
    start_all(pairs)
    for c in range(len(pairs)):
        add_chunk(pairs, c, held, weight_buf, acc)
    out[...] = acc[...].astype(BF16)


def second_kernel(size, count, source, weight, down, *rest):
    done, pieces = rest[:count], rest[count : count + size]
    out, result, acc, low_rows, held, weight_buf, *bufs = rest[count + size :]
    down_buf, *bufs = bufs
    done_bufs, (pieces_buf, sem, extra_sem, out_sem) = bufs[:count], bufs[count:]
    tokens, width = result.shape
    split = sum(part.shape[1] for part in done)
    place = lax.axis_index("tensor")
    rows = tokens // size
    rank = low_rows.shape[1]
    extras = [pltpu.make_async_copy(down, down_buf, extra_sem.at[0])]
    for k, piece in enumerate(pieces):
        extras.append(pltpu.make_async_copy(piece, pieces_buf.at[k], extra_sem.at[1 + k]))
    for k, part in enumerate(done):
        extras.append(pltpu.make_async_copy(part, done_bufs[k], extra_sem.at[1 + size + k]))
    pairs = operand_copies(source, weight, held, weight_buf, sem, split)
    early = 2
    start_all(pairs[:early])
    for copy in extras:
        copy.start()
    start_all(pairs[early:])
    for c in range(early):
        add_chunk(pairs, c, held, weight_buf, acc)
    for copy in extras:
        copy.wait()
    for k in range(size):
        block = lax.rem(place + size - k, size)
        low_rows[pl.ds(pl.multiple_of(block * rows, rows), rows), :] = (
            pieces_buf[k, rank:, :].astype(F32).T.astype(BF16)
        )

    def out_copy(begin, end, k):
        here = pl.ds(begin, end - begin)
        return pltpu.make_async_copy(result.at[:, here], out.at[:, here], out_sem.at[k])

    def finish(base, begin, end, k):
        extra = dot_trailing(low_rows[...], down_buf[begin:end, :])
        result[:, begin:end] = (base[...].astype(F32) + ADAPTER_SCALE * extra).astype(BF16)
        out_copy(begin, end, k).start()

    cuts = [0]
    for k, part in enumerate(done_bufs):
        cuts.append(cuts[-1] + part.shape[1])
        finish(part, cuts[-2], cuts[-1], k)
    cuts.append(width)
    for c in range(early, len(pairs)):
        add_chunk(pairs, c, held, weight_buf, acc)
    finish(acc, split, width, count)
    for k in range(count + 1):
        out_copy(cuts[k], cuts[k + 1], k).wait()


def first_product(source, weight, column, split):
    tokens, depth = source.shape
    return call(
        functools.partial(first_kernel, column),
        jax.ShapeDtypeStruct((tokens, split), BF16),
        [HBM, HBM],
        VMEM,
        [
            pltpu.VMEM((tokens, split), F32),
            pltpu.VMEM((tokens, depth), BF16),
            pltpu.VMEM((split, depth), BF16),
            pltpu.SemaphoreType.DMA((2, len(depth_chunks(depth)) - 1)),
        ],
        2 * tokens * depth * split,
        2 * depth * (tokens + split),
        "first_product",
        FIRST_VMEM,
    )(source, weight)


def second_product(source, weight, down, done, pieces):
    tokens, depth = source.shape
    width, rank = down.shape
    rest = width - sum(part.shape[1] for part in done)
    size, count = len(pieces), len(done)
    return call(
        functools.partial(second_kernel, size, count),
        jax.ShapeDtypeStruct((tokens, width), BF16),
        [HBM] * (3 + count + size),
        HBM,
        [
            pltpu.VMEM((tokens, width), BF16),
            pltpu.VMEM((tokens, rest), F32),
            pltpu.VMEM((tokens, rank), BF16),
            pltpu.VMEM((tokens, depth), BF16),
            pltpu.VMEM((rest, depth), BF16),
            pltpu.VMEM(down.shape, BF16),
        ]
        + [pltpu.VMEM(part.shape, BF16) for part in done]
        + [
            pltpu.VMEM((size,) + pieces[0].shape, BF16),
            pltpu.SemaphoreType.DMA((2, len(depth_chunks(depth)) - 1)),
            pltpu.SemaphoreType.DMA((1 + size + count,)),
            pltpu.SemaphoreType.DMA((count + 1,)),
        ],
        2 * tokens * depth * rest,
        2 * depth * (tokens + rest),
        "second_product",
        SECOND_VMEM,
    )(source, weight, down, *done, *pieces)


def prepare_kernel(source_in, source_grad, width_side, first, second, other, *rest):
    rows_in, columns_grad, right, moments, own, arrived, sem = rest
    place = lax.axis_index("tensor")
    width, rows = right.shape[0], own.shape[2]
    here = pl.ds(pl.multiple_of(place * width, width), width)
    copies = [
        pltpu.make_async_copy(first, own.at[0], sem.at[0]),
        pltpu.make_async_copy(second, own.at[1], sem.at[1]),
        pltpu.make_async_copy(other, arrived, sem.at[2]),
        pltpu.make_async_copy(source_grad.at[:, here], columns_grad, sem.at[3]),
        pltpu.make_async_copy(source_in, rows_in, sem.at[4]),
        pltpu.make_async_copy(width_side.at[here], right, sem.at[5]),
    ]
    for copy in copies:
        copy.start()
    for copy in copies[:3]:
        copy.wait()
    mine = lax.axis_index("dp")
    for i, beta in enumerate((BETA_ONE, BETA_TWO)):
        for m in range(2):
            if arrived.shape[2] == rows:
                at = pl.ds(pl.multiple_of(mine * rows, rows), rows)
                moments[i, m, at, :] = beta * own[i, m]
                at = pl.ds(pl.multiple_of((1 - mine) * rows, rows), rows)
                moments[i, m, at, :] = beta * arrived[i, m].astype(F32)
            else:
                moments[i, m] = beta * arrived[i, m].astype(F32)
    for copy in copies[3:]:
        copy.wait()


def other_moments(own):
    if lax.axis_size("dp") != 2:
        return lax.all_gather(own, "dp", axis=2, tiled=True)
    return shifted(own, "dp", 1)


def prepare(rows_in, rows_grad, width_side, first, second, other):
    tokens, width = rows_in.shape
    columns = width_side.shape[1]
    rank = first.shape[1] * lax.axis_size("dp")
    return call(
        prepare_kernel,
        [
            jax.ShapeDtypeStruct((tokens, width), BF16),
            jax.ShapeDtypeStruct((tokens, width), BF16),
            jax.ShapeDtypeStruct((width, columns), BF16),
            jax.ShapeDtypeStruct((2, 2, rank, width), F32),
        ],
        [HBM] * 6,
        [VMEM] * 4,
        [
            pltpu.VMEM((2,) + first.shape, F32),
            pltpu.VMEM(other.shape, BF16),
            pltpu.SemaphoreType.DMA((6,)),
        ],
        8 * rank * width,
        4 * tokens * width + 8 * rank * width,
        "prepare",
        PREPARE_VMEM,
    )(rows_in, rows_grad, width_side, first, second, other)


def per_device(
    attention_output_rows,
    projection_result_gradient,
    adapter_down_weight,
    adapter_up_weight,
    output_projection_weight,
    adam_first_moments,
    adam_second_moments,
    rank_side_projection,
    width_side_projection,
    bounds,
    example_owner_slot,
):
    packs, blk, width_local = attention_output_rows.shape
    assert packs == 1
    width = projection_result_gradient.shape[2]
    size = lax.axis_size("tensor")
    rows_in = attention_output_rows.reshape(blk, width_local)
    rows_grad = projection_result_gradient.reshape(blk, width)

    own_moments = (adam_first_moments, adam_second_moments)
    *pieces, sent_moments = rank_pieces(
        rows_in, rows_grad, adapter_down_weight, adapter_up_weight, *own_moments, size
    )
    other = other_moments(sent_moments)
    cuts = [0, 3 * width_local // 8, 5 * width_local // 8]

    def product(rows, k):
        return first_product(rows, output_projection_weight, cuts[k], cuts[k + 1] - cuts[k])

    done = [product(rows_grad, 0)]
    sent, done = lax.optimization_barrier((scatter(pieces), done))
    total, rows_late, bounds_late = lax.optimization_barrier((total_of(sent), rows_grad, bounds))
    done.append(product(rows_late, 1))
    done, rows_late, other = lax.optimization_barrier((done, rows_late, other))
    prepared = prepare(rows_in, rows_late, width_side_projection, *own_moments, other)
    first_token = lax.axis_index("seq") * blk
    end_token = first_token + blk
    starts, ends = bounds_late[0, 0], bounds_late[0, 1]
    left = left_side()
    spans = jnp.any(
        jnp.where(
            left,
            (starts < first_token) & (ends >= end_token),
            (starts <= first_token) & (ends > end_token),
        )
    ).astype(F32)
    low, prepared, done, spans = lax.optimization_barrier(
        (gather_pieces(total), prepared, done, spans)
    )
    rows_in, columns_grad, right, moments = prepared
    inner, ordered = inner_parts(bounds, rows_in, columns_grad, low)
    shared = (rank_side_projection, right)
    seq = lax.axis_size("seq")
    middle = seq // 2

    def onward(arrived):
        return inner.astype(F32) + spans * arrived.astype(F32)

    arrived = []
    outgoing = inner
    for k in range(middle - 1):
        pairs = [(k, k + 1), (k + 1, k), (seq - 1 - k, seq - 2 - k), (seq - 2 - k, seq - 1 - k)]
        moved = lax.ppermute(outgoing, "seq", pairs)
        if middle > 2:
            place = lax.axis_index("seq")
            moved = jnp.where((place == k + 1) | (place == seq - 2 - k), moved, 0)
        arrived.append(moved)
        outgoing = onward(arrived[-1]).astype(BF16)
    filled_in, outer_in = slot_features(
        1, bounds, example_owner_slot, columns_grad, moments, *shared, ordered, "slots_in"
    )
    arrived, rows_in, outer_in = lax.optimization_barrier((arrived, rows_in, outer_in))
    summed = onward(arrived[-1]).astype(BF16)
    half = summed.shape[1] // 2
    kept = jnp.where(left, summed[:, :half], summed[:, half:])
    sent = jnp.where(left, summed[:, half:], summed[:, :half])
    received = lax.ppermute(sent, "seq", [(middle - 1, middle), (middle, middle - 1)])
    filled_grad, outer_grad = slot_features(
        0, bounds, example_owner_slot, rows_in, moments, *shared, ordered, "slots_grad"
    )
    received, outer_grad = lax.optimization_barrier((received, outer_grad))
    buffer = crossing_features(
        blk,
        bounds,
        example_owner_slot,
        (filled_grad, filled_in),
        (outer_grad, outer_in),
        kept,
        received,
        moments,
        *shared,
        arrived,
    )
    arrived = lax.all_to_all(buffer, ("seq", "tensor"), split_axis=0, concat_axis=0, tiled=True)
    features = owned_features(arrived)[None]
    out = second_product(
        rows_grad,
        output_projection_weight,
        adapter_down_weight,
        done,
        low,
    )
    return (out.reshape(attention_output_rows.shape), features)


def solution(mesh):
    return jax.shard_map(
        per_device,
        mesh=mesh,
        in_specs=(
            P("dp", "seq", "tensor"),
            P("dp", "seq", None),
            P("tensor", None),
            P(None, "tensor"),
            P("tensor", None),
            P(None, "dp", "tensor"),
            P(None, "dp", "tensor"),
            P(),
            P(),
            P("dp", None, None),
            P("dp", None),
        ),
        out_specs=(P("dp", "seq", "tensor"), P("dp", ("seq", "tensor"), None)),
        check_vma=False,
    )
```

```python
import functools

import jax
import jax.numpy as jnp
from jax import lax
from jax.experimental import pallas as pl
from jax.experimental.pallas import tpu as pltpu
from jax.sharding import PartitionSpec as P

TOUCH = 8
ADAPTER_SCALE = 4.0
BETA_ONE = 0.9
BETA_TWO = 0.999
EPSILON = 1e-08
MIB = 2**20
PIECES_VMEM, FIRST_VMEM, PREPARE_VMEM, SECOND_VMEM = 53.4, 48, 45, 46
BF16 = jnp.bfloat16
F32 = jnp.float32

HBM = pl.BlockSpec(memory_space=pltpu.HBM)
VMEM = pl.BlockSpec(memory_space=pltpu.VMEM)
SMEM = pl.BlockSpec(memory_space=pltpu.SMEM)


def dot_trailing(left, right):
    return lax.dot_general(left, right, (((1,), (1,)), ((), ())), preferred_element_type=F32)


def call(kernel, out_shape, in_specs, out_specs, scratch, flops, nbytes, name, vmem=32):
    return pl.pallas_call(
        kernel,
        out_shape=out_shape,
        in_specs=in_specs,
        out_specs=out_specs,
        scratch_shapes=scratch,
        compiler_params=pltpu.CompilerParams(vmem_limit_bytes=int(vmem * MIB)),
        cost_estimate=pl.CostEstimate(flops=flops, bytes_accessed=nbytes, transcendentals=0),
        name=name,
    )


def pieces_kernel(source_in, source_grad, down, up, first, second, *rest):
    *outs, moments, rows_in, rows_grad, partial, own, cast, down_buf, up_buf, sem, own_sem = rest
    size = len(outs)
    own_copies = [
        pltpu.make_async_copy(moment, own.at[i], own_sem.at[i])
        for i, moment in enumerate((first, second))
    ]
    place = lax.axis_index("tensor")
    tokens, width = rows_in.shape
    rows = tokens // size
    rank = up_buf.shape[0]
    there = pl.ds(pl.multiple_of(place * width, width), width)
    copies = []
    for i in range(size):
        here = pl.ds(i * rows, rows)
        copies.append(pltpu.make_async_copy(source_in.at[here], rows_in.at[here], sem.at[0, i]))
    for i in range(size):
        here = pl.ds(i * rows, rows)
        copies.append(
            pltpu.make_async_copy(source_grad.at[here, there], rows_grad.at[here], sem.at[1, i])
        )
    copies.insert(0, pltpu.make_async_copy(down, down_buf, sem.at[0, size]))
    copies.insert(size + 1, pltpu.make_async_copy(up, up_buf, sem.at[1, size]))
    for copy in copies[: size + 1] + own_copies + copies[size + 1 :]:
        copy.start()
    for copy in copies[: size + 1]:
        copy.wait()
    product = jnp.dot(rows_in[...], down_buf[...], preferred_element_type=F32)
    partial[:, :rank] = product.astype(BF16)
    for i, copy in enumerate(own_copies):
        copy.wait()
        cast[i] = own[i].astype(BF16)
    cast_copy = pltpu.make_async_copy(cast, moments, own_sem.at[2])
    cast_copy.start()
    for copy in copies[size + 1 :]:
        copy.wait()
    partial[:, rank:] = dot_trailing(rows_grad[...], up_buf[...]).astype(BF16)
    for k, out in enumerate(outs):
        block = pl.multiple_of(partner(place, k, size) * rows, rows)
        out[...] = partial[pl.ds(block, rows), :]
    cast_copy.wait()


def rank_pieces(rows_in, rows_grad, down, up, first, second, size):
    tokens, width = rows_in.shape
    rank = up.shape[0]
    rows = tokens // size
    return call(
        pieces_kernel,
        [jax.ShapeDtypeStruct((rows, 2 * rank), BF16)] * size
        + [jax.ShapeDtypeStruct((2,) + first.shape, BF16)],
        [HBM] * 6,
        [VMEM] * size + [HBM],
        [
            pltpu.VMEM((tokens, width), BF16),
            pltpu.VMEM((tokens, width), BF16),
            pltpu.VMEM((tokens, 2 * rank), BF16),
            pltpu.VMEM((2,) + first.shape, F32),
            pltpu.VMEM((2,) + first.shape, BF16),
            pltpu.VMEM(down.shape, BF16),
            pltpu.VMEM(up.shape, BF16),
            pltpu.SemaphoreType.DMA((2, size + 1)),
            pltpu.SemaphoreType.DMA((3,)),
        ],
        4 * tokens * width * rank,
        4 * tokens * width,
        "rank_pieces",
        PIECES_VMEM,
    )(rows_in, rows_grad, down, up, first, second)


def partner(place, k, size):
    if size & (size - 1) == 0:
        return place ^ abs(k)
    return (place + k + size) % size


def exchanged(value, axis, k):
    size = lax.axis_size(axis)
    return lax.ppermute(value, axis, [(i, partner(i, k, size)) for i in range(size)])


def shifted(value, axis, shift):
    size = lax.axis_size(axis)
    return lax.ppermute(value, axis, [(i, (i + shift) % size) for i in range(size)])


def scatter(pieces):
    return [exchanged(piece, "tensor", k) if k else piece for k, piece in enumerate(pieces)]


def total_kernel(*refs):
    *terms, out = refs
    total = terms[0][...].astype(F32)
    for term in terms[1:]:
        total = total + term[...].astype(F32)
    out[...] = total.T.astype(BF16)


def total_of(terms):
    rows, ranks = terms[0].shape
    return call(
        total_kernel,
        jax.ShapeDtypeStruct((ranks, rows), BF16),
        [VMEM] * len(terms),
        VMEM,
        [],
        len(terms) * rows * ranks,
        2 * (len(terms) + 1) * rows * ranks,
        "total_low",
    )(*terms)


def gather_pieces(total):
    size = lax.axis_size("tensor")
    return [total] + [exchanged(total, "tensor", k) for k in range(1, size)]


def example_scalars(bounds, block):
    low = lax.axis_index("seq") * block
    count = bounds.shape[2]
    first = jnp.int32(-1)
    last = jnp.int32(-1)
    for e in range(count):
        start = bounds[0, 0, e]
        first = first + (start <= low).astype(jnp.int32)
        last = last + (start <= low + block - 1).astype(jnp.int32)
    return low, first, last


def place_pieces(pieces, m, low_scratch):
    size = len(pieces)
    place = lax.axis_index("tensor")
    rank = low_scratch.shape[1]
    first = (1 - m) * rank
    for k, piece in enumerate(pieces):
        low_scratch[partner(place, -k, size)] = piece[first : first + rank, :]


def masked(low_piece, offset, start, end):
    tokens = offset + lax.broadcasted_iota(jnp.int32, low_piece.shape, 1)
    return jnp.where((tokens >= start) & (tokens < end), low_piece.astype(F32), 0.0).astype(BF16)


def left_side():
    return lax.axis_index("seq") < lax.axis_size("seq") // 2


def fits(bounds, example, low, tokens):
    return bounds[0, 0, example] >= low, bounds[0, 1, example] <= low + tokens


def edges(bounds, low, first, last, tokens):
    left = left_side()
    inner = jnp.where(left, last, first)
    outer = jnp.where(left, first, last)
    inner_starts, inner_ends = fits(bounds, inner, low, tokens)
    outer_starts, outer_ends = fits(bounds, outer, low, tokens)
    inner_on = (left & ~inner_ends) | (~left & ~inner_starts)
    outer_on = (left & ~outer_starts) | (~left & ~outer_ends)
    outer_inside = (left & outer_ends) | (~left & outer_starts)
    return inner, outer, inner_on, outer_on, outer_on & outer_inside


def sum_part(acc, source, low_scratch, low, start, end):
    size, _, rows = low_scratch.shape
    for c in range(size):
        begin = low + c * rows

        @pl.when((start < begin + rows) & (end > begin))
        def _():
            left = masked(low_scratch[c], begin, start, end)
            term = jnp.dot(
                left, source[c * rows : (c + 1) * rows, :], preferred_element_type=F32
            )
            fresh = (start >= begin) | (c == 0)
            acc[...] = jnp.where(fresh, 0.0, acc[...]) + term


def inner_kernel(size, bounds, rows_in, rows_grad, *rest):
    pieces = rest[:size]
    out, ordered, acc = rest[size:]
    tokens = rows_in.shape[0]
    low, first, last = example_scalars(bounds, tokens)
    inner = edges(bounds, low, first, last, tokens)[0]
    for m, source in enumerate((rows_in, rows_grad)):
        place_pieces(pieces, m, ordered.at[m])
        sum_part(acc, source, ordered.at[m], low, bounds[0, 0, inner], bounds[0, 1, inner])
        out[m] = (ADAPTER_SCALE * acc[...]).astype(BF16)


def inner_parts(bounds, rows_in, rows_grad, low):
    size = len(low)
    rank, rows = low[0].shape[0] // 2, low[0].shape[1]
    tokens, width = rows_in.shape
    return call(
        functools.partial(inner_kernel, size),
        [
            jax.ShapeDtypeStruct((2, rank, width), BF16),
            jax.ShapeDtypeStruct((2, size, rank, rows), BF16),
        ],
        [SMEM] + [VMEM] * (2 + size),
        [VMEM, VMEM],
        [pltpu.VMEM((rank, width), F32)],
        4 * tokens * width * rank,
        4 * tokens * width,
        "inner_parts",
    )(bounds, rows_in, rows_grad, *low)


def normalize(grads, first_moment, second_moment):
    first = first_moment + (1.0 - BETA_ONE) * grads
    second = second_moment + ((1.0 - BETA_TWO) * grads) * grads
    guess = lax.rsqrt(second)
    below = second * guess + EPSILON
    return first * (guess * (2.0 - below * guess))


def split_two(value):
    high = value.astype(BF16)
    return high, (value - high.astype(F32)).astype(BF16)


def rank_side_pair(rank_side, blocks):
    lines, rank = rank_side.shape
    blocks[...] = jnp.zeros_like(blocks)
    for i, term in enumerate(split_two(rank_side[...])):
        for j in range(2):
            at = (2 * i + j) * lines
            blocks[at : at + lines, j * rank : (j + 1) * rank] = term


def project_rank(blocks, normed):
    both = jnp.dot(blocks[...], normed, preferred_element_type=F32)
    half = both.shape[0] // 2
    return both[:half] + both[half:]


def project_width(value, right):
    high, low = split_two(value)
    return jnp.dot(high, right, preferred_element_type=F32) + jnp.dot(
        low, right, preferred_element_type=F32
    )


STEP = 16


def slots_kernel(m, bounds, owner, source, moments, rank_side, width_side, ordered, *rest):
    out, outer_part, acc, normed, blocks, ranked, wide = rest
    size = ordered.shape[1]
    tokens = source.shape[0]
    rows = tokens // size
    rank, width = outer_part.shape
    lines = rank_side.shape[0]
    low, first, last = example_scalars(bounds, tokens)
    count = bounds.shape[2]
    _, outer, _, outer_on, _ = edges(bounds, low, first, last, tokens)
    rank_side_pair(rank_side, blocks)

    def slot(j):
        return jnp.minimum(first + j, count - 1)

    def inside(j):
        starts, ends = fits(bounds, slot(j), low, tokens)
        return (first + j <= last) & starts & ends

    @pl.loop(0, TOUCH // 2)
    def _(pair):
        slots = (2 * pair, 2 * pair + 1)
        here = [inside(j) for j in slots]
        is_outer = [(first + j == outer) & outer_on for j in slots]
        wanted = [h | o for h, o in zip(here, is_outer)]
        starts = [jnp.where(w, bounds[0, 0, slot(j)], 0) for w, j in zip(wanted, slots)]
        ends = [jnp.where(w, bounds[0, 1, slot(j)], 0) for w, j in zip(wanted, slots)]
        begin_pair = jnp.where(wanted[0], starts[0], starts[1])
        end_pair = jnp.where(wanted[1], ends[1], ends[0])
        for c in range(size):
            begin = low + c * rows

            @pl.when((begin_pair < begin + rows) & (end_pair > begin))
            def _():
                left = jnp.concatenate(
                    [masked(ordered[m, c], begin, s, e) for s, e in zip(starts, ends)], axis=0
                )
                term = jnp.dot(
                    left, source[c * rows : (c + 1) * rows, :], preferred_element_type=F32
                )
                fresh = (begin_pair >= begin) | (c == 0)
                acc[...] = jnp.where(fresh, 0.0, acc[...]) + term

        for k, j in enumerate(slots):

            @pl.when(is_outer[k])
            def _():
                part = ADAPTER_SCALE * acc[k * rank : (k + 1) * rank, :]
                outer_part[...] = part.astype(BF16)

            @pl.when(here[k])
            def _():
                for r in range(0, rank, STEP):
                    normed[j, r : r + STEP, :] = normalize(
                        ADAPTER_SCALE * acc[k * rank + r : k * rank + r + STEP, :],
                        moments[0, m, r : r + STEP, :],
                        moments[1, m, r : r + STEP, :],
                    ).astype(BF16)

            @pl.when(~here[k])
            def _():
                normed[j] = jnp.zeros((rank, width), BF16)

    for j in range(0, TOUCH, 2):
        ranked[j * lines : (j + 2) * lines, :] = project_rank(
            blocks, normed[j : j + 2].reshape(2 * rank, width)
        )
    wide[...] = project_width(ranked[...], width_side[...]).reshape(wide.shape)
    out[...] = jnp.zeros_like(out)
    for j in range(TOUCH):

        @pl.when(inside(j))
        def _():
            out[owner[0, slot(j)]] = wide[j].astype(BF16)


def slot_features(m, bounds, owner, source, moments, rank_side, width_side, ordered, name):
    rank = ordered.shape[2]
    tokens, width = source.shape
    lines = rank_side.shape[0]
    columns = width_side.shape[1]
    return call(
        functools.partial(slots_kernel, m),
        [
            jax.ShapeDtypeStruct((owner.shape[1], lines, columns), BF16),
            jax.ShapeDtypeStruct((rank, width), BF16),
        ],
        [SMEM, SMEM] + [VMEM] * 5,
        [VMEM, VMEM],
        [
            pltpu.VMEM((2 * rank, width), F32),
            pltpu.VMEM((TOUCH, rank, width), BF16),
            pltpu.VMEM((4 * lines, 2 * rank), BF16),
            pltpu.VMEM((TOUCH * lines, width), F32),
            pltpu.VMEM((TOUCH, lines, columns), F32),
        ],
        2 * tokens * width * rank * TOUCH,
        4 * tokens * width,
        name,
    )(bounds, owner, source, moments, rank_side, width_side, ordered)


def crossing_kernel(
    tokens,
    hops,
    bounds,
    owner,
    filled_grad,
    filled_in,
    outer_grad,
    outer_in,
    kept,
    received,
    moments,
    rank_side,
    width_side,
    *rest
):
    arrived = rest[:hops]
    out, normed, blocks, ranked = rest[hops:]
    low, first, last = example_scalars(bounds, tokens)
    rank = outer_in.shape[0]
    lines = rank_side.shape[0]
    half = kept.shape[1]
    inner, outer, inner_on, _, outer_done = edges(bounds, low, first, last, tokens)
    place, middle = lax.axis_index("seq"), lax.axis_size("seq") // 2
    inner_done = inner_on & ((place == middle - 1) | (place == middle))
    out[:, :lines] = filled_grad[...]
    out[:, lines:] = filled_in[...]
    rank_side_pair(rank_side, blocks)

    @pl.when(outer_done)
    def _():
        for m, part in enumerate((outer_grad, outer_in)):
            for r in range(0, rank, STEP):
                here = slice(r, r + STEP)
                grads = part[here, :].astype(F32)
                for k in range(hops):
                    grads = grads + arrived[k][m, here, :].astype(F32)
                normed[m * rank + r : m * rank + r + STEP, :] = normalize(
                    grads, moments[0, m, here, :], moments[1, m, here, :]
                ).astype(BF16)
        ranked[: 2 * lines, :] = project_rank(blocks, normed[...])

    @pl.when(inner_done)
    def _():
        offset = jnp.where(left_side(), 0, half)
        normed[...] = jnp.zeros_like(normed)
        for m in range(2):
            for r in range(0, half, STEP):
                here = pl.ds(pl.multiple_of(offset + r, STEP), STEP)
                there = pl.ds(pl.multiple_of(m * rank + offset + r, STEP), STEP)
                grads = kept[m, r : r + STEP, :].astype(F32)
                grads = grads + received[m, r : r + STEP, :].astype(F32)
                normed[there, :] = normalize(
                    grads, moments[0, m, here, :], moments[1, m, here, :]
                ).astype(BF16)
        ranked[2 * lines :, :] = project_rank(blocks, normed[...])

    @pl.when(outer_done | inner_done)
    def _():
        wide = project_width(ranked[...], width_side[...]).astype(BF16)

        @pl.when(outer_done)
        def _():
            out[owner[0, outer]] = wide[: 2 * lines]

        @pl.when(inner_done)
        def _():
            out[owner[0, inner]] = wide[2 * lines :]


def crossing_features(
    tokens, bounds, owner, filled, outer, kept, received, moments, rank_side, width_side, arrived
):
    hops = len(arrived)
    rank, width = outer[0].shape
    slots, lines, columns = filled[0].shape
    return call(
        functools.partial(crossing_kernel, tokens, hops),
        jax.ShapeDtypeStruct((slots, 2 * lines, columns), BF16),
        [SMEM, SMEM] + [VMEM] * (9 + hops),
        VMEM,
        [
            pltpu.VMEM((2 * rank, width), BF16),
            pltpu.VMEM((4 * lines, 2 * rank), BF16),
            pltpu.VMEM((4 * lines, width), F32),
        ],
        8 * width * 2 * rank * 4 * lines,
        12 * rank * width,
        "crossing_features",
    )(
        bounds,
        owner,
        *filled,
        *outer,
        kept,
        received,
        moments,
        rank_side,
        width_side,
        *arrived,
    )


def owned_kernel(arrived, out):
    total = arrived[0].astype(F32)
    for k in range(1, arrived.shape[0]):
        total = total + arrived[k].astype(F32)
    columns = total.shape[1]
    for line in range(total.shape[0]):
        out[:, line * columns : (line + 1) * columns] = total[line : line + 1, :]


def owned_features(arrived):
    _, lines, columns = arrived.shape
    return call(
        owned_kernel,
        jax.ShapeDtypeStruct((1, lines * columns), F32),
        [VMEM],
        VMEM,
        [],
        arrived.size,
        2 * arrived.size,
        "owned_features",
    )(arrived)


TILE = 256


def depth_chunks(depth):
    return [0, depth // 8, 3 * depth // 8, 5 * depth // 8, 7 * depth // 8, depth]


def operand_copies(source, weight, held, weight_buf, sem, column):
    edges = depth_chunks(held.shape[1])
    pairs = []
    for c, (begin, end) in enumerate(zip(edges, edges[1:])):
        depth = pl.ds(begin, end - begin)
        columns = pl.ds(column, weight_buf.shape[0])
        pair = (
            pltpu.make_async_copy(source.at[:, depth], held.at[:, depth], sem.at[0, c]),
            pltpu.make_async_copy(weight.at[columns, depth], weight_buf.at[:, depth], sem.at[1, c]),
        )
        pairs.append((slice(begin, end), pair))
    return pairs


def start_all(pairs):
    for _, pair in pairs:
        for copy in pair:
            copy.start()


def add_chunk(pairs, c, held, weight_buf, out):
    depth, pair = pairs[c]
    for copy in pair:
        copy.wait()
    for n in range(0, weight_buf.shape[0], TILE):
        there = slice(n, min(n + TILE, weight_buf.shape[0]))
        term = dot_trailing(held[:, depth], weight_buf[there, depth])
        out[:, there] = term if c == 0 else out[:, there] + term


def first_kernel(column, source, weight, out, acc, held, weight_buf, sem):
    pairs = operand_copies(source, weight, held, weight_buf, sem, column)
    start_all(pairs)
    for c in range(len(pairs)):
        add_chunk(pairs, c, held, weight_buf, acc)
    out[...] = acc[...].astype(BF16)


def second_kernel(size, count, source, weight, down, *rest):
    done, pieces = rest[:count], rest[count : count + size]
    out, result, acc, low_rows, held, weight_buf, *bufs = rest[count + size :]
    down_buf, *bufs = bufs
    done_bufs, (pieces_buf, sem, extra_sem, out_sem) = bufs[:count], bufs[count:]
    tokens, width = result.shape
    split = sum(part.shape[1] for part in done)
    place = lax.axis_index("tensor")
    rows = tokens // size
    rank = low_rows.shape[1]
    extras = [pltpu.make_async_copy(down, down_buf, extra_sem.at[0])]
    for k, piece in enumerate(pieces):
        extras.append(pltpu.make_async_copy(piece, pieces_buf.at[k], extra_sem.at[1 + k]))
    for k, part in enumerate(done):
        extras.append(pltpu.make_async_copy(part, done_bufs[k], extra_sem.at[1 + size + k]))
    pairs = operand_copies(source, weight, held, weight_buf, sem, split)
    early = 2
    start_all(pairs[:early])
    for copy in extras:
        copy.start()
    start_all(pairs[early:])
    for c in range(early):
        add_chunk(pairs, c, held, weight_buf, acc)
    for copy in extras:
        copy.wait()
    for k in range(size):
        block = partner(place, -k, size)
        low_rows[pl.ds(pl.multiple_of(block * rows, rows), rows), :] = (
            pieces_buf[k, rank:, :].astype(F32).T.astype(BF16)
        )

    def out_copy(begin, end, k):
        here = pl.ds(begin, end - begin)
        return pltpu.make_async_copy(result.at[:, here], out.at[:, here], out_sem.at[k])

    def finish(base, begin, end, k):
        extra = dot_trailing(low_rows[...], down_buf[begin:end, :])
        result[:, begin:end] = (base[...].astype(F32) + ADAPTER_SCALE * extra).astype(BF16)
        out_copy(begin, end, k).start()

    cuts = [0]
    for k, part in enumerate(done_bufs):
        cuts.append(cuts[-1] + part.shape[1])
        finish(part, cuts[-2], cuts[-1], k)
    cuts.append(width)
    for c in range(early, len(pairs)):
        add_chunk(pairs, c, held, weight_buf, acc)
    finish(acc, split, width, count)
    for k in range(count + 1):
        out_copy(cuts[k], cuts[k + 1], k).wait()


def first_product(source, weight, column, split):
    tokens, depth = source.shape
    return call(
        functools.partial(first_kernel, column),
        jax.ShapeDtypeStruct((tokens, split), BF16),
        [HBM, HBM],
        VMEM,
        [
            pltpu.VMEM((tokens, split), F32),
            pltpu.VMEM((tokens, depth), BF16),
            pltpu.VMEM((split, depth), BF16),
            pltpu.SemaphoreType.DMA((2, len(depth_chunks(depth)) - 1)),
        ],
        2 * tokens * depth * split,
        2 * depth * (tokens + split),
        "first_product",
        FIRST_VMEM,
    )(source, weight)


def second_product(source, weight, down, done, pieces):
    tokens, depth = source.shape
    width, rank = down.shape
    rest = width - sum(part.shape[1] for part in done)
    size, count = len(pieces), len(done)
    return call(
        functools.partial(second_kernel, size, count),
        jax.ShapeDtypeStruct((tokens, width), BF16),
        [HBM] * (3 + count + size),
        HBM,
        [
            pltpu.VMEM((tokens, width), BF16),
            pltpu.VMEM((tokens, rest), F32),
            pltpu.VMEM((tokens, rank), BF16),
            pltpu.VMEM((tokens, depth), BF16),
            pltpu.VMEM((rest, depth), BF16),
            pltpu.VMEM(down.shape, BF16),
        ]
        + [pltpu.VMEM(part.shape, BF16) for part in done]
        + [
            pltpu.VMEM((size,) + pieces[0].shape, BF16),
            pltpu.SemaphoreType.DMA((2, len(depth_chunks(depth)) - 1)),
            pltpu.SemaphoreType.DMA((1 + size + count,)),
            pltpu.SemaphoreType.DMA((count + 1,)),
        ],
        2 * tokens * depth * rest,
        2 * depth * (tokens + rest),
        "second_product",
        SECOND_VMEM,
    )(source, weight, down, *done, *pieces)


def prepare_kernel(source_in, source_grad, width_side, first, second, other, *rest):
    rows_in, columns_grad, right, moments, own, arrived, sem = rest
    place = lax.axis_index("tensor")
    width, rows = right.shape[0], own.shape[2]
    here = pl.ds(pl.multiple_of(place * width, width), width)
    copies = [
        pltpu.make_async_copy(first, own.at[0], sem.at[0]),
        pltpu.make_async_copy(second, own.at[1], sem.at[1]),
        pltpu.make_async_copy(other, arrived, sem.at[2]),
        pltpu.make_async_copy(source_grad.at[:, here], columns_grad, sem.at[3]),
        pltpu.make_async_copy(source_in, rows_in, sem.at[4]),
        pltpu.make_async_copy(width_side.at[here], right, sem.at[5]),
    ]
    for copy in copies:
        copy.start()
    for copy in copies[:3]:
        copy.wait()
    mine = lax.axis_index("dp")
    for i, beta in enumerate((BETA_ONE, BETA_TWO)):
        for m in range(2):
            if arrived.shape[2] == rows:
                at = pl.ds(pl.multiple_of(mine * rows, rows), rows)
                moments[i, m, at, :] = beta * own[i, m]
                at = pl.ds(pl.multiple_of((1 - mine) * rows, rows), rows)
                moments[i, m, at, :] = beta * arrived[i, m].astype(F32)
            else:
                moments[i, m] = beta * arrived[i, m].astype(F32)
    for copy in copies[3:]:
        copy.wait()


def other_moments(own):
    if lax.axis_size("dp") != 2:
        return lax.all_gather(own, "dp", axis=2, tiled=True)
    return shifted(own, "dp", 1)


def prepare(rows_in, rows_grad, width_side, first, second, other):
    tokens, width = rows_in.shape
    columns = width_side.shape[1]
    rank = first.shape[1] * lax.axis_size("dp")
    return call(
        prepare_kernel,
        [
            jax.ShapeDtypeStruct((tokens, width), BF16),
            jax.ShapeDtypeStruct((tokens, width), BF16),
            jax.ShapeDtypeStruct((width, columns), BF16),
            jax.ShapeDtypeStruct((2, 2, rank, width), F32),
        ],
        [HBM] * 6,
        [VMEM] * 4,
        [
            pltpu.VMEM((2,) + first.shape, F32),
            pltpu.VMEM(other.shape, BF16),
            pltpu.SemaphoreType.DMA((6,)),
        ],
        8 * rank * width,
        4 * tokens * width + 8 * rank * width,
        "prepare",
        PREPARE_VMEM,
    )(rows_in, rows_grad, width_side, first, second, other)


def per_device(
    attention_output_rows,
    projection_result_gradient,
    adapter_down_weight,
    adapter_up_weight,
    output_projection_weight,
    adam_first_moments,
    adam_second_moments,
    rank_side_projection,
    width_side_projection,
    bounds,
    example_owner_slot,
):
    packs, blk, width_local = attention_output_rows.shape
    assert packs == 1
    width = projection_result_gradient.shape[2]
    size = lax.axis_size("tensor")
    rows_in = attention_output_rows.reshape(blk, width_local)
    rows_grad = projection_result_gradient.reshape(blk, width)

    own_moments = (adam_first_moments, adam_second_moments)
    *pieces, sent_moments = rank_pieces(
        rows_in, rows_grad, adapter_down_weight, adapter_up_weight, *own_moments, size
    )
    other = other_moments(sent_moments)
    cuts = [0, 3 * width_local // 8, 5 * width_local // 8]

    def product(rows, k):
        return first_product(rows, output_projection_weight, cuts[k], cuts[k + 1] - cuts[k])

    done = [product(rows_grad, 0)]
    sent, done = lax.optimization_barrier((scatter(pieces), done))
    total, rows_late, bounds_late = lax.optimization_barrier((total_of(sent), rows_grad, bounds))
    done.append(product(rows_late, 1))
    done, rows_late, other = lax.optimization_barrier((done, rows_late, other))
    prepared = prepare(rows_in, rows_late, width_side_projection, *own_moments, other)
    first_token = lax.axis_index("seq") * blk
    end_token = first_token + blk
    starts, ends = bounds_late[0, 0], bounds_late[0, 1]
    left = left_side()
    spans = jnp.any(
        jnp.where(
            left,
            (starts < first_token) & (ends >= end_token),
            (starts <= first_token) & (ends > end_token),
        )
    ).astype(F32)
    low, prepared, done, spans = lax.optimization_barrier(
        (gather_pieces(total), prepared, done, spans)
    )
    rows_in, columns_grad, right, moments = prepared
    inner, ordered = inner_parts(bounds, rows_in, columns_grad, low)
    shared = (rank_side_projection, right)
    seq = lax.axis_size("seq")
    middle = seq // 2

    def onward(arrived):
        return inner.astype(F32) + spans * arrived.astype(F32)

    arrived = []
    outgoing = inner
    for k in range(middle - 1):
        pairs = [(k, k + 1), (k + 1, k), (seq - 1 - k, seq - 2 - k), (seq - 2 - k, seq - 1 - k)]
        moved = lax.ppermute(outgoing, "seq", pairs)
        if middle > 2:
            place = lax.axis_index("seq")
            moved = jnp.where((place == k + 1) | (place == seq - 2 - k), moved, 0)
        arrived.append(moved)
        outgoing = onward(arrived[-1]).astype(BF16)
    filled_in, outer_in = slot_features(
        1, bounds, example_owner_slot, columns_grad, moments, *shared, ordered, "slots_in"
    )
    arrived, rows_in, outer_in = lax.optimization_barrier((arrived, rows_in, outer_in))
    summed = onward(arrived[-1]).astype(BF16)
    half = summed.shape[1] // 2
    kept = jnp.where(left, summed[:, :half], summed[:, half:])
    sent = jnp.where(left, summed[:, half:], summed[:, :half])
    received = lax.ppermute(sent, "seq", [(middle - 1, middle), (middle, middle - 1)])
    filled_grad, outer_grad = slot_features(
        0, bounds, example_owner_slot, rows_in, moments, *shared, ordered, "slots_grad"
    )
    received, outer_grad = lax.optimization_barrier((received, outer_grad))
    buffer = crossing_features(
        blk,
        bounds,
        example_owner_slot,
        (filled_grad, filled_in),
        (outer_grad, outer_in),
        kept,
        received,
        moments,
        *shared,
        arrived,
    )
    arrived = lax.all_to_all(buffer, ("seq", "tensor"), split_axis=0, concat_axis=0, tiled=True)
    features = owned_features(arrived)[None]
    out = second_product(
        rows_grad,
        output_projection_weight,
        adapter_down_weight,
        done,
        low,
    )
    return (out.reshape(attention_output_rows.shape), features)


def solution(mesh):
    return jax.shard_map(
        per_device,
        mesh=mesh,
        in_specs=(
            P("dp", "seq", "tensor"),
            P("dp", "seq", None),
            P("tensor", None),
            P(None, "tensor"),
            P("tensor", None),
            P(None, "dp", "tensor"),
            P(None, "dp", "tensor"),
            P(),
            P(),
            P("dp", None, None),
            P("dp", None),
        ),
        out_specs=(P("dp", "seq", "tensor"), P("dp", ("seq", "tensor"), None)),
        check_vma=False,
    )
```
